32 devices in a mesh: dp: 4 (over z), space: 8 (over y, x, core).
Axes of the slice: x: 2, y: 2, z: 4, core: 2. Of those that a mesh axis runs over, the one named last changes fastest.
Arguments:
- features: bfloat16 [4, 96, 16, 56, 448], P('dp', None, None, 'space'), may hold values from -6 to 6
- conv_weight: bfloat16 [3, 3, 3, 3, 96], replicated, may hold values from -0.125 to 0.125
- out_grad: bfloat16 [4, 16, 128, 384], P('dp', 'space'), may hold values from -6 to 6
- pos_embed: bfloat16 [128, 384], replicated, may hold values from -3 to 3
- patch_weight: bfloat16 [588, 384], replicated, may hold values from -0.25 to 0.25
- norm1: float32 [384], replicated, may hold values from 0.1 to 1.9
- qkv_weight: bfloat16 [384, 1152], replicated, may hold values from -0.3125 to 0.3125
- proj_weight: bfloat16 [384, 384], replicated, may hold values from -0.3125 to 0.3125
- norm2: float32 [384], replicated, may hold values from 0.1 to 1.9
- fc1_weight: bfloat16 [384, 1536], replicated, may hold values from -0.3125 to 0.3125
- fc2_weight: bfloat16 [1536, 384], replicated, may hold values from -0.15625 to 0.15625
Outputs:
- block_out: bfloat16 [4, 16, 128, 384], P('dp', 'space')
- feature_grad: bfloat16 [4, 96, 16, 56, 448], P('dp', None, None, 'space')
- conv_grad: float32 [3, 3, 3, 3, 96], replicated
- qkv_grad: float32 [384, 1152], P('space')
- proj_grad: float32 [384, 384], P('space')
- fc1_grad: float32 [384, 1536], P('space')
- fc2_grad: float32 [1536, 384], P('space')
The draws below stay inside these ranges and needn't reach their ends.
All inputs are finite; a program needn't handle non-finite values.
Results may differ from the reference program's by a relative error of at most 0.025.
Values may be sent and summed in bfloat16 or wider, within the bound.
No kernel may reach another device: no remote copies, remote signals or barrier semaphores. Data moves between devices by JAX's collectives and lax.ppermute only.
A program may use at most 192 MiB of HBM per device.

```python
import jax
import jax.numpy as jnp
from jax import lax

D = 384
HEADS = 6
MLP = 1536
CH = 96
FRAMES = 16
ROWS_DEV = 7
COLS = 448
H = 56
PATCHES = 128
CLIPS = 4
N_DP = 4
N_SPACE = 8


def block_scale(rng, dims, cuts, least, top_value):
    level, own = 1.0, jax.random.fold_in(rng, 6)
    for position, blocks in cuts:
        heights = jnp.exp(jax.random.uniform(jax.random.fold_in(own, position), (blocks,), jnp.float32, least / len(cuts), top_value / len(cuts)))
        level = level * jnp.repeat(heights, dims[position] // blocks).reshape([-1 if axis == position else 1 for axis in range(len(dims))])
    return level


def normal_values(rng, shape, spread, reach, shards=(), held_as=jnp.bfloat16):
    values = spread * jax.random.normal(rng, shape, jnp.float32)
    if shards:
        values = values * block_scale(rng, shape, shards, -0.22, 0.18)
    return jnp.clip(values, -reach, reach).astype(held_as)


def setup_inputs(seed: int = 0) -> dict:
    splits = jax.random.split(jax.random.key(seed), 12)
    features = normal_values(splits[0], (CLIPS, CH, FRAMES, H, COLS), 1.0, 6.0, ((0, 4), (3, 8)))
    conv_weight = normal_values(splits[1], (3, 3, 3, 3, CH), (27 * CH) ** -0.5, 0.125)
    out_grad = normal_values(splits[2], (CLIPS, FRAMES, PATCHES, D), 1.0, 6.0, ((0, 4), (1, 8)))
    pos_embed = normal_values(splits[3], (PATCHES, D), 0.5, 3.0)
    patch_weight = normal_values(splits[4], (588, D), 588 ** -0.5, 0.25)
    norm1 = jnp.clip(1.0 + 0.18 * jax.random.normal(splits[5], (D,), jnp.float32), 0.1, 1.9)
    qkv_weight = normal_values(splits[6], (D, 3 * D), D ** -0.5, 0.3125)
    proj_weight = normal_values(splits[7], (D, D), D ** -0.5, 0.3125)
    norm2 = jnp.clip(1.0 + 0.18 * jax.random.normal(splits[8], (D,), jnp.float32), 0.1, 1.9)
    fc1_weight = normal_values(splits[9], (D, MLP), D ** -0.5, 0.3125)
    fc2_weight = normal_values(splits[10], (MLP, D), MLP ** -0.5, 0.15625)
    return dict(features=features, conv_weight=conv_weight, out_grad=out_grad, pos_embed=pos_embed, patch_weight=patch_weight, norm1=norm1, qkv_weight=qkv_weight, proj_weight=proj_weight, norm2=norm2, fc1_weight=fc1_weight, fc2_weight=fc2_weight)


def layer_norm(values, gain_vec):
    average = lax.optimization_barrier(jnp.mean(values, axis=-1, keepdims=True))
    centered = values - average
    variance = lax.optimization_barrier(jnp.mean(centered * centered, axis=-1, keepdims=True))
    return centered * lax.rsqrt(variance + 1e-06) * gain_vec

def discriminator(pixels, pos_embed, patch_weight, norm1, qkv_weight, proj_weight, norm2, fc1_weight, fc2_weight):
    channels, height, width = pixels.shape
    patch_rows = height // 14
    patch_cols = width // 14
    count = patch_rows * patch_cols
    patches = pixels.reshape(channels, patch_rows, 14, patch_cols, 14).transpose(1, 3, 0, 2, 4).reshape(count, channels * 196)
    embedded = jnp.dot(patches, patch_weight, preferred_element_type=jnp.float32) + pos_embed.astype(jnp.float32)
    model_width = embedded.shape[1]
    normed = layer_norm(embedded, norm1).astype(jnp.bfloat16)
    packed = jnp.dot(normed, qkv_weight, preferred_element_type=jnp.float32).astype(jnp.bfloat16)
    packed = packed.reshape(count, 3, HEADS, model_width // HEADS)
    queries = packed[:, 0]
    keys_in = packed[:, 1]
    values_in = packed[:, 2]
    head_size = model_width // HEADS
    scores = jnp.einsum('qhd,khd->hqk', queries, keys_in, preferred_element_type=jnp.float32) * (1.0 / float(head_size) ** 0.5)
    probs = jax.nn.softmax(scores, axis=-1).astype(jnp.bfloat16)
    attended = jnp.einsum('hqk,khd->qhd', probs, values_in, preferred_element_type=jnp.float32)
    attended = attended.astype(jnp.bfloat16).reshape(count, model_width)
    residual = embedded + jnp.dot(attended, proj_weight, preferred_element_type=jnp.float32)
    normed_two = layer_norm(residual, norm2).astype(jnp.bfloat16)
    hidden = jax.nn.gelu(jnp.dot(normed_two, fc1_weight, preferred_element_type=jnp.float32), approximate=False).astype(jnp.bfloat16)
    return residual + jnp.dot(hidden, fc2_weight, preferred_element_type=jnp.float32)

def frame_steps(frames, cotangents, params):
    pos_embed, patch_weight, norm1, qkv_weight, proj_weight, norm2, fc1_weight, fc2_weight = params

    def one_frame(pixels, cotangent):

        def forward(pix, qkv_w, proj_w, fc1_w, fc2_w):
            return discriminator(pix, pos_embed, patch_weight, norm1, qkv_w, proj_w, norm2, fc1_w, fc2_w)
        result, pullback = jax.vjp(forward, pixels, qkv_weight, proj_weight, fc1_weight, fc2_weight)
        cotans = pullback(cotangent.astype(jnp.float32))
        return (result.astype(jnp.bfloat16), cotans[0], tuple((item.astype(jnp.float32) for item in cotans[1:])))
    block_out, pixel_grads, weight_grads = jax.vmap(one_frame, in_axes=(1, 0), out_axes=(0, 1, 0))(frames, cotangents)
    return (block_out, pixel_grads, tuple((lax.optimization_barrier(jnp.sum(item, axis=0)) for item in weight_grads)))

def project_taps(feature_tile, tap_matrix):
    return lax.dot_general(tap_matrix, feature_tile, (((1,), (0,)), ((), ())), preferred_element_type=jnp.float32)

def time_parts(tap_values):
    grouped = tap_values.reshape((3, 3, 9) + tap_values.shape[1:])
    frame_count = tap_values.shape[1]
    parts = []
    for row_tap in range(3):
        total = None
        for time_tap in range(3):
            piece = grouped[time_tap, row_tap]
            lag = 2 - time_tap
            if lag > 0:
                piece = jnp.pad(piece[:, :frame_count - lag], ((0, 0), (lag, 0), (0, 0), (0, 0)))
            total = piece if total is None else total + piece
        parts.append(total)
    return parts

def column_sum(planes):
    width = planes.shape[-1]
    padded = jnp.pad(planes, ((0, 0), (0, 0), (0, 0), (1, 1)))
    return padded[0:3, :, :, 0:width] + padded[3:6, :, :, 1:1 + width] + padded[6:9, :, :, 2:2 + width]

def gather_taps(padded_grad, frame_count, row_count, col_count):
    shifted = [padded_grad[:, :, :, 2 - col_tap:2 - col_tap + col_count] for col_tap in range(3)]
    pieces = []
    for time_tap in range(3):
        for row_tap in range(3):
            for col_tap in range(3):
                pieces.append(shifted[col_tap][:, 2 - time_tap:2 - time_tap + frame_count, 2 - row_tap:2 - row_tap + row_count])
    return jnp.stack(pieces, axis=0).reshape(-1, frame_count * row_count * col_count)

def conv_backward(stacked, feature_tile, tap_matrix):
    channels = feature_tile.shape[0]
    flat = feature_tile.reshape(channels, -1)
    feature_grad = lax.dot_general(tap_matrix, stacked, (((0,), (0,)), ((), ())), preferred_element_type=jnp.float32)
    feature_grad = feature_grad.reshape(feature_tile.shape).astype(jnp.bfloat16)
    conv_part = lax.dot_general(stacked, flat, (((1,), (1,)), ((), ())), preferred_element_type=jnp.float32)
    return (feature_grad, conv_part)

def reference(features, conv_weight, out_grad, pos_embed, patch_weight, norm1, qkv_weight, proj_weight, norm2, fc1_weight, fc2_weight):
    params = (pos_embed, patch_weight, norm1, qkv_weight, proj_weight, norm2, fc1_weight, fc2_weight)
    tap_matrix = conv_weight.reshape(-1, CH)
    height = ROWS_DEV * N_SPACE
    blocks = []
    feature_grads = []
    conv_total = jnp.zeros(tap_matrix.shape, jnp.float32)
    totals = (jnp.zeros(qkv_weight.shape, jnp.float32), jnp.zeros(proj_weight.shape, jnp.float32), jnp.zeros(fc1_weight.shape, jnp.float32), jnp.zeros(fc2_weight.shape, jnp.float32))
    for clip in range(N_DP):
        feature_clip = features[clip]
        parts = time_parts(project_taps(feature_clip, tap_matrix))
        planes = None
        for row_tap in range(3):
            piece = jnp.pad(parts[row_tap], ((0, 0), (0, 0), (1, 1), (0, 0)))[:, :, row_tap:row_tap + height]
            planes = piece if planes is None else planes + piece
        pixels = column_sum(planes).astype(jnp.bfloat16)
        block_out, pixel_grads, weight_grads = frame_steps(pixels, out_grad[clip], params)
        padded_grad = jnp.pad(pixel_grads, ((0, 0), (0, 2), (1, 1), (1, 1)))
        stacked = gather_taps(padded_grad, FRAMES, height, COLS)
        feature_grad, conv_part = conv_backward(stacked, feature_clip, tap_matrix)
        blocks.append(block_out)
        feature_grads.append(feature_grad)
        conv_total = conv_total + conv_part
        totals = tuple((total + item for total, item in zip(totals, weight_grads)))
    return (jnp.stack(blocks, axis=0), jnp.stack(feature_grads, axis=0), conv_total.reshape(conv_weight.shape), totals[0], totals[1], totals[2], totals[3])
```

```python
import functools
import math

import jax
import jax.numpy as jnp
from jax import lax
from jax.experimental import pallas as pl
from jax.experimental.pallas import tpu as pltpu
from jax.sharding import PartitionSpec as P

HEADS = 6
PATCH = 14
COLOURS = 3
TAPS = 3
F32 = jnp.float32
BF16 = jnp.bfloat16
MIB = 1 << 20


def dot(a, b):
    return jnp.dot(a, b, preferred_element_type=F32)


def dot_nt(a, b):
    return lax.dot_general(a, b, (((1,), (1,)), ((), ())), preferred_element_type=F32)


def dot_tn(a, b):
    return lax.dot_general(a, b, (((0,), (0,)), ((), ())), preferred_element_type=F32)


def split(index, size):
    if size & (size - 1) == 0:
        shift = size.bit_length() - 1
        return index >> shift, index & (size - 1)
    high = jnp.floor((index.astype(F32) + 0.5) * (1.0 / size)).astype(jnp.int32)
    return high, index - high * size


def rows_of(count):
    return lax.broadcasted_iota(jnp.int32, (count, 1), 0)


def cols_of(count):
    return lax.broadcasted_iota(jnp.int32, (1, count), 1)


def match(left, right):
    return jnp.where(left == right, 1.0, 0.0).astype(BF16)


def round_up(value, unit):
    return -(-value // unit) * unit


class Sizes:
    def __init__(self, features, space):
        self.space = space
        self.channels, self.frames, self.rows, self.cols = features.shape[1:]
        self.per_dev = self.frames // space
        self.ext = self.rows + 2
        self.height = self.rows * space
        self.patch_rows = self.height // PATCH
        self.patch_cols = self.cols // PATCH
        self.tokens = self.patch_rows * self.patch_cols
        self.block = round_up(self.ext * COLOURS * self.per_dev, 16)
        self.q_used = COLOURS * PATCH
        self.q_pad = round_up(self.q_used, 64)
        self.plane = COLOURS * self.frames
        self.group = TAPS * self.plane
        self.window = TAPS * self.group
        self.depth = self.channels * self.frames


def wire_keys(sizes, index):
    peer, rest = split(index, sizes.block)
    plane, frame = split(rest, sizes.per_dev)
    ext, colour = split(plane, COLOURS)
    key = (frame * COLOURS + colour) * 4096 + peer * sizes.rows + ext
    return jnp.where(plane < sizes.ext * COLOURS, key, -2)


def patch_keys(sizes, index):
    lead, q = split(index, sizes.q_pad)
    frame, patch_row = split(lead, sizes.patch_rows)
    colour, row = split(q, PATCH)
    key = (frame * COLOURS + colour) * 4096 + patch_row * PATCH + row + 1
    return jnp.where(q < sizes.q_used, key, -1)


def tile_keys(sizes, index):
    return index


def tile_wire_keys(sizes, index):
    peer, rest = split(index, sizes.block)
    plane, frame = split(rest, sizes.per_dev)
    key = plane * sizes.frames + peer * sizes.per_dev + frame
    return jnp.where(plane < sizes.ext * COLOURS, key, -2)


def flipped(tap):
    row, _ = split(tap, TAPS * COLOURS)
    return tap + (TAPS - 1 - 2 * row) * (TAPS * COLOURS)


def column_order(sizes):
    inner, patch = split(rows_of(sizes.cols), sizes.patch_cols)
    return match(patch * PATCH + inner, cols_of(sizes.cols))


def conv_forward_kernel(sizes, weight_ref, x_ref, out_ref, band_ref, acc_ref, plane_ref):
    step = pl.program_id(0)
    taps = TAPS * TAPS * COLOURS

    @pl.when(step == 0)
    def _():
        tap, frame_out = split(rows_of(sizes.window), sizes.frames)
        channel, frame_in = split(cols_of(sizes.depth), sizes.frames)
        spread = match(rows_of(sizes.channels), channel)
        pick = match(flipped(tap), cols_of(taps))
        lag = frame_in - frame_out + 2
        total = None
        for a in range(TAPS):
            weight = weight_ref[a * taps : (a + 1) * taps, :]
            wide = dot(dot(pick, weight).astype(BF16), spread)
            wide = jnp.where(lag == a, wide, 0.0)
            total = wide if total is None else total + wide
        band_ref[...] = total.astype(BF16)

    x = x_ref[...].reshape(sizes.depth, sizes.cols)
    product = dot(band_ref[...], x)
    base = pl.multiple_of(step * sizes.group, 16)
    keep = sizes.window - sizes.group

    @pl.when(step == 0)
    def _():
        acc_ref[pl.ds(0, sizes.window), :] = product

    @pl.when(step > 0)
    def _():
        acc_ref[pl.ds(base, keep), :] += product[:keep]
        acc_ref[pl.ds(pl.multiple_of(base + keep, 16), sizes.group), :] = product[keep:]

    @pl.when(step == sizes.rows - 1)
    def _():
        zero = jnp.zeros((sizes.plane, 1), F32)
        for ext in range(sizes.ext):
            at = ext * sizes.group
            first = acc_ref[at : at + sizes.plane, :]
            second = acc_ref[at + sizes.plane : at + 2 * sizes.plane, :]
            third = acc_ref[at + 2 * sizes.plane : at + 3 * sizes.plane, :]
            first = jnp.concatenate([zero, first[:, : sizes.cols - 1]], axis=1)
            third = jnp.concatenate([third[:, 1:], zero], axis=1)
            plane_ref[ext * sizes.plane : (ext + 1) * sizes.plane, :] = (
                first + second + third
            ).astype(BF16)
        wire = tile_wire_keys(sizes, rows_of(sizes.space * sizes.block))
        order = match(wire, cols_of(sizes.ext * sizes.plane))
        moved = dot(order, plane_ref[...]).astype(BF16)
        out_ref[...] = moved.reshape(sizes.space, sizes.block, sizes.cols)


def conv_forward(sizes, weight, x):
    return pl.pallas_call(
        functools.partial(conv_forward_kernel, sizes),
        grid=(sizes.rows,),
        in_specs=[
            pl.BlockSpec(weight.shape, lambda h: (0, 0)),
            pl.BlockSpec((sizes.channels, 1, sizes.frames, sizes.cols), lambda h: (0, h, 0, 0)),
        ],
        out_specs=pl.BlockSpec((sizes.space, sizes.block, sizes.cols), lambda h: (0, 0, 0)),
        out_shape=jax.ShapeDtypeStruct((sizes.space, sizes.block, sizes.cols), BF16),
        scratch_shapes=[
            pltpu.VMEM((sizes.window, sizes.depth), BF16),
            pltpu.VMEM((sizes.ext * sizes.group, sizes.cols), F32),
            pltpu.VMEM((sizes.ext * sizes.plane, sizes.cols), BF16),
        ],
        compiler_params=pltpu.CompilerParams(vmem_limit_bytes=48 * MIB),
        cost_estimate=pl.CostEstimate(
            flops=2 * sizes.rows * sizes.window * sizes.depth * sizes.cols,
            bytes_accessed=2 * x.size,
            transcendentals=0,
        ),
        name="conv_forward",
    )(weight, x)


def prepare_kernel(sizes, weight_ref, patch_ref, patch_out_ref, band_ref):
    taps = TAPS * TAPS * COLOURS
    inner, q = split(rows_of(PATCH * sizes.q_pad), sizes.q_pad)
    source = jnp.where(q < sizes.q_used, q * PATCH + inner, -1)
    patch_out_ref[...] = dot(match(source, cols_of(patch_ref.shape[0])), patch_ref[...]).astype(BF16)

    tap, frame_in = split(cols_of(sizes.window), sizes.frames)
    pick = match(rows_of(taps), flipped(tap))
    chunk = sizes.depth // 4
    for part in range(4):
        channel, frame_out = split(rows_of(chunk) + part * chunk, sizes.frames)
        spread = match(channel, cols_of(sizes.channels))
        lag = frame_out - frame_in + 2
        total = None
        for a in range(TAPS):
            weight = weight_ref[a * taps : (a + 1) * taps, :]
            wide = dot(spread, dot_tn(weight, pick).astype(BF16))
            wide = jnp.where(lag == a, wide, 0.0)
            total = wide if total is None else total + wide
        band_ref[part * chunk : (part + 1) * chunk, :] = total.astype(BF16)


def prepare(sizes, weight, patch_weight):
    width = patch_weight.shape[1]
    return pl.pallas_call(
        functools.partial(prepare_kernel, sizes),
        out_shape=(
            jax.ShapeDtypeStruct((PATCH * sizes.q_pad, width), BF16),
            jax.ShapeDtypeStruct((sizes.depth, sizes.window), BF16),
        ),
        compiler_params=pltpu.CompilerParams(vmem_limit_bytes=48 * MIB),
        cost_estimate=pl.CostEstimate(
            flops=4 * 10**9, bytes_accessed=4 * MIB, transcendentals=0
        ),
        name="prepare",
    )(weight, patch_weight)


def normalise(values):
    average = jnp.mean(values, axis=-1, keepdims=True)
    centered = values - average
    variance = jnp.mean(centered * centered, axis=-1, keepdims=True)
    scale = lax.rsqrt(variance + 1e-06)
    return centered * scale, scale


def normalise_back(grad, unit, scale):
    mean_grad = jnp.mean(grad, axis=-1, keepdims=True)
    mean_both = jnp.mean(grad * unit, axis=-1, keepdims=True)
    return scale * (grad - mean_grad - unit * mean_both)


def block_kernel(
    sizes,
    me_ref,
    wire_ref,
    cotangent_ref,
    pos_ref,
    patch_ref,
    norm1_ref,
    qkv_ref,
    proj_ref,
    norm2_ref,
    fc1_ref,
    fc2_ref,
    out_ref,
    wire_out_ref,
    grads_ref,
    pixels_ref,
    patches_ref,
    column_ref,
    packed_ref,
    probs_ref,
    attended_ref,
    grad_packed_ref,
    qkv_grad_ref,
    proj_grad_ref,
    fc1_grad_ref,
    fc2_grad_ref,
):
    tokens, width = pos_ref.shape
    frames = sizes.per_dev
    count = frames * tokens
    hidden_width = fc1_ref.shape[1]
    head = width // HEADS
    wire_rows = sizes.space * sizes.block
    leads = frames * sizes.patch_rows
    q_pad = sizes.q_pad
    pc = sizes.patch_cols

    order = match(patch_keys(sizes, rows_of(leads * q_pad)), wire_keys(sizes, cols_of(wire_rows)))
    pixels_ref[...] = dot(order, wire_ref[...].reshape(wire_rows, sizes.cols)).astype(BF16)
    columns = column_order(sizes)
    column_ref[...] = columns
    for lead in range(leads):
        turned = dot_nt(columns, pixels_ref[lead * q_pad : (lead + 1) * q_pad, :])
        for inner in range(PATCH):
            patches_ref[lead * pc : (lead + 1) * pc, inner * q_pad : (inner + 1) * q_pad] = turned[
                inner * pc : (inner + 1) * pc, :
            ].astype(BF16)

    pos = pos_ref[...].astype(F32)
    embedded = dot(patches_ref[...], patch_ref[...])
    embedded = embedded + (pos if frames == 1 else jnp.concatenate([pos] * frames, axis=0))
    gain1 = norm1_ref[...]
    gain2 = norm2_ref[...]
    unit1, scale1 = normalise(embedded)
    normed = (unit1 * gain1).astype(BF16)
    packed_ref[...] = dot(normed, qkv_ref[...]).astype(BF16)

    lanes = min(128, width)
    per_group = lanes // head
    lane_head, _ = split(cols_of(lanes), head)
    inv = 1.0 / float(head) ** 0.5
    for frame in range(frames):
        at = slice(frame * tokens, (frame + 1) * tokens)
        for group in range(width // lanes):
            cut = slice(group * lanes, (group + 1) * lanes)
            queries = packed_ref[at, cut]
            keys_in = packed_ref[at, width + group * lanes : width + (group + 1) * lanes]
            values_in = packed_ref[at, 2 * width + group * lanes : 2 * width + (group + 1) * lanes]
            joined = None
            for sub in range(per_group):
                mine = lane_head == sub
                masked = queries * jnp.where(mine, 1.0, 0.0).astype(BF16)
                scores = dot_nt(masked, keys_in) * inv
                scores = jnp.exp(scores - jnp.max(scores, axis=-1, keepdims=True))
                probs = scores / jnp.sum(scores, axis=-1, keepdims=True)
                probs_ref[(frame * HEADS) + group * per_group + sub] = probs
                value = dot(probs.astype(BF16), values_in)
                joined = value if joined is None else jnp.where(mine, value, joined)
            attended_ref[at, cut] = joined.astype(BF16)

    residual = embedded + dot(attended_ref[...], proj_ref[...])
    unit2, scale2 = normalise(residual)
    normed2 = (unit2 * gain2).astype(BF16)
    cotangent = cotangent_ref[...].reshape(count, width)

    chunk = width
    result = residual
    grad_normed2 = None
    for part in range(hidden_width // chunk):
        cut = slice(part * chunk, (part + 1) * chunk)
        before = dot(normed2, fc1_ref[:, cut])
        cdf = 0.5 + 0.5 * lax.erf(before * math.sqrt(0.5))
        hidden = (before * cdf).astype(BF16)
        result = result + dot(hidden, fc2_ref[cut, :])
        slope = cdf + before * (jnp.exp(-0.5 * before * before) * (1.0 / math.sqrt(2.0 * math.pi)))
        grad_hidden = dot_nt(cotangent, fc2_ref[cut, :]).astype(BF16)
        grad_before = (grad_hidden.astype(F32) * slope).astype(BF16)
        fc2_grad_ref[cut, :] = dot_tn(hidden, cotangent)
        fc1_grad_ref[:, cut] = dot_tn(normed2, grad_before)
        piece = dot_nt(grad_before, fc1_ref[:, cut])
        grad_normed2 = piece if grad_normed2 is None else grad_normed2 + piece
    out_ref[...] = result.astype(BF16).reshape(frames, tokens, width)

    grad_normed2 = grad_normed2.astype(BF16).astype(F32) * gain2
    grad_residual = cotangent.astype(F32) + normalise_back(grad_normed2, unit2, scale2)
    grad_residual_b = grad_residual.astype(BF16)
    proj_grad_ref[...] = dot_tn(attended_ref[...], grad_residual_b)
    attended_ref[...] = dot_nt(grad_residual_b, proj_ref[...]).astype(BF16)

    for frame in range(frames):
        at = slice(frame * tokens, (frame + 1) * tokens)
        for group in range(width // lanes):
            cut = slice(group * lanes, (group + 1) * lanes)
            cut_k = slice(width + group * lanes, width + (group + 1) * lanes)
            cut_v = slice(2 * width + group * lanes, 2 * width + (group + 1) * lanes)
            queries = packed_ref[at, cut]
            keys_in = packed_ref[at, cut_k]
            values_in = packed_ref[at, cut_v]
            grad_att = attended_ref[at, cut]
            grad_q = grad_k = grad_v = None
            for sub in range(per_group):
                mine = lane_head == sub
                mask = jnp.where(mine, 1.0, 0.0).astype(BF16)
                masked_q = queries * mask
                masked_g = grad_att * mask
                probs = probs_ref[(frame * HEADS) + group * per_group + sub]
                probs_b = probs.astype(BF16)
                grad_probs = dot_nt(masked_g, values_in).astype(BF16).astype(F32)
                inner = jnp.sum(grad_probs * probs, axis=-1, keepdims=True)
                grad_scores = (probs * (grad_probs - inner) * inv).astype(BF16)
                one_q = dot(grad_scores, keys_in)
                one_k = dot_tn(grad_scores, masked_q)
                one_v = dot_tn(probs_b, masked_g)
                grad_q = one_q if grad_q is None else jnp.where(mine, one_q, grad_q)
                grad_k = one_k if grad_k is None else grad_k + one_k
                grad_v = one_v if grad_v is None else grad_v + one_v
            grad_packed_ref[at, cut] = grad_q.astype(BF16)
            grad_packed_ref[at, cut_k] = grad_k.astype(BF16)
            grad_packed_ref[at, cut_v] = grad_v.astype(BF16)

    grad_packed = grad_packed_ref[...]
    grad_normed = dot_nt(grad_packed, qkv_ref[...]).astype(BF16).astype(F32) * gain1
    grad_embedded = (grad_residual + normalise_back(grad_normed, unit1, scale1)).astype(BF16)
    patches_ref[...] = dot_nt(grad_embedded, patch_ref[...]).astype(BF16)
    columns = column_ref[...]
    for lead in range(leads):
        turned = jnp.concatenate(
            [
                patches_ref[lead * pc : (lead + 1) * pc, inner * q_pad : (inner + 1) * q_pad]
                for inner in range(PATCH)
            ],
            axis=0,
        )
        pixels_ref[lead * q_pad : (lead + 1) * q_pad, :] = dot_tn(turned, columns).astype(BF16)
    order = match(wire_keys(sizes, rows_of(wire_rows)), patch_keys(sizes, cols_of(leads * q_pad)))
    moved = dot(order, pixels_ref[...]).astype(BF16)
    wire_out_ref[...] = moved.reshape(sizes.space, sizes.block, sizes.cols)

    qkv_grad_ref[...] = dot_tn(normed, grad_packed)
    me = me_ref[0]
    share = width // sizes.space
    for peer in range(sizes.space):
        at = slice(peer * share, (peer + 1) * share)
        pieces = [fc1_grad_ref[at, c * width : (c + 1) * width] for c in range(hidden_width // width)]
        wide = hidden_width // sizes.space
        pieces.append(fc2_grad_ref[peer * wide : (peer + 1) * wide, :])
        pieces += [qkv_grad_ref[at, c * width : (c + 1) * width] for c in range(3)]
        pieces.append(proj_grad_ref[at, :])
        grads_ref[me ^ peer] = jnp.concatenate(pieces, axis=0).astype(BF16)


def transformer(sizes, me, wire, cotangent, params):
    pos, patch, norm1, qkv, proj, norm2, fc1, fc2 = params
    tokens, width = pos.shape
    hidden_width = fc1.shape[1]
    count = sizes.per_dev * tokens
    share_rows = (qkv.size + proj.size + fc1.size + fc2.size) // (width * sizes.space)
    vmem = pl.BlockSpec(memory_space=pltpu.VMEM)
    return pl.pallas_call(
        functools.partial(block_kernel, sizes),
        in_specs=[pl.BlockSpec(memory_space=pltpu.SMEM)] + [vmem] * 10,
        out_specs=(vmem, vmem, vmem),
        out_shape=(
            jax.ShapeDtypeStruct(cotangent.shape, BF16),
            jax.ShapeDtypeStruct(wire.shape, BF16),
            jax.ShapeDtypeStruct((sizes.space, share_rows, width), BF16),
        ),
        scratch_shapes=[
            pltpu.VMEM((sizes.per_dev * sizes.patch_rows * sizes.q_pad, sizes.cols), BF16),
            pltpu.VMEM((count, PATCH * sizes.q_pad), BF16),
            pltpu.VMEM((sizes.cols, sizes.cols), BF16),
            pltpu.VMEM((count, 3 * width), BF16),
            pltpu.VMEM((sizes.per_dev * HEADS, tokens, tokens), F32),
            pltpu.VMEM((count, width), BF16),
            pltpu.VMEM((count, 3 * width), BF16),
            pltpu.VMEM(qkv.shape, F32),
            pltpu.VMEM(proj.shape, F32),
            pltpu.VMEM(fc1.shape, F32),
            pltpu.VMEM(fc2.shape, F32),
        ],
        compiler_params=pltpu.CompilerParams(vmem_limit_bytes=48 * MIB),
        cost_estimate=pl.CostEstimate(
            flops=6 * count * (patch.size + qkv.size + proj.size + fc1.size + fc2.size),
            bytes_accessed=16 * MIB,
            transcendentals=2 * count * hidden_width,
        ),
        name="transformer",
    )(me, wire, cotangent, pos, patch, norm1[None], qkv, proj, norm2[None], fc1, fc2)


def conv_weight_kernel(sizes, wire_ref, x_ref, out_ref, taps_ref, cross_ref, diag_ref):
    step = pl.program_id(0)
    wire_rows = sizes.space * sizes.block
    taps = TAPS * TAPS * COLOURS

    @pl.when(step == 0)
    def _():
        order = match(rows_of(sizes.ext * sizes.plane), tile_wire_keys(sizes, cols_of(wire_rows)))
        tile = dot(order, wire_ref[...].reshape(wire_rows, sizes.cols)).astype(BF16)
        for tap in range(TAPS):
            if tap == 1:
                moved = tile
            else:
                shift = match(rows_of(sizes.cols), cols_of(sizes.cols) + (1 - tap))
                moved = dot(tile, shift).astype(BF16)
            for ext in range(sizes.ext):
                at = ext * sizes.group + tap * sizes.plane
                taps_ref[at : at + sizes.plane, :] = moved[
                    ext * sizes.plane : (ext + 1) * sizes.plane
                ]

    x = x_ref[...].reshape(sizes.depth, sizes.cols)
    window = taps_ref[pl.ds(pl.multiple_of(step * sizes.group, 16), sizes.window), :]
    product = dot_nt(window, x)

    @pl.when(step == 0)
    def _():
        cross_ref[...] = product

    @pl.when(step > 0)
    def _():
        cross_ref[...] += product

    @pl.when(step == sizes.rows - 1)
    def _():
        diag_ref[...] = jnp.zeros(diag_ref.shape, F32)
        channel, frame_in = split(cols_of(sizes.depth), sizes.frames)
        lag = frame_in - rows_of(sizes.frames) + 2
        for tap in range(taps):
            cross = cross_ref[tap * sizes.frames : (tap + 1) * sizes.frames, :]
            row, rest = divmod(tap, TAPS * COLOURS)
            real = (TAPS - 1 - row) * TAPS * COLOURS + rest
            for a in range(TAPS):
                at = a * taps + real
                diag_ref[at : at + 1, :] = jnp.sum(
                    jnp.where(lag == a, cross, 0.0), axis=0, keepdims=True
                )
        spread = match(rows_of(out_ref.shape[1]), channel)
        left = diag_ref[...]
        total = jnp.zeros(out_ref.shape, F32)
        for _ in range(3):
            part = left.astype(BF16)
            left = left - part.astype(F32)
            total = total + dot_nt(part, spread)
        out_ref[...] = total


def conv_weight_grad(sizes, wire, x):
    taps = TAPS * TAPS * TAPS * COLOURS
    taps_pad = round_up(taps, 16)
    lanes = round_up(sizes.channels, 128)
    return pl.pallas_call(
        functools.partial(conv_weight_kernel, sizes),
        grid=(sizes.rows,),
        in_specs=[
            pl.BlockSpec(wire.shape, lambda h: (0, 0, 0)),
            pl.BlockSpec((sizes.channels, 1, sizes.frames, sizes.cols), lambda h: (0, h, 0, 0)),
        ],
        out_specs=(
            pl.BlockSpec((taps_pad, lanes), lambda h: (0, 0)),
            pl.BlockSpec((sizes.ext * sizes.group, sizes.cols), lambda h: (0, 0)),
        ),
        out_shape=(
            jax.ShapeDtypeStruct((taps_pad, lanes), F32),
            jax.ShapeDtypeStruct((sizes.ext * sizes.group, sizes.cols), BF16),
        ),
        scratch_shapes=[
            pltpu.VMEM((sizes.window, sizes.depth), F32),
            pltpu.VMEM((taps_pad, sizes.depth), F32),
        ],
        compiler_params=pltpu.CompilerParams(vmem_limit_bytes=48 * MIB),
        cost_estimate=pl.CostEstimate(
            flops=2 * sizes.rows * sizes.window * sizes.depth * sizes.cols,
            bytes_accessed=2 * x.size,
            transcendentals=0,
        ),
        name="conv_weight_grad",
    )(wire, x)


def feature_kernel(sizes, band_ref, taps_ref, out_ref):
    step = pl.program_id(0)
    window = taps_ref[pl.ds(pl.multiple_of(step * sizes.group, 16), sizes.window), :]
    out_ref[...] = dot(band_ref[...], window).astype(BF16).reshape(out_ref.shape)


def feature_gradient(sizes, band, taps):
    shape = (sizes.channels, sizes.rows, sizes.frames, sizes.cols)
    return pl.pallas_call(
        functools.partial(feature_kernel, sizes),
        grid=(sizes.rows,),
        in_specs=[
            pl.BlockSpec(band.shape, lambda h: (0, 0)),
            pl.BlockSpec(taps.shape, lambda h: (0, 0)),
        ],
        out_specs=pl.BlockSpec((shape[0], 1, shape[2], shape[3]), lambda h: (0, h, 0, 0)),
        out_shape=jax.ShapeDtypeStruct(shape, BF16),
        compiler_params=pltpu.CompilerParams(vmem_limit_bytes=48 * MIB),
        cost_estimate=pl.CostEstimate(
            flops=2 * sizes.rows * sizes.window * sizes.depth * sizes.cols,
            bytes_accessed=2 * math.prod(shape),
            transcendentals=0,
        ),
        name="feature_grad",
    )(band, taps)


def swap(values, axis, bit):
    return lax.ppermute(values, axis, [(i, i ^ (1 << bit)) for i in range(lax.axis_size(axis))])


def add(left, right):
    return (left.astype(F32) + right.astype(F32)).astype(BF16)


def reduce_blocks(blocks, bits):
    size = len(bits)
    blocks = blocks.reshape((2,) * size + blocks.shape[1:])
    while bits:
        bit, bits = bits[0], bits[1:]
        dim = blocks.ndim - 3 - sorted((bit,) + bits).index(bit)
        keep = lax.index_in_dim(blocks, 0, dim, keepdims=False)
        send = lax.index_in_dim(blocks, 1, dim, keepdims=False)
        blocks = add(keep, swap(send, "space", bit))
    return blocks


def sum_over_dp(values):
    index = lax.axis_index("dp")
    stages = (lax.axis_size("dp") - 1).bit_length()
    for bit in range(stages):
        mine = (index >> bit) & 1
        half = values.shape[0] // 2
        low, high = values[:half], values[half:]
        keep = jnp.where(mine == 0, low, high)
        send = jnp.where(mine == 0, high, low)
        values = add(keep, swap(send, "dp", bit))
    for bit in reversed(range(stages)):
        mine = (index >> bit) & 1
        other = swap(values, "dp", bit)
        values = jnp.where(
            mine == 0,
            jnp.concatenate([values, other], axis=0),
            jnp.concatenate([other, values], axis=0),
        )
    return values


def shards(
    features,
    conv_weight,
    out_grad,
    pos_embed,
    patch_weight,
    norm1,
    qkv_weight,
    proj_weight,
    norm2,
    fc1_weight,
    fc2_weight,
):
    space = lax.axis_size("space")
    sizes = Sizes(features, space)
    width = pos_embed.shape[1]
    hidden_width = fc1_weight.shape[1]
    me = lax.axis_index("space").astype(jnp.int32).reshape(1)
    x = features[0].transpose(0, 2, 1, 3)
    taps = conv_weight.reshape(-1, sizes.channels)

    wire = conv_forward(sizes, taps, x)
    wire = lax.all_to_all(wire, "space", split_axis=0, concat_axis=0, tiled=True)
    patch, band = prepare(sizes, taps, patch_weight)
    params = (pos_embed, patch, norm1, qkv_weight, proj_weight, norm2, fc1_weight, fc2_weight)
    block_out, wire_grad, grads = transformer(sizes, me, wire, out_grad[0], params)

    wire_grad = lax.all_to_all(wire_grad, "space", split_axis=0, concat_axis=0, tiled=True)
    conv_part, tap_rows = conv_weight_grad(sizes, wire_grad, x)
    feature_grad = feature_gradient(sizes, band, tap_rows)

    bits = tuple(range((space - 1).bit_length()))
    rows = grads.shape[1]
    half = rows // 2
    first = reduce_blocks(grads[:, :half], bits)
    second = reduce_blocks(grads[:, half:], bits[:1] + bits[2:] + bits[1:2])
    total = sum_over_dp(jnp.concatenate([first, second], axis=0)).astype(F32)

    share = width // space
    wide = hidden_width // space
    parts = hidden_width // width
    at = 0
    fc1_grad = jnp.concatenate([total[i * share : (i + 1) * share] for i in range(parts)], axis=1)
    at = parts * share
    fc2_grad = total[at : at + wide]
    at += wide
    qkv_grad = jnp.concatenate(
        [total[at + i * share : at + (i + 1) * share] for i in range(3)], axis=1
    )
    proj_grad = total[at + 3 * share :]

    conv_all = lax.all_to_all(
        jnp.broadcast_to(conv_part.astype(BF16)[None], (space,) + conv_part.shape),
        "space",
        split_axis=0,
        concat_axis=0,
        tiled=True,
    )
    conv_total = jnp.sum(conv_all.astype(F32), axis=0)
    for bit in range((lax.axis_size("dp") - 1).bit_length()):
        conv_total = conv_total + swap(conv_total, "dp", bit)
    conv_total = conv_total[: taps.shape[0], : sizes.channels].reshape(conv_weight.shape)

    return (
        block_out[None],
        feature_grad.transpose(0, 2, 1, 3)[None],
        conv_total,
        qkv_grad,
        proj_grad,
        fc1_grad,
        fc2_grad,
    )


def solution(mesh):
    placed = (
        P("dp", None, None, "space", None),
        P(),
        P("dp", "space", None, None),
        P(),
        P(),
        P(),
        P(),
        P(),
        P(),
        P(),
        P(),
    )
    return jax.shard_map(
        shards,
        mesh=mesh,
        in_specs=placed,
        out_specs=(
            P("dp", "space", None, None),
            P("dp", None, None, "space", None),
            P(),
            P("space", None),
            P("space", None),
            P("space", None),
            P("space", None),
        ),
        check_vma=False,
    )
```

```python
import functools
import math

import jax
import jax.numpy as jnp
from jax import lax
from jax.experimental import pallas as pl
from jax.experimental.pallas import tpu as pltpu
from jax.sharding import PartitionSpec as P

HEADS = 6
PATCH = 14
COLOURS = 3
TAPS = 3
F32 = jnp.float32
BF16 = jnp.bfloat16
MIB = 1 << 20
VMEM = pl.BlockSpec(memory_space=pltpu.VMEM)
SMEM = pl.BlockSpec(memory_space=pltpu.SMEM)
HBM = pl.BlockSpec(memory_space=pltpu.HBM)


def in_hbm(array):
    return pltpu.with_memory_space_constraint(array, pltpu.HBM)


def dot(a, b):
    return jnp.dot(a, b, preferred_element_type=F32)


def dot_nt(a, b):
    return lax.dot_general(a, b, (((1,), (1,)), ((), ())), preferred_element_type=F32)


def dot_tn(a, b):
    return lax.dot_general(a, b, (((0,), (0,)), ((), ())), preferred_element_type=F32)


def split(index, size):
    if size & (size - 1) == 0:
        shift = size.bit_length() - 1
        return index >> shift, index & (size - 1)
    high = jnp.floor((index.astype(F32) + 0.5) * (1.0 / size)).astype(jnp.int32)
    return high, index - high * size


def rows_of(count):
    return lax.broadcasted_iota(jnp.int32, (count, 1), 0)


def cols_of(count):
    return lax.broadcasted_iota(jnp.int32, (1, count), 1)


def match(left, right):
    return jnp.where(left == right, 1.0, 0.0).astype(BF16)


def round_up(value, unit):
    return -(-value // unit) * unit


class Sizes:
    def __init__(self, features, space):
        self.space = space
        self.channels, self.frames, self.rows, self.cols = features.shape[1:]
        self.per_dev = self.frames // space
        self.ext = self.rows + 2
        self.height = self.rows * space
        self.patch_rows = self.height // PATCH
        self.patch_cols = self.cols // PATCH
        self.tokens = self.patch_rows * self.patch_cols
        self.block = round_up(self.ext * COLOURS * self.per_dev, 16)
        self.q_used = COLOURS * PATCH
        self.q_pad = round_up(self.q_used, 64)
        self.plane = COLOURS * self.frames
        self.group = TAPS * self.plane
        self.window = TAPS * self.group
        self.depth = self.channels * self.frames


def wire_keys(sizes, index):
    peer, rest = split(index, sizes.block)
    plane, frame = split(rest, sizes.per_dev)
    ext, colour = split(plane, COLOURS)
    key = (frame * COLOURS + colour) * 4096 + peer * sizes.rows + ext
    return jnp.where(plane < sizes.ext * COLOURS, key, -2)


def patch_keys(sizes, index):
    lead, q = split(index, sizes.q_pad)
    frame, patch_row = split(lead, sizes.patch_rows)
    colour, row = split(q, PATCH)
    key = (frame * COLOURS + colour) * 4096 + patch_row * PATCH + row + 1
    return jnp.where(q < sizes.q_used, key, -1)


def tile_keys(sizes, index):
    return index


def tile_wire_keys(sizes, index):
    peer, rest = split(index, sizes.block)
    plane, frame = split(rest, sizes.per_dev)
    key = plane * sizes.frames + peer * sizes.per_dev + frame
    return jnp.where(plane < sizes.ext * COLOURS, key, -2)


def flipped(tap):
    row, _ = split(tap, TAPS * COLOURS)
    return tap + (TAPS - 1 - 2 * row) * (TAPS * COLOURS)


def column_order(sizes):
    inner, patch = split(rows_of(sizes.cols), sizes.patch_cols)
    return match(patch * PATCH + inner, cols_of(sizes.cols))


def conv_forward_kernel(
    sizes, weight_ref, x_hbm, out_ref, x_ref, band_ref, acc_ref, plane_ref, sems
):
    taps = TAPS * TAPS * COLOURS

    def arrival(row):
        return pltpu.make_async_copy(x_hbm.at[:, row], x_ref.at[row], sems.at[row])

    for row in range(sizes.rows):
        arrival(row).start()

    channel, frame_in = split(cols_of(sizes.depth), sizes.frames)
    spread = match(rows_of(sizes.channels), channel)
    wide = dot(weight_ref[...], spread)
    lag = frame_in - rows_of(sizes.frames) + 2
    here = [lag == a for a in range(TAPS)]
    for tap in range(taps):
        row, rest = divmod(tap, TAPS * COLOURS)
        real = (TAPS - 1 - row) * TAPS * COLOURS + rest
        block = jnp.zeros((sizes.frames, sizes.depth), F32)
        for a in range(TAPS):
            at = a * taps + real
            block = jnp.where(here[a], wide[at : at + 1, :], block)
        band_ref[tap * sizes.frames : (tap + 1) * sizes.frames, :] = block.astype(BF16)
    acc_ref[...] = jnp.zeros(acc_ref.shape, F32)

    def step(row, carry):
        arrival(row).wait()
        x = x_ref[row].reshape(sizes.depth, sizes.cols)
        at = pl.ds(pl.multiple_of(row * sizes.group, 16), sizes.window)
        acc_ref[at, :] += dot(band_ref[...], x)
        return carry

    lax.fori_loop(0, sizes.rows, step, 0)

    zero = jnp.zeros((sizes.plane, 1), F32)
    for ext in range(sizes.ext):
        at = ext * sizes.group
        first = acc_ref[at : at + sizes.plane, :]
        second = acc_ref[at + sizes.plane : at + 2 * sizes.plane, :]
        third = acc_ref[at + 2 * sizes.plane : at + 3 * sizes.plane, :]
        first = jnp.concatenate([zero, first[:, : sizes.cols - 1]], axis=1)
        third = jnp.concatenate([third[:, 1:], zero], axis=1)
        plane_ref[ext * sizes.plane : (ext + 1) * sizes.plane, :] = (
            first + second + third
        ).astype(BF16)
    wire = tile_wire_keys(sizes, rows_of(sizes.space * sizes.block))
    order = match(wire, cols_of(sizes.ext * sizes.plane))
    moved = dot(order, plane_ref[...]).astype(BF16)
    out_ref[...] = moved.reshape(sizes.space, sizes.block, sizes.cols)


def conv_forward(sizes, weight, x):
    return pl.pallas_call(
        functools.partial(conv_forward_kernel, sizes),
        in_specs=[VMEM, HBM],
        out_specs=VMEM,
        out_shape=jax.ShapeDtypeStruct((sizes.space, sizes.block, sizes.cols), BF16),
        scratch_shapes=[
            pltpu.VMEM((sizes.rows, sizes.channels, sizes.frames, sizes.cols), BF16),
            pltpu.VMEM((sizes.window, sizes.depth), BF16),
            pltpu.VMEM((sizes.ext * sizes.group, sizes.cols), F32),
            pltpu.VMEM((sizes.ext * sizes.plane, sizes.cols), BF16),
            pltpu.SemaphoreType.DMA((sizes.rows,)),
        ],
        compiler_params=pltpu.CompilerParams(vmem_limit_bytes=32 * MIB),
        cost_estimate=pl.CostEstimate(
            flops=2 * sizes.rows * sizes.window * sizes.depth * sizes.cols,
            bytes_accessed=2 * x.size,
            transcendentals=0,
        ),
        name="conv_forward",
    )(weight, x)


def prepare_kernel(sizes, weight_ref, patch_ref, patch_out_ref, band_ref):
    step = pl.program_id(0)
    taps = TAPS * TAPS * COLOURS

    @pl.when(step == 0)
    def _():
        inner, q = split(rows_of(PATCH * sizes.q_pad), sizes.q_pad)
        source = jnp.where(q < sizes.q_used, q * PATCH + inner, -1)
        order = match(source, cols_of(patch_ref.shape[0]))
        patch_out_ref[...] = dot(order, patch_ref[...]).astype(BF16)

    chunk = band_ref.shape[0]
    tap, frame_in = split(cols_of(sizes.window), sizes.frames)
    pick = match(rows_of(taps), flipped(tap))
    channel, frame_out = split(rows_of(chunk) + step * chunk, sizes.frames)
    spread = match(channel, cols_of(sizes.channels))
    lag = frame_out - frame_in + 2
    total = None
    for a in range(TAPS):
        weight = weight_ref[a * taps : (a + 1) * taps, :]
        wide = dot(spread, dot_tn(weight, pick).astype(BF16))
        wide = jnp.where(lag == a, wide, 0.0)
        total = wide if total is None else total + wide
    band_ref[...] = total.astype(BF16)


def prepare(sizes, weight, patch_weight):
    width = patch_weight.shape[1]
    steps = 4
    patch_shape = (PATCH * sizes.q_pad, width)
    return pl.pallas_call(
        functools.partial(prepare_kernel, sizes),
        grid=(steps,),
        in_specs=[
            pl.BlockSpec(weight.shape, lambda i: (0, 0)),
            pl.BlockSpec(patch_weight.shape, lambda i: (0, 0)),
        ],
        out_specs=(
            pl.BlockSpec(patch_shape, lambda i: (0, 0)),
            pl.BlockSpec((sizes.depth // steps, sizes.window), lambda i: (i, 0)),
        ),
        out_shape=(
            pltpu.HBM(patch_shape, BF16),
            pltpu.HBM((sizes.depth, sizes.window), BF16),
        ),
        compiler_params=pltpu.CompilerParams(vmem_limit_bytes=24 * MIB),
        cost_estimate=pl.CostEstimate(
            flops=4 * 10**9, bytes_accessed=4 * MIB, transcendentals=0
        ),
        name="prepare",
    )(weight, patch_weight)


def normalise(values):
    average = jnp.mean(values, axis=-1, keepdims=True)
    centered = values - average
    variance = jnp.mean(centered * centered, axis=-1, keepdims=True)
    scale = lax.rsqrt(variance + 1e-06)
    return centered * scale, scale


def normalise_back(grad, unit, scale):
    mean_grad = jnp.mean(grad, axis=-1, keepdims=True)
    mean_both = jnp.mean(grad * unit, axis=-1, keepdims=True)
    return scale * (grad - mean_grad - unit * mean_both)


def fetch(pairs, sems):
    copies = [pltpu.make_async_copy(src, dst, sems.at[i]) for i, (src, dst) in enumerate(pairs)]
    for copy in copies:
        copy.start()
    return copies


def first_kernel(
    sizes,
    wire_ref,
    norm1_ref,
    norm2_ref,
    patch_hbm,
    pos_hbm,
    cotangent_hbm,
    qkv_hbm,
    proj_hbm,
    fc1_hbm,
    fc2_hbm,
    out_ref,
    normed_ref,
    packed_ref,
    probs_ref,
    attended_ref,
    unit_ref,
    scale_ref,
    grad_ref,
    normed2_ref,
    hidden_ref,
    grad_before_ref,
    pixels_ref,
    patches_ref,
    *held,
):
    fixed = (patch_hbm, pos_hbm, cotangent_hbm, qkv_hbm, proj_hbm, fc1_hbm, fc2_hbm)
    arrivals = fetch(tuple(zip(fixed, held[:-1])), held[-1])
    patch_ref, pos_ref, cotangent_ref, qkv_ref, proj_ref, fc1_ref, fc2_ref = held[:-1]
    tokens, width = pos_ref.shape
    frames = sizes.per_dev
    count = frames * tokens
    hidden_width = fc1_ref.shape[1]
    head = width // HEADS
    wire_rows = sizes.space * sizes.block
    leads = frames * sizes.patch_rows
    q_pad = sizes.q_pad
    pc = sizes.patch_cols

    order = match(patch_keys(sizes, rows_of(leads * q_pad)), wire_keys(sizes, cols_of(wire_rows)))
    pixels_ref[...] = dot(order, wire_ref[...].reshape(wire_rows, sizes.cols)).astype(BF16)
    columns = column_order(sizes)
    for lead in range(leads):
        turned = dot_nt(columns, pixels_ref[lead * q_pad : (lead + 1) * q_pad, :])
        for inner in range(PATCH):
            patches_ref[lead * pc : (lead + 1) * pc, inner * q_pad : (inner + 1) * q_pad] = turned[
                inner * pc : (inner + 1) * pc, :
            ].astype(BF16)

    for arrival in arrivals:
        arrival.wait()
    pos = pos_ref[...].astype(F32)
    embedded = dot(patches_ref[...], patch_ref[...])
    embedded = embedded + (pos if frames == 1 else jnp.concatenate([pos] * frames, axis=0))
    unit1, scale1 = normalise(embedded)
    unit_ref[...] = unit1
    scale_ref[...] = scale1
    normed = (unit1 * norm1_ref[...]).astype(BF16)
    normed_ref[...] = normed
    packed_ref[...] = dot(normed, qkv_ref[...]).astype(BF16)

    lanes = min(128, width)
    per_group = lanes // head
    lane_head, _ = split(cols_of(lanes), head)
    inv = 1.0 / float(head) ** 0.5
    for frame in range(frames):
        at = slice(frame * tokens, (frame + 1) * tokens)
        for group in range(width // lanes):
            cut = slice(group * lanes, (group + 1) * lanes)
            queries = packed_ref[at, cut]
            keys_in = packed_ref[at, width + group * lanes : width + (group + 1) * lanes]
            values_in = packed_ref[at, 2 * width + group * lanes : 2 * width + (group + 1) * lanes]
            joined = None
            for sub in range(per_group):
                mine = lane_head == sub
                masked = queries * jnp.where(mine, 1.0, 0.0).astype(BF16)
                scores = dot_nt(masked, keys_in) * inv
                scores = jnp.exp(scores - jnp.max(scores, axis=-1, keepdims=True))
                probs = scores / jnp.sum(scores, axis=-1, keepdims=True)
                probs_ref[(frame * HEADS) + group * per_group + sub] = probs
                value = dot(probs.astype(BF16), values_in)
                joined = value if joined is None else jnp.where(mine, value, joined)
            attended_ref[at, cut] = joined.astype(BF16)

    residual = embedded + dot(attended_ref[...], proj_ref[...])
    unit2, scale2 = normalise(residual)
    gain2 = norm2_ref[...]
    normed2 = (unit2 * gain2).astype(BF16)
    normed2_ref[...] = normed2
    cotangent = cotangent_ref[...].reshape(count, width)

    chunk = width
    result = residual
    grad_normed2 = None
    for part in range(hidden_width // chunk):
        cut = slice(part * chunk, (part + 1) * chunk)
        before = dot(normed2, fc1_ref[:, cut])
        cdf = 0.5 + 0.5 * lax.erf(before * math.sqrt(0.5))
        hidden = (before * cdf).astype(BF16)
        result = result + dot(hidden, fc2_ref[cut, :])
        slope = cdf + before * (jnp.exp(-0.5 * before * before) * (1.0 / math.sqrt(2.0 * math.pi)))
        grad_hidden = dot_nt(cotangent, fc2_ref[cut, :]).astype(BF16)
        grad_before = (grad_hidden.astype(F32) * slope).astype(BF16)
        hidden_ref[:, cut] = hidden
        grad_before_ref[:, cut] = grad_before
        piece = dot_nt(grad_before, fc1_ref[:, cut])
        grad_normed2 = piece if grad_normed2 is None else grad_normed2 + piece
    out_ref[...] = result.astype(BF16).reshape(frames, tokens, width)

    grad_normed2 = grad_normed2.astype(BF16).astype(F32) * gain2
    grad_ref[...] = cotangent.astype(F32) + normalise_back(grad_normed2, unit2, scale2)


def second_kernel(
    sizes,
    packed_ref,
    probs_ref,
    grad_ref,
    unit_ref,
    scale_ref,
    norm1_ref,
    patch_hbm,
    qkv_hbm,
    proj_hbm,
    wire_hbm,
    grad_packed_ref,
    grad_att_ref,
    pixels_ref,
    patches_ref,
    wire_out_ref,
    patch_ref,
    qkv_ref,
    proj_ref,
    sems,
    wire_sem,
):
    pairs = ((proj_hbm, proj_ref), (qkv_hbm, qkv_ref), (patch_hbm, patch_ref))
    arrivals = fetch(pairs, sems)
    arrivals[0].wait()
    count, width = grad_ref.shape
    frames = sizes.per_dev
    tokens = count // frames
    head = width // HEADS
    wire_rows = sizes.space * sizes.block
    leads = frames * sizes.patch_rows
    q_pad = sizes.q_pad
    pc = sizes.patch_cols
    lanes = min(128, width)
    per_group = lanes // head
    lane_head, _ = split(cols_of(lanes), head)
    inv = 1.0 / float(head) ** 0.5

    grad_residual = grad_ref[...]
    grad_att_ref[...] = dot_nt(grad_residual.astype(BF16), proj_ref[...]).astype(BF16)
    for frame in range(frames):
        at = slice(frame * tokens, (frame + 1) * tokens)
        for group in range(width // lanes):
            cut = slice(group * lanes, (group + 1) * lanes)
            cut_k = slice(width + group * lanes, width + (group + 1) * lanes)
            cut_v = slice(2 * width + group * lanes, 2 * width + (group + 1) * lanes)
            queries = packed_ref[at, cut]
            keys_in = packed_ref[at, cut_k]
            values_in = packed_ref[at, cut_v]
            grad_att = grad_att_ref[at, cut]
            grad_q = grad_k = grad_v = None
            for sub in range(per_group):
                mine = lane_head == sub
                mask = jnp.where(mine, 1.0, 0.0).astype(BF16)
                masked_q = queries * mask
                masked_g = grad_att * mask
                probs = probs_ref[(frame * HEADS) + group * per_group + sub]
                probs_b = probs.astype(BF16)
                grad_probs = dot_nt(masked_g, values_in).astype(BF16).astype(F32)
                inner = jnp.sum(grad_probs * probs, axis=-1, keepdims=True)
                grad_scores = (probs * (grad_probs - inner) * inv).astype(BF16)
                one_q = dot(grad_scores, keys_in)
                one_k = dot_tn(grad_scores, masked_q)
                one_v = dot_tn(probs_b, masked_g)
                grad_q = one_q if grad_q is None else jnp.where(mine, one_q, grad_q)
                grad_k = one_k if grad_k is None else grad_k + one_k
                grad_v = one_v if grad_v is None else grad_v + one_v
            grad_packed_ref[at, cut] = grad_q.astype(BF16)
            grad_packed_ref[at, cut_k] = grad_k.astype(BF16)
            grad_packed_ref[at, cut_v] = grad_v.astype(BF16)

    for arrival in arrivals[1:]:
        arrival.wait()
    grad_normed = dot_nt(grad_packed_ref[...], qkv_ref[...]).astype(BF16).astype(F32) * norm1_ref[...]
    back = normalise_back(grad_normed, unit_ref[...], scale_ref[...])
    grad_embedded = (grad_residual + back).astype(BF16)
    patches_ref[...] = dot_nt(grad_embedded, patch_ref[...]).astype(BF16)
    columns = column_order(sizes)
    for lead in range(leads):
        turned = jnp.concatenate(
            [
                patches_ref[lead * pc : (lead + 1) * pc, inner * q_pad : (inner + 1) * q_pad]
                for inner in range(PATCH)
            ],
            axis=0,
        )
        pixels_ref[lead * q_pad : (lead + 1) * q_pad, :] = dot_tn(turned, columns).astype(BF16)
    order = match(wire_keys(sizes, rows_of(wire_rows)), patch_keys(sizes, cols_of(leads * q_pad)))
    moved = dot(order, pixels_ref[...]).astype(BF16)
    wire_out_ref[...] = moved.reshape(sizes.space, sizes.block, sizes.cols)
    leave = pltpu.make_async_copy(wire_out_ref, wire_hbm, wire_sem)
    leave.start()
    leave.wait()


def third_kernel(
    space,
    me_ref,
    normed_ref,
    grad_packed_ref,
    attended_ref,
    grad_ref,
    normed2_ref,
    grad_before_ref,
    hidden_ref,
    cotangent_ref,
    keep_ref,
    send_ref,
    qkv_grad_ref,
    proj_grad_ref,
    fc1_grad_ref,
    fc2_grad_ref,
):
    count, width = grad_ref.shape
    hidden_width = hidden_ref.shape[1]
    qkv_grad_ref[...] = dot_tn(normed_ref[...], grad_packed_ref[...])
    proj_grad_ref[...] = dot_tn(attended_ref[...], grad_ref[...].astype(BF16))
    fc1_grad_ref[...] = dot_tn(normed2_ref[...], grad_before_ref[...])
    fc2_grad_ref[...] = dot_tn(hidden_ref[...], cotangent_ref[...].reshape(count, width))
    share = width // space
    pieces = [(fc1_grad_ref, share, c) for c in range(0, hidden_width, width)]
    pieces.append((fc2_grad_ref, hidden_width // space, 0))
    pieces += [(qkv_grad_ref, share, c) for c in range(0, 3 * width, width)]
    pieces.append((proj_grad_ref, share, 0))
    spare = keep_ref.shape[1] - sum(rows for _, rows, _ in pieces)
    for chip in range(space // 2):
        for other, target in ((0, keep_ref), (1, send_ref)):
            peer = me_ref[0] ^ (2 * chip + other)
            blocks = [
                ref[pl.ds(pl.multiple_of(peer * rows, 8), rows), column : column + width]
                for ref, rows, column in pieces
            ]
            if spare:
                blocks.append(jnp.zeros((spare, width), F32))
            target[chip] = jnp.concatenate(blocks, axis=0).astype(BF16)


def transformer(sizes, copies, me, wire, cotangent, params):
    pos, patch, norm1, qkv, proj, norm2, fc1, fc2 = params
    tokens, width = pos.shape
    hidden_width = fc1.shape[1]
    count = sizes.per_dev * tokens
    pixel_shape = (sizes.per_dev * sizes.patch_rows * sizes.q_pad, sizes.cols)
    patches_shape = (count, PATCH * sizes.q_pad)
    norm1, norm2 = norm1[None], norm2[None]

    def held(*arrays):
        return [pltpu.VMEM(array.shape, array.dtype) for array in arrays] + [
            pltpu.SemaphoreType.DMA((len(arrays),))
        ]

    tall = jax.ShapeDtypeStruct((count, width), BF16)
    wide = jax.ShapeDtypeStruct((count, hidden_width), BF16)
    (
        block_out,
        normed,
        packed,
        probs,
        attended,
        unit,
        scale,
        grad,
        normed2,
        hidden,
        grad_before,
    ) = pl.pallas_call(
        functools.partial(first_kernel, sizes),
        in_specs=[VMEM] * 3 + [HBM] * 7,
        out_specs=(VMEM,) * 11,
        out_shape=(
            jax.ShapeDtypeStruct(cotangent.shape, BF16),
            tall,
            jax.ShapeDtypeStruct((count, 3 * width), BF16),
            jax.ShapeDtypeStruct((sizes.per_dev * HEADS, tokens, tokens), F32),
            tall,
            jax.ShapeDtypeStruct((count, width), F32),
            jax.ShapeDtypeStruct((count, 1), F32),
            jax.ShapeDtypeStruct((count, width), F32),
            tall,
            wide,
            wide,
        ),
        scratch_shapes=[
            pltpu.VMEM(pixel_shape, BF16),
            pltpu.VMEM(patches_shape, BF16),
        ]
        + held(patch, pos, cotangent, qkv, proj, fc1, fc2),
        compiler_params=pltpu.CompilerParams(vmem_limit_bytes=24 * MIB),
        cost_estimate=pl.CostEstimate(
            flops=4 * count * (patch.size + qkv.size + proj.size + fc1.size + fc2.size),
            bytes_accessed=12 * MIB,
            transcendentals=2 * count * hidden_width,
        ),
        name="block_forward",
    )(wire, norm1, norm2, patch, pos, cotangent, qkv, proj, fc1, fc2)

    wire_grad, grad_packed = pl.pallas_call(
        functools.partial(second_kernel, sizes),
        in_specs=[VMEM] * 6 + [HBM] * 3,
        out_specs=(HBM, VMEM),
        out_shape=(
            pltpu.HBM(wire.shape, BF16),
            jax.ShapeDtypeStruct((count, 3 * width), BF16),
        ),
        scratch_shapes=[
            pltpu.VMEM((count, width), BF16),
            pltpu.VMEM(pixel_shape, BF16),
            pltpu.VMEM(patches_shape, BF16),
            pltpu.VMEM(wire.shape, BF16),
        ]
        + held(patch, qkv, proj)
        + [pltpu.SemaphoreType.DMA(())],
        compiler_params=pltpu.CompilerParams(vmem_limit_bytes=20 * MIB),
        cost_estimate=pl.CostEstimate(
            flops=4 * count * (patch.size + qkv.size + proj.size),
            bytes_accessed=6 * MIB,
            transcendentals=0,
        ),
        name="block_backward",
    )(packed, probs, grad, unit, scale, norm1, patch, qkv, proj)

    total = qkv.size + proj.size + fc1.size + fc2.size
    rows = round_up(total // (width * sizes.space), 16 * copies)
    shares = jax.ShapeDtypeStruct((sizes.space // 2, rows, width), BF16)
    keep, send = pl.pallas_call(
        functools.partial(third_kernel, sizes.space),
        in_specs=[SMEM] + [VMEM] * 8,
        out_specs=(VMEM, VMEM),
        out_shape=(shares, shares),
        scratch_shapes=[pltpu.VMEM(array.shape, F32) for array in (qkv, proj, fc1, fc2)],
        compiler_params=pltpu.CompilerParams(vmem_limit_bytes=24 * MIB),
        cost_estimate=pl.CostEstimate(
            flops=2 * count * total, bytes_accessed=8 * MIB, transcendentals=0
        ),
        name="weight_grads",
    )(me, normed, grad_packed, attended, grad, normed2, grad_before, hidden, cotangent)
    return block_out, wire_grad, keep, send


def conv_weight_kernel(
    sizes, wire_ref, x_hbm, out_ref, taps_hbm, x_ref, taps_ref, cross_ref, diag_ref, sems, sem
):
    wire_rows = sizes.space * sizes.block
    taps = TAPS * TAPS * COLOURS

    def arrival(row):
        return pltpu.make_async_copy(x_hbm.at[:, row], x_ref.at[row], sems.at[row])

    for row in range(sizes.rows):
        arrival(row).start()

    order = match(rows_of(sizes.ext * sizes.plane), tile_wire_keys(sizes, cols_of(wire_rows)))
    tile = dot(order, wire_ref[...].reshape(wire_rows, sizes.cols)).astype(BF16)
    for tap in range(TAPS):
        if tap == 1:
            moved = tile
        else:
            shift = match(rows_of(sizes.cols), cols_of(sizes.cols) + (1 - tap))
            moved = dot(tile, shift).astype(BF16)
        for ext in range(sizes.ext):
            at = ext * sizes.group + tap * sizes.plane
            taps_ref[at : at + sizes.plane, :] = moved[ext * sizes.plane : (ext + 1) * sizes.plane]

    departure = pltpu.make_async_copy(taps_ref, taps_hbm, sem)
    departure.start()
    cross_ref[...] = jnp.zeros(cross_ref.shape, F32)

    def step(row, carry):
        arrival(row).wait()
        x = x_ref[row].reshape(sizes.depth, sizes.cols)
        window = taps_ref[pl.ds(pl.multiple_of(row * sizes.group, 16), sizes.window), :]
        cross_ref[...] += dot_nt(window, x)
        return carry

    lax.fori_loop(0, sizes.rows, step, 0)

    diag_ref[...] = jnp.zeros(diag_ref.shape, F32)
    channel, frame_in = split(cols_of(sizes.depth), sizes.frames)
    lag = frame_in - rows_of(sizes.frames) + 2
    for tap in range(taps):
        cross = cross_ref[tap * sizes.frames : (tap + 1) * sizes.frames, :]
        row, rest = divmod(tap, TAPS * COLOURS)
        real = (TAPS - 1 - row) * TAPS * COLOURS + rest
        for a in range(TAPS):
            at = a * taps + real
            diag_ref[at : at + 1, :] = jnp.sum(
                jnp.where(lag == a, cross, 0.0), axis=0, keepdims=True
            )
    spread = match(rows_of(out_ref.shape[1]), channel)
    left = diag_ref[...]
    total = jnp.zeros(out_ref.shape, F32)
    for _ in range(3):
        part = left.astype(BF16)
        left = left - part.astype(F32)
        total = total + dot_nt(part, spread)
    out_ref[...] = total
    departure.wait()


def conv_weight_grad(sizes, wire, x):
    taps = TAPS * TAPS * TAPS * COLOURS
    taps_pad = round_up(taps, 16)
    lanes = round_up(sizes.channels, 128)
    return pl.pallas_call(
        functools.partial(conv_weight_kernel, sizes),
        in_specs=[VMEM, HBM],
        out_specs=(VMEM, HBM),
        out_shape=(
            jax.ShapeDtypeStruct((taps_pad, lanes), F32),
            pltpu.HBM((sizes.ext * sizes.group, sizes.cols), BF16),
        ),
        scratch_shapes=[
            pltpu.VMEM((sizes.rows, sizes.channels, sizes.frames, sizes.cols), BF16),
            pltpu.VMEM((sizes.ext * sizes.group, sizes.cols), BF16),
            pltpu.VMEM((sizes.window, sizes.depth), F32),
            pltpu.VMEM((taps_pad, sizes.depth), F32),
            pltpu.SemaphoreType.DMA((sizes.rows,)),
            pltpu.SemaphoreType.DMA(()),
        ],
        compiler_params=pltpu.CompilerParams(vmem_limit_bytes=32 * MIB),
        cost_estimate=pl.CostEstimate(
            flops=2 * sizes.rows * sizes.window * sizes.depth * sizes.cols,
            bytes_accessed=2 * x.size,
            transcendentals=0,
        ),
        name="conv_weight_grad",
    )(wire, x)


def feature_kernel(
    sizes, band_hbm, taps_hbm, out_hbm, held_ref, band_ref, taps_ref, sems, fetch_sems
):
    arrivals = fetch(((band_hbm, band_ref), (taps_hbm, taps_ref)), fetch_sems)

    def departure(row):
        return pltpu.make_async_copy(held_ref.at[row], out_hbm.at[:, row], sems.at[row])

    def step(row, carry):
        window = taps_ref[pl.ds(pl.multiple_of(row * sizes.group, 16), sizes.window), :]
        held_ref[row] = dot(band_ref[...], window).astype(BF16).reshape(held_ref.shape[1:])
        departure(row).start()
        return carry

    for arrival in arrivals:
        arrival.wait()

    lax.fori_loop(0, sizes.rows, step, 0)

    def close(row, carry):
        departure(row).wait()
        return carry

    lax.fori_loop(0, sizes.rows, close, 0)


def feature_gradient(sizes, band, taps):
    shape = (sizes.channels, sizes.rows, sizes.frames, sizes.cols)
    return pl.pallas_call(
        functools.partial(feature_kernel, sizes),
        in_specs=[HBM, HBM],
        out_specs=HBM,
        out_shape=pltpu.HBM(shape, BF16),
        scratch_shapes=[
            pltpu.VMEM((sizes.rows, sizes.channels, sizes.frames, sizes.cols), BF16),
            pltpu.VMEM(band.shape, BF16),
            pltpu.VMEM(taps.shape, BF16),
            pltpu.SemaphoreType.DMA((sizes.rows,)),
            pltpu.SemaphoreType.DMA((2,)),
        ],
        compiler_params=pltpu.CompilerParams(vmem_limit_bytes=32 * MIB),
        cost_estimate=pl.CostEstimate(
            flops=2 * sizes.rows * sizes.window * sizes.depth * sizes.cols,
            bytes_accessed=2 * math.prod(shape),
            transcendentals=0,
        ),
        name="feature_grad",
    )(band, taps)


def scatter(values, axis):
    return lax.all_to_all(values, axis, split_axis=0, concat_axis=0, tiled=True)


def exchange(values, axis, relative):
    return lax.ppermute(values, axis, [(i, i ^ relative) for i in range(lax.axis_size(axis))])


def small_call(kernel, inputs, specs, outputs, name):
    return pl.pallas_call(
        kernel,
        in_specs=specs,
        out_specs=jax.tree.map(lambda _: VMEM, outputs),
        out_shape=outputs,
        compiler_params=pltpu.CompilerParams(vmem_limit_bytes=8 * MIB),
        name=name,
    )(*inputs)


def add_pair_kernel(keep_ref, got_ref, *out_refs):
    for place, out_ref in enumerate(out_refs):
        total = keep_ref[place].astype(F32) + got_ref[place].astype(F32)
        out_ref[...] = total.astype(BF16)


def add_pair(keep, got):
    outs = (jax.ShapeDtypeStruct(keep.shape[1:], BF16),) * keep.shape[0]
    return small_call(add_pair_kernel, (keep, got), [VMEM, VMEM], outs, "add_pair")


def add_cut_kernel(copies, me_ref, *refs):
    terms, outs = refs[:-copies], refs[-copies:]
    rows = outs[0].shape[0]
    for relative, out_ref in enumerate(outs):
        at = pl.ds(pl.multiple_of((me_ref[0] ^ relative) * rows, 16), rows)
        total = terms[0][at, :].astype(F32)
        for term in terms[1:]:
            total = total + term[at, :].astype(F32)
        out_ref[...] = total.astype(BF16)


def add_cut(me, copies, terms):
    rows, width = terms[0].shape
    outs = (jax.ShapeDtypeStruct((rows // copies, width), BF16),) * copies
    return small_call(
        functools.partial(add_cut_kernel, copies),
        (me,) + tuple(terms),
        [SMEM] + [VMEM] * len(terms),
        outs,
        "add_cut",
    )


def join_kernel(conv_ref, *refs):
    terms, out_ref = refs[:-1], refs[-1]
    rows = terms[0].shape[0]
    total = terms[0][...].astype(F32)
    for term in terms[1:]:
        total = total + term[...].astype(F32)
    out_ref[:rows, :] = total.astype(BF16)
    conv = conv_ref[0].astype(F32)
    for place in range(1, conv_ref.shape[0]):
        conv = conv + conv_ref[place].astype(F32)
    strips = out_ref.shape[1] // conv.shape[1]
    tall = conv.shape[0] // strips
    conv = [conv[strip * tall : (strip + 1) * tall] for strip in range(strips)]
    out_ref[rows:, :] = jnp.concatenate(conv, axis=1).astype(BF16)


def join(terms, conv_all):
    rows, width = terms[0].shape
    more = conv_all.shape[1] * conv_all.shape[2] // width
    out = jax.ShapeDtypeStruct((rows + more, width), BF16)
    return small_call(
        join_kernel, (conv_all,) + tuple(terms), [VMEM] * (1 + len(terms)), out, "join"
    )


def finish_kernel(copies, lanes, me_ref, *refs):
    pieces = refs[:copies]
    qkv_ref, proj_ref, fc1_ref, fc2_ref, conv_ref, whole = refs[copies:]
    width = proj_ref.shape[1]
    rows = whole.shape[0] // copies
    total = None
    for relative, piece in enumerate(pieces):
        at = pl.ds(pl.multiple_of((me_ref[0] ^ relative) * rows, 16), rows)
        whole[at, :] = piece[:rows, :].astype(F32)
        conv = piece[rows:, :].astype(F32)
        total = conv if total is None else total + conv
    share = proj_ref.shape[0]
    at = 0
    for part in range(0, fc1_ref.shape[1], width):
        fc1_ref[:, part : part + width] = whole[at : at + share, :]
        at += share
    fc2_ref[...] = whole[at : at + fc2_ref.shape[0], :]
    at += fc2_ref.shape[0]
    for part in range(0, qkv_ref.shape[1], width):
        qkv_ref[:, part : part + width] = whole[at : at + share, :]
        at += share
    proj_ref[...] = whole[at : at + share, :]
    total = jnp.concatenate(
        [total[:, strip : strip + lanes] for strip in range(0, width, lanes)], axis=0
    )
    time_taps, row_taps, col_taps, colours, channels = conv_ref.shape
    for a in range(time_taps):
        for b in range(row_taps):
            for e in range(col_taps):
                at = ((a * row_taps + b) * col_taps + e) * colours
                conv_ref[a, b, e] = total[at : at + colours, :channels]


def finish(me, pieces, rows, lanes, shapes):
    copies, width = len(pieces), pieces[0].shape[1]
    return pl.pallas_call(
        functools.partial(finish_kernel, copies, lanes),
        in_specs=[SMEM] + [VMEM] * copies,
        out_specs=(VMEM,) * 5,
        out_shape=tuple(jax.ShapeDtypeStruct(shape, F32) for shape in shapes),
        scratch_shapes=[pltpu.VMEM((copies * rows, width), F32)],
        compiler_params=pltpu.CompilerParams(vmem_limit_bytes=12 * MIB),
        name="finish",
    )(me, *pieces)


def shards(
    features,
    conv_weight,
    out_grad,
    pos_embed,
    patch_weight,
    norm1,
    qkv_weight,
    proj_weight,
    norm2,
    fc1_weight,
    fc2_weight,
):
    space = lax.axis_size("space")
    copies = lax.axis_size("dp")
    sizes = Sizes(features, space)
    width = pos_embed.shape[1]
    hidden_width = fc1_weight.shape[1]
    me = lax.axis_index("space").astype(jnp.int32).reshape(1)
    me_dp = lax.axis_index("dp").astype(jnp.int32).reshape(1)
    x = in_hbm(features[0].transpose(0, 2, 1, 3))
    taps = conv_weight.reshape(-1, sizes.channels)

    wire = conv_forward(sizes, taps, x)
    wire = scatter(wire, "space")
    patch, band = prepare(sizes, taps, patch_weight)
    patch = in_hbm(patch)
    pos, qkv, proj, fc1, fc2, cotangent = (
        in_hbm(array)
        for array in (pos_embed, qkv_weight, proj_weight, fc1_weight, fc2_weight, out_grad[0])
    )
    params = (pos, patch, norm1, qkv, proj, norm2, fc1, fc2)
    block_out, wire_grad, keep, send = transformer(sizes, copies, me, wire, cotangent, params)

    wire_grad = scatter(wire_grad, "space")
    conv_part, tap_rows = conv_weight_grad(sizes, wire_grad, x)
    feature_grad = feature_gradient(sizes, in_hbm(band), in_hbm(tap_rows))

    conv_all = scatter(
        jnp.broadcast_to(conv_part.astype(BF16)[None], (space,) + conv_part.shape), "space"
    )

    chips = add_pair(keep, exchange(send, "space", 1))
    terms = [exchange(chips[r], "space", 2 * r) for r in range(1, len(chips))]
    cuts = add_cut(me_dp, copies, [chips[0]] + terms)
    terms = [exchange(cuts[r], "dp", r) for r in range(1, copies)]
    conv_all, feature_grad = lax.optimization_barrier((conv_all, feature_grad))
    piece = join([cuts[0]] + terms, conv_all)
    pieces = [piece] + [exchange(piece, "dp", r) for r in range(1, copies)]
    share = width // space
    shapes = (
        (share, 3 * width),
        (share, width),
        (share, hidden_width),
        (hidden_width // space, width),
        conv_weight.shape,
    )
    qkv_grad, proj_grad, fc1_grad, fc2_grad, conv_grad = finish(
        me_dp, pieces, cuts[0].shape[0], conv_part.shape[1], shapes
    )

    return (
        block_out[None],
        feature_grad.transpose(0, 2, 1, 3)[None],
        conv_grad,
        qkv_grad,
        proj_grad,
        fc1_grad,
        fc2_grad,
    )


def solution(mesh):
    placed = (
        P("dp", None, None, "space", None),
        P(),
        P("dp", "space", None, None),
        P(),
        P(),
        P(),
        P(),
        P(),
        P(),
        P(),
        P(),
    )
    return jax.shard_map(
        shards,
        mesh=mesh,
        in_specs=placed,
        out_specs=(
            P("dp", "space", None, None),
            P("dp", None, None, "space", None),
            P(),
            P("space", None),
            P("space", None),
            P("space", None),
            P("space", None),
        ),
        check_vma=False,
    )
```

```python
import functools
import math

import jax
import jax.numpy as jnp
from jax import lax
from jax.experimental import pallas as pl
from jax.experimental.pallas import tpu as pltpu
from jax.sharding import PartitionSpec as P

HEADS = 6
PATCH = 14
COLOURS = 3
TAPS = 3
F32 = jnp.float32
BF16 = jnp.bfloat16
MIB = 1 << 20
VMEM = pl.BlockSpec(memory_space=pltpu.VMEM)
SMEM = pl.BlockSpec(memory_space=pltpu.SMEM)
HBM = pl.BlockSpec(memory_space=pltpu.HBM)


def in_hbm(array):
    return pltpu.with_memory_space_constraint(array, pltpu.HBM)


def dot(a, b):
    return jnp.dot(a, b, preferred_element_type=F32)


def dot_nt(a, b):
    return lax.dot_general(a, b, (((1,), (1,)), ((), ())), preferred_element_type=F32)


def dot_tn(a, b):
    return lax.dot_general(a, b, (((0,), (0,)), ((), ())), preferred_element_type=F32)


def split(index, size):
    if size & (size - 1) == 0:
        shift = size.bit_length() - 1
        return index >> shift, index & (size - 1)
    high = jnp.floor((index.astype(F32) + 0.5) * (1.0 / size)).astype(jnp.int32)
    return high, index - high * size


def rows_of(count):
    return lax.broadcasted_iota(jnp.int32, (count, 1), 0)


def cols_of(count):
    return lax.broadcasted_iota(jnp.int32, (1, count), 1)


def match(left, right):
    return jnp.where(left == right, 1.0, 0.0).astype(BF16)


def round_up(value, unit):
    return -(-value // unit) * unit


class Sizes:
    def __init__(self, features, space):
        self.space = space
        self.channels, self.frames, self.rows, self.cols = features.shape[1:]
        self.per_dev = self.frames // space
        self.ext = self.rows + 2
        self.height = self.rows * space
        self.patch_rows = self.height // PATCH
        self.patch_cols = self.cols // PATCH
        self.tokens = self.patch_rows * self.patch_cols
        self.block = round_up(self.ext * COLOURS * self.per_dev, 8)
        self.q_used = COLOURS * PATCH
        self.q_pad = round_up(self.q_used, 64)
        self.plane = COLOURS * self.frames
        self.group = TAPS * self.plane
        self.window = TAPS * self.group
        self.depth = self.channels * self.frames


def wire_keys(sizes, index):
    peer, rest = split(index, sizes.block)
    plane, frame = split(rest, sizes.per_dev)
    ext, colour = split(plane, COLOURS)
    key = (frame * COLOURS + colour) * 4096 + peer * sizes.rows + ext
    return jnp.where(plane < sizes.ext * COLOURS, key, -2)


def patch_keys(sizes, index):
    lead, q = split(index, sizes.q_pad)
    frame, patch_row = split(lead, sizes.patch_rows)
    colour, row = split(q, PATCH)
    key = (frame * COLOURS + colour) * 4096 + patch_row * PATCH + row + 1
    return jnp.where(q < sizes.q_used, key, -1)


def tile_keys(sizes, index):
    return index


def tile_wire_keys(sizes, index):
    peer, rest = split(index, sizes.block)
    plane, frame = split(rest, sizes.per_dev)
    key = plane * sizes.frames + peer * sizes.per_dev + frame
    return jnp.where(plane < sizes.ext * COLOURS, key, -2)


def flipped(tap):
    row, _ = split(tap, TAPS * COLOURS)
    return tap + (TAPS - 1 - 2 * row) * (TAPS * COLOURS)


def column_order(sizes):
    inner, patch = split(rows_of(sizes.cols), sizes.patch_cols)
    return match(patch * PATCH + inner, cols_of(sizes.cols))


def conv_forward_kernel(
    sizes, weight_ref, x_hbm, out_ref, weight_out_ref, x_ref, band_ref, acc_ref, plane_ref, rows_ref, sems
):
    taps = TAPS * TAPS * COLOURS

    def arrival(row):
        return pltpu.make_async_copy(x_hbm.at[:, row], x_ref.at[row], sems.at[row])

    for row in range(sizes.rows):
        arrival(row).start()

    channel, frame_in = split(cols_of(sizes.depth), sizes.frames)
    spread = match(rows_of(sizes.channels), channel)
    for at in range(weight_ref.shape[0]):
        rows_ref[at * COLOURS : (at + 1) * COLOURS, :] = weight_ref[at].astype(F32)
    weight_out_ref[...] = rows_ref[...].astype(BF16)
    wide = dot(weight_out_ref[...], spread)
    lag = frame_in - rows_of(sizes.frames) + 2
    here = [lag == a for a in range(TAPS)]
    for tap in range(taps):
        row, rest = divmod(tap, TAPS * COLOURS)
        real = (TAPS - 1 - row) * TAPS * COLOURS + rest
        block = jnp.zeros((sizes.frames, sizes.depth), F32)
        for a in range(TAPS):
            at = a * taps + real
            block = jnp.where(here[a], wide[at : at + 1, :], block)
        band_ref[tap * sizes.frames : (tap + 1) * sizes.frames, :] = block.astype(BF16)
    acc_ref[...] = jnp.zeros(acc_ref.shape, F32)

    def step(row, carry):
        arrival(row).wait()
        x = x_ref[row].reshape(sizes.depth, sizes.cols)
        at = pl.ds(pl.multiple_of(row * sizes.group, 16), sizes.window)
        acc_ref[at, :] += dot(band_ref[...], x)
        return carry

    lax.fori_loop(0, sizes.rows, step, 0)

    zero = jnp.zeros((sizes.plane, 1), F32)
    for ext in range(sizes.ext):
        at = ext * sizes.group
        first = acc_ref[at : at + sizes.plane, :]
        second = acc_ref[at + sizes.plane : at + 2 * sizes.plane, :]
        third = acc_ref[at + 2 * sizes.plane : at + 3 * sizes.plane, :]
        first = jnp.concatenate([zero, first[:, : sizes.cols - 1]], axis=1)
        third = jnp.concatenate([third[:, 1:], zero], axis=1)
        plane_ref[ext * sizes.plane : (ext + 1) * sizes.plane, :] = (
            first + second + third
        ).astype(BF16)
    wire = tile_wire_keys(sizes, rows_of(sizes.space * sizes.block))
    order = match(wire, cols_of(sizes.ext * sizes.plane))
    moved = dot(order, plane_ref[...]).astype(BF16)
    out_ref[...] = moved


def conv_forward(sizes, weight, x):
    return pl.pallas_call(
        functools.partial(conv_forward_kernel, sizes),
        in_specs=[VMEM, HBM],
        out_specs=(VMEM, VMEM),
        out_shape=(
            jax.ShapeDtypeStruct((sizes.space * sizes.block, sizes.cols), BF16),
            jax.ShapeDtypeStruct((weight.shape[0] * weight.shape[1], sizes.channels), BF16),
        ),
        scratch_shapes=[
            pltpu.VMEM((sizes.rows, sizes.channels, sizes.frames, sizes.cols), BF16),
            pltpu.VMEM((sizes.window, sizes.depth), BF16),
            pltpu.VMEM((sizes.ext * sizes.group, sizes.cols), F32),
            pltpu.VMEM((sizes.ext * sizes.plane, sizes.cols), BF16),
            pltpu.VMEM((weight.shape[0] * weight.shape[1], sizes.channels), F32),
            pltpu.SemaphoreType.DMA((sizes.rows,)),
        ],
        compiler_params=pltpu.CompilerParams(vmem_limit_bytes=32 * MIB),
        cost_estimate=pl.CostEstimate(
            flops=2 * sizes.rows * sizes.window * sizes.depth * sizes.cols,
            bytes_accessed=2 * x.size,
            transcendentals=0,
        ),
        name="conv_forward",
    )(weight, x)


def prepare_kernel(sizes, weight_ref, patch_ref, patch_out_ref, band_ref):
    step = pl.program_id(0)
    taps = TAPS * TAPS * COLOURS

    @pl.when(step == 0)
    def _():
        inner, q = split(rows_of(PATCH * sizes.q_pad), sizes.q_pad)
        source = jnp.where(q < sizes.q_used, q * PATCH + inner, -1)
        order = match(source, cols_of(patch_ref.shape[0]))
        patch_out_ref[...] = dot(order, patch_ref[...]).astype(BF16)

    chunk = band_ref.shape[0]
    tap, frame_in = split(cols_of(sizes.window), sizes.frames)
    pick = match(rows_of(taps), flipped(tap))
    channel, frame_out = split(rows_of(chunk) + step * chunk, sizes.frames)
    spread = match(channel, cols_of(sizes.channels))
    lag = frame_out - frame_in + 2
    total = None
    for a in range(TAPS):
        weight = weight_ref[a * taps : (a + 1) * taps, :]
        wide = dot(spread, dot_tn(weight, pick).astype(BF16))
        wide = jnp.where(lag == a, wide, 0.0)
        total = wide if total is None else total + wide
    band_ref[...] = total.astype(BF16)


def prepare(sizes, weight, patch_weight):
    width = patch_weight.shape[1]
    steps = 4
    patch_shape = (PATCH * sizes.q_pad, width)
    return pl.pallas_call(
        functools.partial(prepare_kernel, sizes),
        grid=(steps,),
        in_specs=[
            pl.BlockSpec(weight.shape, lambda i: (0, 0)),
            pl.BlockSpec(patch_weight.shape, lambda i: (0, 0)),
        ],
        out_specs=(
            pl.BlockSpec(patch_shape, lambda i: (0, 0)),
            pl.BlockSpec((sizes.depth // steps, sizes.window), lambda i: (i, 0)),
        ),
        out_shape=(
            pltpu.HBM(patch_shape, BF16),
            pltpu.HBM((sizes.depth, sizes.window), BF16),
        ),
        compiler_params=pltpu.CompilerParams(vmem_limit_bytes=24 * MIB),
        cost_estimate=pl.CostEstimate(
            flops=4 * 10**9, bytes_accessed=4 * MIB, transcendentals=0
        ),
        name="prepare",
    )(weight, patch_weight)


def normalise(values):
    average = jnp.mean(values, axis=-1, keepdims=True)
    centered = values - average
    variance = jnp.mean(centered * centered, axis=-1, keepdims=True)
    scale = lax.rsqrt(variance + 1e-06)
    return centered * scale, scale


def normalise_back(grad, unit, scale):
    mean_grad = jnp.mean(grad, axis=-1, keepdims=True)
    mean_both = jnp.mean(grad * unit, axis=-1, keepdims=True)
    return scale * (grad - mean_grad - unit * mean_both)


def fetch(pairs, sems):
    copies = [pltpu.make_async_copy(src, dst, sems.at[i]) for i, (src, dst) in enumerate(pairs)]
    for copy in copies:
        copy.start()
    return copies


def first_kernel(
    sizes,
    wire_ref,
    norm1_ref,
    norm2_ref,
    patch_hbm,
    pos_hbm,
    cotangent_hbm,
    qkv_hbm,
    proj_hbm,
    fc1_hbm,
    fc2_hbm,
    out_ref,
    normed_ref,
    packed_ref,
    probs_ref,
    probs_b_ref,
    attended_ref,
    unit_ref,
    scale_ref,
    grad_ref,
    normed2_ref,
    hidden_ref,
    grad_before_ref,
    patch_ref,
    qkv_ref,
    proj_ref,
    pixels_ref,
    patches_ref,
    pos_ref,
    cotangent_ref,
    fc1_ref,
    fc2_ref,
    sems,
):
    pairs = (
        (patch_hbm, patch_ref),
        (pos_hbm, pos_ref),
        (qkv_hbm, qkv_ref),
        (proj_hbm, proj_ref),
        (fc1_hbm, fc1_ref),
        (cotangent_hbm, cotangent_ref),
        (fc2_hbm, fc2_ref),
    )
    arrivals = fetch(pairs, sems)
    tokens, width = pos_ref.shape
    frames = sizes.per_dev
    count = frames * tokens
    hidden_width = fc1_ref.shape[1]
    head = width // HEADS
    wire_rows = sizes.space * sizes.block
    leads = frames * sizes.patch_rows
    q_pad = sizes.q_pad
    pc = sizes.patch_cols

    order = match(patch_keys(sizes, rows_of(leads * q_pad)), wire_keys(sizes, cols_of(wire_rows)))
    pixels_ref[...] = dot(order, wire_ref[...]).astype(BF16)
    columns = column_order(sizes)
    for lead in range(leads):
        turned = dot_nt(columns, pixels_ref[lead * q_pad : (lead + 1) * q_pad, :])
        for inner in range(PATCH):
            patches_ref[lead * pc : (lead + 1) * pc, inner * q_pad : (inner + 1) * q_pad] = turned[
                inner * pc : (inner + 1) * pc, :
            ].astype(BF16)

    for arrival in arrivals[:2]:
        arrival.wait()
    pos = pos_ref[...].astype(F32)
    embedded = dot(patches_ref[...], patch_ref[...])
    embedded = embedded + (pos if frames == 1 else jnp.concatenate([pos] * frames, axis=0))
    unit1, scale1 = normalise(embedded)
    unit_ref[...] = unit1
    scale_ref[...] = scale1
    normed = (unit1 * norm1_ref[...]).astype(BF16)
    normed_ref[...] = normed
    arrivals[2].wait()
    packed_ref[...] = dot(normed, qkv_ref[...]).astype(BF16)

    lanes = min(128, width)
    per_group = lanes // head
    lane_head, _ = split(cols_of(lanes), head)
    inv = 1.0 / float(head) ** 0.5
    masks = [jnp.where(lane_head == sub, 1.0, 0.0).astype(BF16) for sub in range(per_group)]
    places = [
        (frame, group, slice(frame * tokens, (frame + 1) * tokens))
        for frame in range(frames)
        for group in range(width // lanes)
    ]
    for frame, group, at in places:
        queries = packed_ref[at, group * lanes : (group + 1) * lanes]
        keys_in = packed_ref[at, width + group * lanes : width + (group + 1) * lanes]
        for sub in range(per_group):
            probs_ref[frame * HEADS + group * per_group + sub] = dot_nt(
                queries * masks[sub], keys_in
            )
    scores = probs_ref[...] * inv
    scores = jnp.exp(scores - jnp.max(scores, axis=-1, keepdims=True))
    probs = scores * (1.0 / jnp.sum(scores, axis=-1, keepdims=True))
    probs_ref[...] = probs
    probs_b_ref[...] = probs.astype(BF16)
    for frame, group, at in places:
        values_in = packed_ref[at, 2 * width + group * lanes : 2 * width + (group + 1) * lanes]
        joined = None
        for sub in range(per_group):
            value = dot(probs_b_ref[frame * HEADS + group * per_group + sub], values_in)
            joined = value if joined is None else jnp.where(lane_head == sub, value, joined)
        attended_ref[at, group * lanes : (group + 1) * lanes] = joined.astype(BF16)

    for arrival in arrivals[3:]:
        arrival.wait()
    residual = embedded + dot(attended_ref[...], proj_ref[...])
    unit2, scale2 = normalise(residual)
    gain2 = norm2_ref[...]
    normed2 = (unit2 * gain2).astype(BF16)
    normed2_ref[...] = normed2
    cotangent = cotangent_ref[...].reshape(count, width)

    chunk = width
    result = residual
    grad_normed2 = None
    for part in range(hidden_width // chunk):
        cut = slice(part * chunk, (part + 1) * chunk)
        before = dot(normed2, fc1_ref[:, cut])
        cdf = 0.5 + 0.5 * lax.erf(before * math.sqrt(0.5))
        hidden = (before * cdf).astype(BF16)
        result = result + dot(hidden, fc2_ref[cut, :])
        slope = cdf + before * (jnp.exp(-0.5 * before * before) * (1.0 / math.sqrt(2.0 * math.pi)))
        grad_hidden = dot_nt(cotangent, fc2_ref[cut, :]).astype(BF16)
        grad_before = (grad_hidden.astype(F32) * slope).astype(BF16)
        hidden_ref[:, cut] = hidden
        grad_before_ref[:, cut] = grad_before
        piece = dot_nt(grad_before, fc1_ref[:, cut])
        grad_normed2 = piece if grad_normed2 is None else grad_normed2 + piece
    out_ref[...] = result.astype(BF16).reshape(frames, tokens, width)

    grad_normed2 = grad_normed2.astype(BF16).astype(F32) * gain2
    grad_ref[...] = cotangent.astype(F32) + normalise_back(grad_normed2, unit2, scale2)


def second_kernel(
    sizes,
    packed_ref,
    probs_ref,
    probs_b_ref,
    grad_ref,
    unit_ref,
    scale_ref,
    norm1_ref,
    patch_ref,
    qkv_ref,
    proj_ref,
    wire_hbm,
    grad_packed_ref,
    grad_att_ref,
    scores_ref,
    scores_b_ref,
    pixels_ref,
    patches_ref,
    wire_out_ref,
    wire_sems,
):
    count, width = grad_ref.shape
    frames = sizes.per_dev
    tokens = count // frames
    head = width // HEADS
    wire_rows = sizes.space * sizes.block
    leads = frames * sizes.patch_rows
    q_pad = sizes.q_pad
    pc = sizes.patch_cols
    lanes = min(128, width)
    per_group = lanes // head
    lane_head, _ = split(cols_of(lanes), head)
    inv = 1.0 / float(head) ** 0.5

    grad_residual = grad_ref[...]
    grad_att_ref[...] = dot_nt(grad_residual.astype(BF16), proj_ref[...]).astype(BF16)
    masks = [jnp.where(lane_head == sub, 1.0, 0.0).astype(BF16) for sub in range(per_group)]
    places = [
        (frame, group, slice(frame * tokens, (frame + 1) * tokens))
        for frame in range(frames)
        for group in range(width // lanes)
    ]
    for frame, group, at in places:
        grad_att = grad_att_ref[at, group * lanes : (group + 1) * lanes]
        values_in = packed_ref[at, 2 * width + group * lanes : 2 * width + (group + 1) * lanes]
        for sub in range(per_group):
            scores_ref[frame * HEADS + group * per_group + sub] = dot_nt(
                grad_att * masks[sub], values_in
            )
    grad_probs = scores_ref[...].astype(BF16).astype(F32)
    weighted = grad_probs * probs_ref[...]
    inner = jnp.sum(weighted, axis=-1, keepdims=True)
    scores_b_ref[...] = ((weighted - probs_ref[...] * inner) * inv).astype(BF16)
    for frame, group, at in places:
        cut = slice(group * lanes, (group + 1) * lanes)
        cut_k = slice(width + group * lanes, width + (group + 1) * lanes)
        cut_v = slice(2 * width + group * lanes, 2 * width + (group + 1) * lanes)
        queries = packed_ref[at, cut]
        keys_in = packed_ref[at, cut_k]
        grad_att = grad_att_ref[at, cut]
        grad_q = grad_k = grad_v = None
        for sub in range(per_group):
            place = frame * HEADS + group * per_group + sub
            grad_scores = scores_b_ref[place]
            one_q = dot(grad_scores, keys_in)
            one_k = dot_tn(grad_scores, queries * masks[sub])
            one_v = dot_tn(probs_b_ref[place], grad_att * masks[sub])
            grad_q = one_q if grad_q is None else jnp.where(lane_head == sub, one_q, grad_q)
            grad_k = one_k if grad_k is None else grad_k + one_k
            grad_v = one_v if grad_v is None else grad_v + one_v
        grad_packed_ref[at, cut] = grad_q.astype(BF16)
        grad_packed_ref[at, cut_k] = grad_k.astype(BF16)
        grad_packed_ref[at, cut_v] = grad_v.astype(BF16)

    grad_normed = dot_nt(grad_packed_ref[...], qkv_ref[...]).astype(BF16).astype(F32) * norm1_ref[...]
    back = normalise_back(grad_normed, unit_ref[...], scale_ref[...])
    grad_embedded = (grad_residual + back).astype(BF16)
    patches_ref[...] = dot_nt(grad_embedded, patch_ref[...]).astype(BF16)
    columns = column_order(sizes)
    for lead in range(leads):
        turned = jnp.concatenate(
            [
                patches_ref[lead * pc : (lead + 1) * pc, inner * q_pad : (inner + 1) * q_pad]
                for inner in range(PATCH)
            ],
            axis=0,
        )
        pixels_ref[lead * q_pad : (lead + 1) * q_pad, :] = dot_tn(turned, columns).astype(BF16)
    order = match(wire_keys(sizes, rows_of(wire_rows)), patch_keys(sizes, cols_of(leads * q_pad)))
    parts = wire_sems.shape[0]
    tall = wire_rows // parts
    leaving = []
    for part in range(parts):
        at = slice(part * tall, (part + 1) * tall)
        wire_out_ref[at, :] = dot(order[at], pixels_ref[...]).astype(BF16)
        leaving.append(
            pltpu.make_async_copy(wire_out_ref.at[at, :], wire_hbm.at[at, :], wire_sems.at[part])
        )
        leaving[-1].start()
    for copy in leaving:
        copy.wait()


def third_kernel(
    space,
    me_ref,
    normed_ref,
    grad_packed_ref,
    attended_ref,
    grad_ref,
    normed2_ref,
    grad_before_ref,
    hidden_ref,
    cotangent_ref,
    keep_ref,
    send_ref,
    qkv_grad_ref,
    proj_grad_ref,
    fc1_grad_ref,
    fc2_grad_ref,
):
    count, width = grad_ref.shape
    hidden_width = hidden_ref.shape[1]
    qkv_grad_ref[...] = dot_tn(normed_ref[...], grad_packed_ref[...])
    proj_grad_ref[...] = dot_tn(attended_ref[...], grad_ref[...].astype(BF16))
    fc1_grad_ref[...] = dot_tn(normed2_ref[...], grad_before_ref[...])
    fc2_grad_ref[...] = dot_tn(hidden_ref[...], cotangent_ref[...].reshape(count, width))
    share = width // space
    pieces = [(fc1_grad_ref, share, c) for c in range(0, hidden_width, width)]
    pieces.append((fc2_grad_ref, hidden_width // space, 0))
    pieces += [(qkv_grad_ref, share, c) for c in range(0, 3 * width, width)]
    pieces.append((proj_grad_ref, share, 0))
    spare = keep_ref.shape[1] - sum(rows for _, rows, _ in pieces)
    for chip in range(space // 2):
        for other, target in ((0, keep_ref), (1, send_ref)):
            peer = me_ref[0] ^ (2 * chip + other)
            blocks = [
                ref[pl.ds(pl.multiple_of(peer * rows, 8), rows), column : column + width]
                for ref, rows, column in pieces
            ]
            if spare:
                blocks.append(jnp.zeros((spare, width), F32))
            target[chip] = jnp.concatenate(blocks, axis=0).astype(BF16)


def transformer(sizes, copies, me, wire, cotangent, params):
    pos, patch, norm1, qkv, proj, norm2, fc1, fc2 = params
    tokens, width = pos.shape
    hidden_width = fc1.shape[1]
    count = sizes.per_dev * tokens
    pixel_shape = (sizes.per_dev * sizes.patch_rows * sizes.q_pad, sizes.cols)
    patches_shape = (count, PATCH * sizes.q_pad)
    norm1, norm2 = norm1[None], norm2[None]

    tall = jax.ShapeDtypeStruct((count, width), BF16)
    wide = jax.ShapeDtypeStruct((count, hidden_width), BF16)
    (
        block_out,
        normed,
        packed,
        probs,
        probs_b,
        attended,
        unit,
        scale,
        grad,
        normed2,
        hidden,
        grad_before,
        patch,
        qkv,
        proj,
    ) = pl.pallas_call(
        functools.partial(first_kernel, sizes),
        in_specs=[VMEM] * 3 + [HBM] * 7,
        out_specs=(VMEM,) * 15,
        out_shape=(
            jax.ShapeDtypeStruct(cotangent.shape, BF16),
            tall,
            jax.ShapeDtypeStruct((count, 3 * width), BF16),
            jax.ShapeDtypeStruct((sizes.per_dev * HEADS, tokens, tokens), F32),
            jax.ShapeDtypeStruct((sizes.per_dev * HEADS, tokens, tokens), BF16),
            tall,
            jax.ShapeDtypeStruct((count, width), F32),
            jax.ShapeDtypeStruct((count, 1), F32),
            jax.ShapeDtypeStruct((count, width), F32),
            tall,
            wide,
            wide,
            jax.ShapeDtypeStruct(patch.shape, BF16),
            jax.ShapeDtypeStruct(qkv.shape, BF16),
            jax.ShapeDtypeStruct(proj.shape, BF16),
        ),
        scratch_shapes=[
            pltpu.VMEM(pixel_shape, BF16),
            pltpu.VMEM(patches_shape, BF16),
        ]
        + [pltpu.VMEM(array.shape, BF16) for array in (pos, cotangent, fc1, fc2)]
        + [pltpu.SemaphoreType.DMA((7,))],
        compiler_params=pltpu.CompilerParams(vmem_limit_bytes=24 * MIB),
        cost_estimate=pl.CostEstimate(
            flops=4 * count * (patch.size + qkv.size + proj.size + fc1.size + fc2.size),
            bytes_accessed=12 * MIB,
            transcendentals=2 * count * hidden_width,
        ),
        name="block_forward",
    )(wire, norm1, norm2, patch, pos, cotangent, qkv, proj, fc1, fc2)

    wire_grad, grad_packed = pl.pallas_call(
        functools.partial(second_kernel, sizes),
        in_specs=[VMEM] * 10,
        out_specs=(HBM, VMEM),
        out_shape=(
            pltpu.HBM(wire.shape, BF16),
            jax.ShapeDtypeStruct((count, 3 * width), BF16),
        ),
        scratch_shapes=[
            pltpu.VMEM((count, width), BF16),
            pltpu.VMEM(probs.shape, F32),
            pltpu.VMEM(probs.shape, BF16),
            pltpu.VMEM(pixel_shape, BF16),
            pltpu.VMEM(patches_shape, BF16),
            pltpu.VMEM(wire.shape, BF16),
            pltpu.SemaphoreType.DMA((4,)),
        ],
        compiler_params=pltpu.CompilerParams(vmem_limit_bytes=20 * MIB),
        cost_estimate=pl.CostEstimate(
            flops=4 * count * (patch.size + qkv.size + proj.size),
            bytes_accessed=6 * MIB,
            transcendentals=0,
        ),
        name="block_backward",
    )(packed, probs, probs_b, grad, unit, scale, norm1, patch, qkv, proj)

    total = qkv.size + proj.size + fc1.size + fc2.size
    rows = round_up(total // (width * sizes.space), 16 * copies)
    shares = jax.ShapeDtypeStruct((sizes.space // 2, rows, width), BF16)
    keep, send = pl.pallas_call(
        functools.partial(third_kernel, sizes.space),
        in_specs=[SMEM] + [VMEM] * 8,
        out_specs=(VMEM, VMEM),
        out_shape=(shares, shares),
        scratch_shapes=[pltpu.VMEM(array.shape, F32) for array in (qkv, proj, fc1, fc2)],
        compiler_params=pltpu.CompilerParams(vmem_limit_bytes=24 * MIB),
        cost_estimate=pl.CostEstimate(
            flops=2 * count * total, bytes_accessed=8 * MIB, transcendentals=0
        ),
        name="weight_grads",
    )(me, normed, grad_packed, attended, grad, normed2, grad_before, hidden, cotangent)
    return block_out, wire_grad, keep, send


def conv_weight_kernel(
    sizes, wire_ref, x_hbm, out_ref, taps_hbm, x_ref, taps_ref, cross_ref, diag_ref, sems, sem
):
    wire_rows = sizes.space * sizes.block
    taps = TAPS * TAPS * COLOURS

    def arrival(row):
        return pltpu.make_async_copy(x_hbm.at[:, row], x_ref.at[row], sems.at[row])

    for row in range(sizes.rows):
        arrival(row).start()

    order = match(rows_of(sizes.ext * sizes.plane), tile_wire_keys(sizes, cols_of(wire_rows)))
    tile = dot(order, wire_ref[...]).astype(BF16)
    for tap in range(TAPS):
        if tap == 1:
            moved = tile
        else:
            shift = match(rows_of(sizes.cols), cols_of(sizes.cols) + (1 - tap))
            moved = dot(tile, shift).astype(BF16)
        for ext in range(sizes.ext):
            at = ext * sizes.group + tap * sizes.plane
            taps_ref[at : at + sizes.plane, :] = moved[ext * sizes.plane : (ext + 1) * sizes.plane]

    departure = pltpu.make_async_copy(taps_ref, taps_hbm, sem)
    departure.start()
    cross_ref[...] = jnp.zeros(cross_ref.shape, F32)

    def step(row, carry):
        arrival(row).wait()
        x = x_ref[row].reshape(sizes.depth, sizes.cols)
        window = taps_ref[pl.ds(pl.multiple_of(row * sizes.group, 16), sizes.window), :]
        cross_ref[...] += dot_nt(window, x)
        return carry

    lax.fori_loop(0, sizes.rows, step, 0)

    diag_ref[...] = jnp.zeros(diag_ref.shape, F32)
    channel, frame_in = split(cols_of(sizes.depth), sizes.frames)
    lag = frame_in - rows_of(sizes.frames) + 2
    for tap in range(taps):
        cross = cross_ref[tap * sizes.frames : (tap + 1) * sizes.frames, :]
        row, rest = divmod(tap, TAPS * COLOURS)
        real = (TAPS - 1 - row) * TAPS * COLOURS + rest
        for a in range(TAPS):
            at = a * taps + real
            diag_ref[at : at + 1, :] = jnp.sum(
                jnp.where(lag == a, cross, 0.0), axis=0, keepdims=True
            )
    spread = match(rows_of(out_ref.shape[1]), channel)
    left = diag_ref[...]
    total = jnp.zeros(out_ref.shape, F32)
    for _ in range(3):
        part = left.astype(BF16)
        left = left - part.astype(F32)
        total = total + dot_nt(part, spread)
    out_ref[...] = total
    departure.wait()


def conv_weight_grad(sizes, wire, x):
    taps = TAPS * TAPS * TAPS * COLOURS
    taps_pad = round_up(taps, 16)
    lanes = round_up(sizes.channels, 128)
    return pl.pallas_call(
        functools.partial(conv_weight_kernel, sizes),
        in_specs=[VMEM, HBM],
        out_specs=(VMEM, HBM),
        out_shape=(
            jax.ShapeDtypeStruct((taps_pad, lanes), F32),
            pltpu.HBM((sizes.ext * sizes.group, sizes.cols), BF16),
        ),
        scratch_shapes=[
            pltpu.VMEM((sizes.rows, sizes.channels, sizes.frames, sizes.cols), BF16),
            pltpu.VMEM((sizes.ext * sizes.group, sizes.cols), BF16),
            pltpu.VMEM((sizes.window, sizes.depth), F32),
            pltpu.VMEM((taps_pad, sizes.depth), F32),
            pltpu.SemaphoreType.DMA((sizes.rows,)),
            pltpu.SemaphoreType.DMA(()),
        ],
        compiler_params=pltpu.CompilerParams(vmem_limit_bytes=32 * MIB),
        cost_estimate=pl.CostEstimate(
            flops=2 * sizes.rows * sizes.window * sizes.depth * sizes.cols,
            bytes_accessed=2 * x.size,
            transcendentals=0,
        ),
        name="conv_weight_grad",
    )(wire, x)


def feature_kernel(
    sizes, band_hbm, taps_hbm, out_hbm, held_ref, band_ref, taps_ref, sems, fetch_sems
):
    arrivals = fetch(((band_hbm, band_ref), (taps_hbm, taps_ref)), fetch_sems)

    def departure(row):
        return pltpu.make_async_copy(held_ref.at[row], out_hbm.at[:, row], sems.at[row])

    def step(row, carry):
        window = taps_ref[pl.ds(pl.multiple_of(row * sizes.group, 16), sizes.window), :]
        held_ref[row] = dot(band_ref[...], window).astype(BF16).reshape(held_ref.shape[1:])
        departure(row).start()
        return carry

    for arrival in arrivals:
        arrival.wait()

    lax.fori_loop(0, sizes.rows, step, 0)

    def close(row, carry):
        departure(row).wait()
        return carry

    lax.fori_loop(0, sizes.rows, close, 0)


def feature_gradient(sizes, band, taps):
    shape = (sizes.channels, sizes.rows, sizes.frames, sizes.cols)
    return pl.pallas_call(
        functools.partial(feature_kernel, sizes),
        in_specs=[HBM, HBM],
        out_specs=HBM,
        out_shape=pltpu.HBM(shape, BF16),
        scratch_shapes=[
            pltpu.VMEM((sizes.rows, sizes.channels, sizes.frames, sizes.cols), BF16),
            pltpu.VMEM(band.shape, BF16),
            pltpu.VMEM(taps.shape, BF16),
            pltpu.SemaphoreType.DMA((sizes.rows,)),
            pltpu.SemaphoreType.DMA((2,)),
        ],
        compiler_params=pltpu.CompilerParams(vmem_limit_bytes=32 * MIB),
        cost_estimate=pl.CostEstimate(
            flops=2 * sizes.rows * sizes.window * sizes.depth * sizes.cols,
            bytes_accessed=2 * math.prod(shape),
            transcendentals=0,
        ),
        name="feature_grad",
    )(band, taps)


def scatter(values, axis):
    return lax.all_to_all(values, axis, split_axis=0, concat_axis=0, tiled=True)


def exchange(values, axis, relative):
    return lax.ppermute(values, axis, [(i, i ^ relative) for i in range(lax.axis_size(axis))])


def small_call(kernel, inputs, specs, outputs, name):
    return pl.pallas_call(
        kernel,
        in_specs=specs,
        out_specs=jax.tree.map(lambda _: VMEM, outputs),
        out_shape=outputs,
        compiler_params=pltpu.CompilerParams(vmem_limit_bytes=8 * MIB),
        name=name,
    )(*inputs)


def add_pair_kernel(keep_ref, got_ref, first_hbm, *refs):
    out_refs, (first_ref, sem) = refs[:-2], refs[-2:]
    leave = pltpu.make_async_copy(first_ref, first_hbm, sem)
    for place, out_ref in enumerate((first_ref,) + tuple(out_refs)):
        total = keep_ref[place].astype(F32) + got_ref[place].astype(F32)
        out_ref[...] = total.astype(BF16)
        if place == 0:
            leave.start()
    leave.wait()


def add_pair(keep, got):
    shape = keep.shape[1:]
    outs = (pltpu.HBM(shape, BF16),) + (jax.ShapeDtypeStruct(shape, BF16),) * (keep.shape[0] - 1)
    return pl.pallas_call(
        add_pair_kernel,
        in_specs=[VMEM, VMEM],
        out_specs=(HBM,) + (VMEM,) * (keep.shape[0] - 1),
        out_shape=outs,
        scratch_shapes=[pltpu.VMEM(shape, BF16), pltpu.SemaphoreType.DMA(())],
        compiler_params=pltpu.CompilerParams(vmem_limit_bytes=8 * MIB),
        name="add_pair",
    )(keep, got)


def add_cut_kernel(copies, me_ref, *refs):
    terms, outs = refs[:-copies], refs[-copies:]
    rows = outs[0].shape[0]
    for relative, out_ref in enumerate(outs):
        at = pl.ds(pl.multiple_of((me_ref[0] ^ relative) * rows, 16), rows)
        total = terms[0][at, :].astype(F32)
        for term in terms[1:]:
            total = total + term[at, :].astype(F32)
        out_ref[...] = total.astype(BF16)


def add_cut(me, copies, terms):
    rows, width = terms[0].shape
    outs = (jax.ShapeDtypeStruct((rows // copies, width), BF16),) * copies
    return small_call(
        functools.partial(add_cut_kernel, copies),
        (me,) + tuple(terms),
        [SMEM] + [VMEM] * len(terms),
        outs,
        "add_cut",
    )


def join_kernel(conv_ref, *refs):
    terms, out_ref = refs[:-1], refs[-1]
    rows = terms[0].shape[0]
    total = terms[0][...].astype(F32)
    for term in terms[1:]:
        total = total + term[...].astype(F32)
    out_ref[:rows, :] = total.astype(BF16)
    conv = conv_ref[0].astype(F32)
    for place in range(1, conv_ref.shape[0]):
        conv = conv + conv_ref[place].astype(F32)
    strips = out_ref.shape[1] // conv.shape[1]
    tall = conv.shape[0] // strips
    conv = [conv[strip * tall : (strip + 1) * tall] for strip in range(strips)]
    out_ref[rows:, :] = jnp.concatenate(conv, axis=1).astype(BF16)


def join(terms, conv_all):
    rows, width = terms[0].shape
    more = conv_all.shape[1] * conv_all.shape[2] // width
    out = jax.ShapeDtypeStruct((rows + more, width), BF16)
    return small_call(
        join_kernel, (conv_all,) + tuple(terms), [VMEM] * (1 + len(terms)), out, "join"
    )


def finish_kernel(copies, lanes, me_ref, *refs):
    pieces = refs[:copies]
    qkv_ref, proj_ref, fc1_ref, fc2_ref, conv_ref, whole = refs[copies:]
    width = proj_ref.shape[1]
    rows = whole.shape[0] // copies
    total = None
    for relative, piece in enumerate(pieces):
        at = pl.ds(pl.multiple_of((me_ref[0] ^ relative) * rows, 16), rows)
        whole[at, :] = piece[:rows, :].astype(F32)
        conv = piece[rows:, :].astype(F32)
        total = conv if total is None else total + conv
    share = proj_ref.shape[0]
    at = 0
    for part in range(0, fc1_ref.shape[1], width):
        fc1_ref[:, part : part + width] = whole[at : at + share, :]
        at += share
    fc2_ref[...] = whole[at : at + fc2_ref.shape[0], :]
    at += fc2_ref.shape[0]
    for part in range(0, qkv_ref.shape[1], width):
        qkv_ref[:, part : part + width] = whole[at : at + share, :]
        at += share
    proj_ref[...] = whole[at : at + share, :]
    total = jnp.concatenate(
        [total[:, strip : strip + lanes] for strip in range(0, width, lanes)], axis=0
    )
    time_taps, row_taps, col_taps, colours, channels = conv_ref.shape
    for a in range(time_taps):
        for b in range(row_taps):
            for e in range(col_taps):
                at = ((a * row_taps + b) * col_taps + e) * colours
                conv_ref[a, b, e] = total[at : at + colours, :channels]


def finish(me, pieces, rows, lanes, shapes):
    copies, width = len(pieces), pieces[0].shape[1]
    return pl.pallas_call(
        functools.partial(finish_kernel, copies, lanes),
        in_specs=[SMEM] + [VMEM] * copies,
        out_specs=(VMEM,) * 5,
        out_shape=tuple(jax.ShapeDtypeStruct(shape, F32) for shape in shapes),
        scratch_shapes=[pltpu.VMEM((copies * rows, width), F32)],
        compiler_params=pltpu.CompilerParams(vmem_limit_bytes=12 * MIB),
        name="finish",
    )(me, *pieces)


def shards(
    features,
    conv_weight,
    out_grad,
    pos_embed,
    patch_weight,
    norm1,
    qkv_weight,
    proj_weight,
    norm2,
    fc1_weight,
    fc2_weight,
):
    space = lax.axis_size("space")
    copies = lax.axis_size("dp")
    sizes = Sizes(features, space)
    width = pos_embed.shape[1]
    hidden_width = fc1_weight.shape[1]
    me = lax.axis_index("space").astype(jnp.int32).reshape(1)
    me_dp = lax.axis_index("dp").astype(jnp.int32).reshape(1)
    x = in_hbm(features[0].transpose(0, 2, 1, 3))
    wire, taps = conv_forward(sizes, conv_weight.reshape(-1, COLOURS, sizes.channels), x)
    wire = scatter(wire, "space")
    patch, band = prepare(sizes, taps, patch_weight)
    patch = in_hbm(patch)
    pos, qkv, proj, fc1, fc2, cotangent = (
        in_hbm(array)
        for array in (pos_embed, qkv_weight, proj_weight, fc1_weight, fc2_weight, out_grad[0])
    )
    params = (pos, patch, norm1, qkv, proj, norm2, fc1, fc2)
    block_out, wire_grad, keep, send = transformer(sizes, copies, me, wire, cotangent, params)

    wire_grad = scatter(wire_grad, "space")
    conv_part, tap_rows = conv_weight_grad(sizes, wire_grad, x)
    feature_grad = feature_gradient(sizes, in_hbm(band), in_hbm(tap_rows))

    conv_all = scatter(
        jnp.broadcast_to(conv_part.astype(BF16)[None], (space,) + conv_part.shape), "space"
    )

    chips = add_pair(keep, exchange(send, "space", 1))
    terms = [exchange(chips[r], "space", 2 * r) for r in range(1, len(chips))]
    cuts = add_cut(me_dp, copies, [chips[0]] + terms)
    terms = [exchange(cuts[r], "dp", r) for r in range(1, copies)]
    conv_all, feature_grad = lax.optimization_barrier((conv_all, feature_grad))
    piece = join([cuts[0]] + terms, conv_all)
    pieces = [piece] + [exchange(piece, "dp", r) for r in range(1, copies)]
    share = width // space
    shapes = (
        (share, 3 * width),
        (share, width),
        (share, hidden_width),
        (hidden_width // space, width),
        conv_weight.shape,
    )
    qkv_grad, proj_grad, fc1_grad, fc2_grad, conv_grad = finish(
        me_dp, pieces, cuts[0].shape[0], conv_part.shape[1], shapes
    )

    return (
        block_out[None],
        feature_grad.transpose(0, 2, 1, 3)[None],
        conv_grad,
        qkv_grad,
        proj_grad,
        fc1_grad,
        fc2_grad,
    )


def solution(mesh):
    placed = (
        P("dp", None, None, "space", None),
        P(),
        P("dp", "space", None, None),
        P(),
        P(),
        P(),
        P(),
        P(),
        P(),
        P(),
        P(),
    )
    return jax.shard_map(
        shards,
        mesh=mesh,
        in_specs=placed,
        out_specs=(
            P("dp", "space", None, None),
            P("dp", None, None, "space", None),
            P(),
            P("space", None),
            P("space", None),
            P("space", None),
            P("space", None),
        ),
        check_vma=False,
    )
```

```python
import functools
import math

import jax
import jax.numpy as jnp
from jax import lax
from jax.experimental import pallas as pl
from jax.experimental.pallas import tpu as pltpu
from jax.sharding import PartitionSpec as P

HEADS = 6
PATCH = 14
COLOURS = 3
TAPS = 3
F32 = jnp.float32
BF16 = jnp.bfloat16
MIB = 1 << 20
VMEM = pl.BlockSpec(memory_space=pltpu.VMEM)
SMEM = pl.BlockSpec(memory_space=pltpu.SMEM)
HBM = pl.BlockSpec(memory_space=pltpu.HBM)


def in_hbm(array):
    return pltpu.with_memory_space_constraint(array, pltpu.HBM)


def dot(a, b):
    return jnp.dot(a, b, preferred_element_type=F32)


def dot_nt(a, b):
    return lax.dot_general(a, b, (((1,), (1,)), ((), ())), preferred_element_type=F32)


def dot_tn(a, b):
    return lax.dot_general(a, b, (((0,), (0,)), ((), ())), preferred_element_type=F32)


def split(index, size):
    if size & (size - 1) == 0:
        shift = size.bit_length() - 1
        return index >> shift, index & (size - 1)
    high = jnp.floor((index.astype(F32) + 0.5) * (1.0 / size)).astype(jnp.int32)
    return high, index - high * size


def rows_of(count):
    return lax.broadcasted_iota(jnp.int32, (count, 1), 0)


def cols_of(count):
    return lax.broadcasted_iota(jnp.int32, (1, count), 1)


def match(left, right):
    return jnp.where(left == right, 1.0, 0.0).astype(BF16)


def round_up(value, unit):
    return -(-value // unit) * unit


class Sizes:
    def __init__(self, features, space):
        self.space = space
        self.channels, self.frames, self.rows, self.cols = features.shape[1:]
        self.per_dev = self.frames // space
        self.ext = self.rows + 2
        self.height = self.rows * space
        self.patch_rows = self.height // PATCH
        self.patch_cols = self.cols // PATCH
        self.tokens = self.patch_rows * self.patch_cols
        self.block = round_up(self.ext * COLOURS * self.per_dev, 8)
        self.q_used = COLOURS * PATCH
        self.q_pad = round_up(self.q_used, 64)
        self.plane = COLOURS * self.frames
        self.group = TAPS * self.plane
        self.window = TAPS * self.group
        self.depth = self.channels * self.frames


def wire_keys(sizes, index):
    peer, rest = split(index, sizes.block)
    plane, frame = split(rest, sizes.per_dev)
    ext, colour = split(plane, COLOURS)
    key = (frame * COLOURS + colour) * 4096 + peer * sizes.rows + ext
    return jnp.where(plane < sizes.ext * COLOURS, key, -2)


def patch_keys(sizes, index):
    lead, q = split(index, sizes.q_pad)
    frame, patch_row = split(lead, sizes.patch_rows)
    colour, row = split(q, PATCH)
    key = (frame * COLOURS + colour) * 4096 + patch_row * PATCH + row + 1
    return jnp.where(q < sizes.q_used, key, -1)


def tile_keys(sizes, index):
    return index


def tile_wire_keys(sizes, index):
    peer, rest = split(index, sizes.block)
    plane, frame = split(rest, sizes.per_dev)
    key = plane * sizes.frames + peer * sizes.per_dev + frame
    return jnp.where(plane < sizes.ext * COLOURS, key, -2)


def flipped(tap):
    row, _ = split(tap, TAPS * COLOURS)
    return tap + (TAPS - 1 - 2 * row) * (TAPS * COLOURS)


def column_order(sizes):
    inner, patch = split(rows_of(sizes.cols), sizes.patch_cols)
    return match(patch * PATCH + inner, cols_of(sizes.cols))


def conv_forward_kernel(
    sizes, weight_ref, x_hbm, out_ref, weight_out_ref, x_ref, band_ref, acc_ref, plane_ref, rows_ref, sems
):
    taps = TAPS * TAPS * COLOURS

    def arrival(row):
        return pltpu.make_async_copy(x_hbm.at[:, row], x_ref.at[row], sems.at[row])

    for row in range(sizes.rows):
        arrival(row).start()

    channel, frame_in = split(cols_of(sizes.depth), sizes.frames)
    spread = match(rows_of(sizes.channels), channel)
    for at in range(weight_ref.shape[0]):
        rows_ref[at * COLOURS : (at + 1) * COLOURS, :] = weight_ref[at].astype(F32)
    weight_out_ref[...] = rows_ref[...].astype(BF16)
    wide = dot(weight_out_ref[...], spread)
    lag = frame_in - rows_of(sizes.frames) + 2
    here = [lag == a for a in range(TAPS)]
    for tap in range(taps):
        row, rest = divmod(tap, TAPS * COLOURS)
        real = (TAPS - 1 - row) * TAPS * COLOURS + rest
        block = jnp.zeros((sizes.frames, sizes.depth), F32)
        for a in range(TAPS):
            at = a * taps + real
            block = jnp.where(here[a], wide[at : at + 1, :], block)
        band_ref[tap * sizes.frames : (tap + 1) * sizes.frames, :] = block.astype(BF16)
    acc_ref[...] = jnp.zeros(acc_ref.shape, F32)

    def step(row, carry):
        arrival(row).wait()
        x = x_ref[row].reshape(sizes.depth, sizes.cols)
        at = pl.ds(pl.multiple_of(row * sizes.group, 16), sizes.window)
        acc_ref[at, :] += dot(band_ref[...], x)
        return carry

    lax.fori_loop(0, sizes.rows, step, 0)

    zero = jnp.zeros((sizes.plane, 1), F32)
    for ext in range(sizes.ext):
        at = ext * sizes.group
        first = acc_ref[at : at + sizes.plane, :]
        second = acc_ref[at + sizes.plane : at + 2 * sizes.plane, :]
        third = acc_ref[at + 2 * sizes.plane : at + 3 * sizes.plane, :]
        first = jnp.concatenate([zero, first[:, : sizes.cols - 1]], axis=1)
        third = jnp.concatenate([third[:, 1:], zero], axis=1)
        plane_ref[ext * sizes.plane : (ext + 1) * sizes.plane, :] = (
            first + second + third
        ).astype(BF16)
    wire = tile_wire_keys(sizes, rows_of(sizes.space * sizes.block))
    order = match(wire, cols_of(sizes.ext * sizes.plane))
    moved = dot(order, plane_ref[...]).astype(BF16)
    out_ref[...] = moved


def conv_forward(sizes, weight, x):
    return pl.pallas_call(
        functools.partial(conv_forward_kernel, sizes),
        in_specs=[VMEM, HBM],
        out_specs=(VMEM, VMEM),
        out_shape=(
            jax.ShapeDtypeStruct((sizes.space * sizes.block, sizes.cols), BF16),
            jax.ShapeDtypeStruct((weight.shape[0] * weight.shape[1], sizes.channels), BF16),
        ),
        scratch_shapes=[
            pltpu.VMEM((sizes.rows, sizes.channels, sizes.frames, sizes.cols), BF16),
            pltpu.VMEM((sizes.window, sizes.depth), BF16),
            pltpu.VMEM((sizes.ext * sizes.group, sizes.cols), F32),
            pltpu.VMEM((sizes.ext * sizes.plane, sizes.cols), BF16),
            pltpu.VMEM((weight.shape[0] * weight.shape[1], sizes.channels), F32),
            pltpu.SemaphoreType.DMA((sizes.rows,)),
        ],
        compiler_params=pltpu.CompilerParams(vmem_limit_bytes=32 * MIB),
        cost_estimate=pl.CostEstimate(
            flops=2 * sizes.rows * sizes.window * sizes.depth * sizes.cols,
            bytes_accessed=2 * x.size,
            transcendentals=0,
        ),
        name="conv_forward",
    )(weight, x)


def prepare_kernel(sizes, weight_ref, patch_ref, patch_out_ref, band_ref):
    step = pl.program_id(0)
    taps = TAPS * TAPS * COLOURS

    @pl.when(step == 0)
    def _():
        inner, q = split(rows_of(PATCH * sizes.q_pad), sizes.q_pad)
        source = jnp.where(q < sizes.q_used, q * PATCH + inner, -1)
        order = match(source, cols_of(patch_ref.shape[0]))
        patch_out_ref[...] = dot(order, patch_ref[...]).astype(BF16)

    chunk = band_ref.shape[0]
    tap, frame_in = split(cols_of(sizes.window), sizes.frames)
    pick = match(rows_of(taps), flipped(tap))
    channel, frame_out = split(rows_of(chunk) + step * chunk, sizes.frames)
    spread = match(channel, cols_of(sizes.channels))
    lag = frame_out - frame_in + 2
    total = None
    for a in range(TAPS):
        weight = weight_ref[a * taps : (a + 1) * taps, :]
        wide = dot(spread, dot_tn(weight, pick).astype(BF16))
        wide = jnp.where(lag == a, wide, 0.0)
        total = wide if total is None else total + wide
    band_ref[...] = total.astype(BF16)


def prepare(sizes, weight, patch_weight):
    width = patch_weight.shape[1]
    steps = 4
    patch_shape = (PATCH * sizes.q_pad, width)
    return pl.pallas_call(
        functools.partial(prepare_kernel, sizes),
        grid=(steps,),
        in_specs=[
            pl.BlockSpec(weight.shape, lambda i: (0, 0)),
            pl.BlockSpec(patch_weight.shape, lambda i: (0, 0)),
        ],
        out_specs=(
            pl.BlockSpec(patch_shape, lambda i: (0, 0)),
            pl.BlockSpec((sizes.depth // steps, sizes.window), lambda i: (i, 0)),
        ),
        out_shape=(
            pltpu.HBM(patch_shape, BF16),
            pltpu.HBM((sizes.depth, sizes.window), BF16),
        ),
        compiler_params=pltpu.CompilerParams(vmem_limit_bytes=24 * MIB),
        cost_estimate=pl.CostEstimate(
            flops=4 * 10**9, bytes_accessed=4 * MIB, transcendentals=0
        ),
        name="prepare",
    )(weight, patch_weight)


def normalise(values):
    average = jnp.mean(values, axis=-1, keepdims=True)
    centered = values - average
    variance = jnp.mean(centered * centered, axis=-1, keepdims=True)
    scale = lax.rsqrt(variance + 1e-06)
    return centered * scale, scale


def normalise_back(grad, unit, scale):
    mean_grad = jnp.mean(grad, axis=-1, keepdims=True)
    mean_both = jnp.mean(grad * unit, axis=-1, keepdims=True)
    return scale * (grad - mean_grad - unit * mean_both)


def fetch(pairs, sems):
    copies = [pltpu.make_async_copy(src, dst, sems.at[i]) for i, (src, dst) in enumerate(pairs)]
    for copy in copies:
        copy.start()
    return copies


def first_kernel(
    sizes,
    wire_ref,
    norm1_ref,
    norm2_ref,
    patch_hbm,
    pos_hbm,
    cotangent_hbm,
    qkv_hbm,
    proj_hbm,
    fc1_hbm,
    fc2_hbm,
    out_ref,
    normed_ref,
    packed_ref,
    probs_ref,
    probs_b_ref,
    attended_ref,
    unit_ref,
    scale_ref,
    grad_ref,
    normed2_ref,
    hidden_ref,
    grad_before_ref,
    patch_ref,
    qkv_ref,
    proj_ref,
    pixels_ref,
    patches_ref,
    pos_ref,
    cotangent_ref,
    fc1_ref,
    fc2_ref,
    sems,
):
    pairs = (
        (patch_hbm, patch_ref),
        (pos_hbm, pos_ref),
        (qkv_hbm, qkv_ref),
        (proj_hbm, proj_ref),
        (fc1_hbm, fc1_ref),
        (cotangent_hbm, cotangent_ref),
        (fc2_hbm, fc2_ref),
    )
    arrivals = fetch(pairs, sems)
    tokens, width = pos_ref.shape
    frames = sizes.per_dev
    count = frames * tokens
    hidden_width = fc1_ref.shape[1]
    head = width // HEADS
    wire_rows = sizes.space * sizes.block
    leads = frames * sizes.patch_rows
    q_pad = sizes.q_pad
    pc = sizes.patch_cols

    order = match(patch_keys(sizes, rows_of(leads * q_pad)), wire_keys(sizes, cols_of(wire_rows)))
    pixels_ref[...] = dot(order, wire_ref[...]).astype(BF16)
    columns = column_order(sizes)
    for lead in range(leads):
        turned = dot_nt(columns, pixels_ref[lead * q_pad : (lead + 1) * q_pad, :])
        for inner in range(PATCH):
            patches_ref[lead * pc : (lead + 1) * pc, inner * q_pad : (inner + 1) * q_pad] = turned[
                inner * pc : (inner + 1) * pc, :
            ].astype(BF16)

    for arrival in arrivals[:2]:
        arrival.wait()
    pos = pos_ref[...].astype(F32)
    embedded = dot(patches_ref[...], patch_ref[...])
    embedded = embedded + (pos if frames == 1 else jnp.concatenate([pos] * frames, axis=0))
    unit1, scale1 = normalise(embedded)
    unit_ref[...] = unit1
    scale_ref[...] = scale1
    normed = (unit1 * norm1_ref[...]).astype(BF16)
    normed_ref[...] = normed
    arrivals[2].wait()
    packed_ref[...] = dot(normed, qkv_ref[...]).astype(BF16)

    lanes = min(128, width)
    per_group = lanes // head
    lane_head, _ = split(cols_of(lanes), head)
    inv = 1.0 / float(head) ** 0.5
    masks = [jnp.where(lane_head == sub, 1.0, 0.0).astype(BF16) for sub in range(per_group)]
    places = [
        (frame, group, slice(frame * tokens, (frame + 1) * tokens))
        for frame in range(frames)
        for group in range(width // lanes)
    ]
    for frame, group, at in places:
        queries = packed_ref[at, group * lanes : (group + 1) * lanes]
        keys_in = packed_ref[at, width + group * lanes : width + (group + 1) * lanes]
        for sub in range(per_group):
            probs_ref[frame * HEADS + group * per_group + sub] = dot_nt(
                queries * masks[sub], keys_in
            )
    scores = probs_ref[...] * inv
    scores = jnp.exp(scores - jnp.max(scores, axis=-1, keepdims=True))
    probs = scores * (1.0 / jnp.sum(scores, axis=-1, keepdims=True))
    probs_ref[...] = probs
    probs_b_ref[...] = probs.astype(BF16)
    for frame, group, at in places:
        values_in = packed_ref[at, 2 * width + group * lanes : 2 * width + (group + 1) * lanes]
        joined = None
        for sub in range(per_group):
            value = dot(probs_b_ref[frame * HEADS + group * per_group + sub], values_in)
            joined = value if joined is None else jnp.where(lane_head == sub, value, joined)
        attended_ref[at, group * lanes : (group + 1) * lanes] = joined.astype(BF16)

    for arrival in arrivals[3:]:
        arrival.wait()
    residual = embedded + dot(attended_ref[...], proj_ref[...])
    unit2, scale2 = normalise(residual)
    gain2 = norm2_ref[...]
    normed2 = (unit2 * gain2).astype(BF16)
    normed2_ref[...] = normed2
    cotangent = cotangent_ref[...].reshape(count, width)

    chunk = width
    result = residual
    grad_normed2 = None
    for part in range(hidden_width // chunk):
        cut = slice(part * chunk, (part + 1) * chunk)
        before = dot(normed2, fc1_ref[:, cut])
        cdf = 0.5 + 0.5 * lax.erf(before * math.sqrt(0.5))
        hidden = (before * cdf).astype(BF16)
        result = result + dot(hidden, fc2_ref[cut, :])
        slope = cdf + before * (jnp.exp(-0.5 * before * before) * (1.0 / math.sqrt(2.0 * math.pi)))
        grad_hidden = dot_nt(cotangent, fc2_ref[cut, :]).astype(BF16)
        grad_before = (grad_hidden.astype(F32) * slope).astype(BF16)
        hidden_ref[:, cut] = hidden
        grad_before_ref[:, cut] = grad_before
        piece = dot_nt(grad_before, fc1_ref[:, cut])
        grad_normed2 = piece if grad_normed2 is None else grad_normed2 + piece
    out_ref[...] = result.astype(BF16).reshape(frames, tokens, width)

    grad_normed2 = grad_normed2.astype(BF16).astype(F32) * gain2
    grad_ref[...] = cotangent.astype(F32) + normalise_back(grad_normed2, unit2, scale2)


def second_kernel(
    sizes,
    packed_ref,
    probs_ref,
    probs_b_ref,
    grad_ref,
    unit_ref,
    scale_ref,
    norm1_ref,
    patch_ref,
    qkv_ref,
    proj_ref,
    wire_hbm,
    grad_packed_ref,
    grad_att_ref,
    scores_ref,
    scores_b_ref,
    pixels_ref,
    patches_ref,
    wire_out_ref,
    wire_sems,
):
    count, width = grad_ref.shape
    frames = sizes.per_dev
    tokens = count // frames
    head = width // HEADS
    wire_rows = sizes.space * sizes.block
    leads = frames * sizes.patch_rows
    q_pad = sizes.q_pad
    pc = sizes.patch_cols
    lanes = min(128, width)
    per_group = lanes // head
    lane_head, _ = split(cols_of(lanes), head)
    inv = 1.0 / float(head) ** 0.5

    grad_residual = grad_ref[...]
    grad_att_ref[...] = dot_nt(grad_residual.astype(BF16), proj_ref[...]).astype(BF16)
    masks = [jnp.where(lane_head == sub, 1.0, 0.0).astype(BF16) for sub in range(per_group)]
    places = [
        (frame, group, slice(frame * tokens, (frame + 1) * tokens))
        for frame in range(frames)
        for group in range(width // lanes)
    ]
    for frame, group, at in places:
        grad_att = grad_att_ref[at, group * lanes : (group + 1) * lanes]
        values_in = packed_ref[at, 2 * width + group * lanes : 2 * width + (group + 1) * lanes]
        for sub in range(per_group):
            scores_ref[frame * HEADS + group * per_group + sub] = dot_nt(
                grad_att * masks[sub], values_in
            )
    grad_probs = scores_ref[...].astype(BF16).astype(F32)
    weighted = grad_probs * probs_ref[...]
    inner = jnp.sum(weighted, axis=-1, keepdims=True)
    scores_b_ref[...] = ((weighted - probs_ref[...] * inner) * inv).astype(BF16)
    for frame, group, at in places:
        cut = slice(group * lanes, (group + 1) * lanes)
        cut_k = slice(width + group * lanes, width + (group + 1) * lanes)
        cut_v = slice(2 * width + group * lanes, 2 * width + (group + 1) * lanes)
        queries = packed_ref[at, cut]
        keys_in = packed_ref[at, cut_k]
        grad_att = grad_att_ref[at, cut]
        grad_q = grad_k = grad_v = None
        for sub in range(per_group):
            place = frame * HEADS + group * per_group + sub
            grad_scores = scores_b_ref[place]
            one_q = dot(grad_scores, keys_in)
            one_k = dot_tn(grad_scores, queries * masks[sub])
            one_v = dot_tn(probs_b_ref[place], grad_att * masks[sub])
            grad_q = one_q if grad_q is None else jnp.where(lane_head == sub, one_q, grad_q)
            grad_k = one_k if grad_k is None else grad_k + one_k
            grad_v = one_v if grad_v is None else grad_v + one_v
        grad_packed_ref[at, cut] = grad_q.astype(BF16)
        grad_packed_ref[at, cut_k] = grad_k.astype(BF16)
        grad_packed_ref[at, cut_v] = grad_v.astype(BF16)

    grad_normed = dot_nt(grad_packed_ref[...], qkv_ref[...]).astype(BF16).astype(F32) * norm1_ref[...]
    back = normalise_back(grad_normed, unit_ref[...], scale_ref[...])
    grad_embedded = (grad_residual + back).astype(BF16)
    patches_ref[...] = dot_nt(grad_embedded, patch_ref[...]).astype(BF16)
    columns = column_order(sizes)
    for lead in range(leads):
        turned = jnp.concatenate(
            [
                patches_ref[lead * pc : (lead + 1) * pc, inner * q_pad : (inner + 1) * q_pad]
                for inner in range(PATCH)
            ],
            axis=0,
        )
        pixels_ref[lead * q_pad : (lead + 1) * q_pad, :] = dot_tn(turned, columns).astype(BF16)
    order = match(wire_keys(sizes, rows_of(wire_rows)), patch_keys(sizes, cols_of(leads * q_pad)))
    parts = wire_sems.shape[0]
    tall = wire_rows // parts
    leaving = []
    for part in range(parts):
        at = slice(part * tall, (part + 1) * tall)
        wire_out_ref[at, :] = dot(order[at], pixels_ref[...]).astype(BF16)
        leaving.append(
            pltpu.make_async_copy(wire_out_ref.at[at, :], wire_hbm.at[at, :], wire_sems.at[part])
        )
        leaving[-1].start()
    for copy in leaving:
        copy.wait()


def third_kernel(
    space,
    fc_rows,
    me_ref,
    normed_ref,
    grad_packed_ref,
    attended_ref,
    grad_ref,
    normed2_ref,
    grad_before_ref,
    hidden_ref,
    cotangent_ref,
    keep_ref,
    send_ref,
    qkv_grad_ref,
    proj_grad_ref,
    fc1_grad_ref,
    fc2_grad_ref,
):
    count, width = grad_ref.shape
    hidden_width = hidden_ref.shape[1]
    qkv_grad_ref[...] = dot_tn(normed_ref[...], grad_packed_ref[...])
    proj_grad_ref[...] = dot_tn(attended_ref[...], grad_ref[...].astype(BF16))
    fc1_grad_ref[...] = dot_tn(normed2_ref[...], grad_before_ref[...])
    fc2_grad_ref[...] = dot_tn(hidden_ref[...], cotangent_ref[...].reshape(count, width))
    share = width // space
    fc = [(fc1_grad_ref, share, c) for c in range(0, hidden_width, width)]
    fc.append((fc2_grad_ref, hidden_width // space, 0))
    att = [(qkv_grad_ref, share, c) for c in range(0, 3 * width, width)]
    att.append((proj_grad_ref, share, 0))
    for chip in range(space // 2):
        for other, target in ((0, keep_ref), (1, send_ref)):
            peer = me_ref[0] ^ (2 * chip + other)
            blocks = []
            for pieces, held in ((fc, fc_rows), (att, keep_ref.shape[1] - fc_rows)):
                blocks += [
                    ref[pl.ds(pl.multiple_of(peer * rows, 8), rows), column : column + width]
                    for ref, rows, column in pieces
                ]
                spare = held - sum(rows for _, rows, _ in pieces)
                if spare:
                    blocks.append(jnp.zeros((spare, width), F32))
            target[chip] = jnp.concatenate(blocks, axis=0).astype(BF16)


def transformer(sizes, copies, me, wire, cotangent, params):
    pos, patch, norm1, qkv, proj, norm2, fc1, fc2 = params
    tokens, width = pos.shape
    hidden_width = fc1.shape[1]
    count = sizes.per_dev * tokens
    pixel_shape = (sizes.per_dev * sizes.patch_rows * sizes.q_pad, sizes.cols)
    patches_shape = (count, PATCH * sizes.q_pad)
    norm1, norm2 = norm1[None], norm2[None]

    tall = jax.ShapeDtypeStruct((count, width), BF16)
    wide = jax.ShapeDtypeStruct((count, hidden_width), BF16)
    (
        block_out,
        normed,
        packed,
        probs,
        probs_b,
        attended,
        unit,
        scale,
        grad,
        normed2,
        hidden,
        grad_before,
        patch,
        qkv,
        proj,
    ) = pl.pallas_call(
        functools.partial(first_kernel, sizes),
        in_specs=[VMEM] * 3 + [HBM] * 7,
        out_specs=(VMEM,) * 15,
        out_shape=(
            jax.ShapeDtypeStruct(cotangent.shape, BF16),
            tall,
            jax.ShapeDtypeStruct((count, 3 * width), BF16),
            jax.ShapeDtypeStruct((sizes.per_dev * HEADS, tokens, tokens), F32),
            jax.ShapeDtypeStruct((sizes.per_dev * HEADS, tokens, tokens), BF16),
            tall,
            jax.ShapeDtypeStruct((count, width), F32),
            jax.ShapeDtypeStruct((count, 1), F32),
            jax.ShapeDtypeStruct((count, width), F32),
            tall,
            wide,
            wide,
            jax.ShapeDtypeStruct(patch.shape, BF16),
            jax.ShapeDtypeStruct(qkv.shape, BF16),
            jax.ShapeDtypeStruct(proj.shape, BF16),
        ),
        scratch_shapes=[
            pltpu.VMEM(pixel_shape, BF16),
            pltpu.VMEM(patches_shape, BF16),
        ]
        + [pltpu.VMEM(array.shape, BF16) for array in (pos, cotangent, fc1, fc2)]
        + [pltpu.SemaphoreType.DMA((7,))],
        compiler_params=pltpu.CompilerParams(vmem_limit_bytes=24 * MIB),
        cost_estimate=pl.CostEstimate(
            flops=4 * count * (patch.size + qkv.size + proj.size + fc1.size + fc2.size),
            bytes_accessed=12 * MIB,
            transcendentals=2 * count * hidden_width,
        ),
        name="block_forward",
    )(wire, norm1, norm2, patch, pos, cotangent, qkv, proj, fc1, fc2)

    wire_grad, grad_packed = pl.pallas_call(
        functools.partial(second_kernel, sizes),
        in_specs=[VMEM] * 10,
        out_specs=(HBM, VMEM),
        out_shape=(
            pltpu.HBM(wire.shape, BF16),
            jax.ShapeDtypeStruct((count, 3 * width), BF16),
        ),
        scratch_shapes=[
            pltpu.VMEM((count, width), BF16),
            pltpu.VMEM(probs.shape, F32),
            pltpu.VMEM(probs.shape, BF16),
            pltpu.VMEM(pixel_shape, BF16),
            pltpu.VMEM(patches_shape, BF16),
            pltpu.VMEM(wire.shape, BF16),
            pltpu.SemaphoreType.DMA((4,)),
        ],
        compiler_params=pltpu.CompilerParams(vmem_limit_bytes=20 * MIB),
        cost_estimate=pl.CostEstimate(
            flops=4 * count * (patch.size + qkv.size + proj.size),
            bytes_accessed=6 * MIB,
            transcendentals=0,
        ),
        name="block_backward",
    )(packed, probs, probs_b, grad, unit, scale, norm1, patch, qkv, proj)

    total = qkv.size + proj.size + fc1.size + fc2.size
    fc_rows = round_up((fc1.size + fc2.size) // (width * sizes.space), 16 * copies)
    att_rows = round_up((qkv.size + proj.size) // (width * sizes.space), 16 * copies)
    shares = jax.ShapeDtypeStruct((sizes.space // 2, fc_rows + att_rows, width), BF16)
    keep, send = pl.pallas_call(
        functools.partial(third_kernel, sizes.space, fc_rows),
        in_specs=[SMEM] + [VMEM] * 8,
        out_specs=(VMEM, VMEM),
        out_shape=(shares, shares),
        scratch_shapes=[pltpu.VMEM(array.shape, F32) for array in (qkv, proj, fc1, fc2)],
        compiler_params=pltpu.CompilerParams(vmem_limit_bytes=24 * MIB),
        cost_estimate=pl.CostEstimate(
            flops=2 * count * total, bytes_accessed=8 * MIB, transcendentals=0
        ),
        name="weight_grads",
    )(me, normed, grad_packed, attended, grad, normed2, grad_before, hidden, cotangent)
    return block_out, wire_grad, keep, send, fc_rows


def conv_weight_kernel(
    sizes, wire_ref, x_hbm, out_ref, taps_hbm, x_ref, taps_ref, cross_ref, diag_ref, sems, sem
):
    wire_rows = sizes.space * sizes.block
    taps = TAPS * TAPS * COLOURS

    def arrival(row):
        return pltpu.make_async_copy(x_hbm.at[:, row], x_ref.at[row], sems.at[row])

    for row in range(sizes.rows):
        arrival(row).start()

    order = match(rows_of(sizes.ext * sizes.plane), tile_wire_keys(sizes, cols_of(wire_rows)))
    tile = dot(order, wire_ref[...]).astype(BF16)
    for tap in range(TAPS):
        if tap == 1:
            moved = tile
        else:
            shift = match(rows_of(sizes.cols), cols_of(sizes.cols) + (1 - tap))
            moved = dot(tile, shift).astype(BF16)
        for ext in range(sizes.ext):
            at = ext * sizes.group + tap * sizes.plane
            taps_ref[at : at + sizes.plane, :] = moved[ext * sizes.plane : (ext + 1) * sizes.plane]

    departure = pltpu.make_async_copy(taps_ref, taps_hbm, sem)
    departure.start()
    cross_ref[...] = jnp.zeros(cross_ref.shape, F32)

    def step(row, carry):
        arrival(row).wait()
        x = x_ref[row].reshape(sizes.depth, sizes.cols)
        window = taps_ref[pl.ds(pl.multiple_of(row * sizes.group, 16), sizes.window), :]
        cross_ref[...] += dot_nt(window, x)
        return carry

    lax.fori_loop(0, sizes.rows, step, 0)

    diag_ref[...] = jnp.zeros(diag_ref.shape, F32)
    channel, frame_in = split(cols_of(sizes.depth), sizes.frames)
    lag = frame_in - rows_of(sizes.frames) + 2
    for tap in range(taps):
        cross = cross_ref[tap * sizes.frames : (tap + 1) * sizes.frames, :]
        row, rest = divmod(tap, TAPS * COLOURS)
        real = (TAPS - 1 - row) * TAPS * COLOURS + rest
        for a in range(TAPS):
            at = a * taps + real
            diag_ref[at : at + 1, :] = jnp.sum(
                jnp.where(lag == a, cross, 0.0), axis=0, keepdims=True
            )
    spread = match(rows_of(out_ref.shape[1]), channel)
    left = diag_ref[...]
    total = jnp.zeros(out_ref.shape, F32)
    for _ in range(3):
        part = left.astype(BF16)
        left = left - part.astype(F32)
        total = total + dot_nt(part, spread)
    out_ref[...] = total
    departure.wait()


def conv_weight_grad(sizes, wire, x):
    taps = TAPS * TAPS * TAPS * COLOURS
    taps_pad = round_up(taps, 16)
    lanes = round_up(sizes.channels, 128)
    return pl.pallas_call(
        functools.partial(conv_weight_kernel, sizes),
        in_specs=[VMEM, HBM],
        out_specs=(VMEM, HBM),
        out_shape=(
            jax.ShapeDtypeStruct((taps_pad, lanes), F32),
            pltpu.HBM((sizes.ext * sizes.group, sizes.cols), BF16),
        ),
        scratch_shapes=[
            pltpu.VMEM((sizes.rows, sizes.channels, sizes.frames, sizes.cols), BF16),
            pltpu.VMEM((sizes.ext * sizes.group, sizes.cols), BF16),
            pltpu.VMEM((sizes.window, sizes.depth), F32),
            pltpu.VMEM((taps_pad, sizes.depth), F32),
            pltpu.SemaphoreType.DMA((sizes.rows,)),
            pltpu.SemaphoreType.DMA(()),
        ],
        compiler_params=pltpu.CompilerParams(vmem_limit_bytes=32 * MIB),
        cost_estimate=pl.CostEstimate(
            flops=2 * sizes.rows * sizes.window * sizes.depth * sizes.cols,
            bytes_accessed=2 * x.size,
            transcendentals=0,
        ),
        name="conv_weight_grad",
    )(wire, x)


def feature_kernel(
    sizes, band_hbm, taps_hbm, _, out_hbm, held_ref, band_ref, taps_ref, sems, fetch_sems
):
    arrivals = fetch(((band_hbm, band_ref), (taps_hbm, taps_ref)), fetch_sems)

    def departure(row):
        return pltpu.make_async_copy(held_ref.at[row], out_hbm.at[:, row], sems.at[row])

    def step(row, carry):
        window = taps_ref[pl.ds(pl.multiple_of(row * sizes.group, 16), sizes.window), :]
        held_ref[row] = dot(band_ref[...], window).astype(BF16).reshape(held_ref.shape[1:])
        departure(row).start()
        return carry

    for arrival in arrivals:
        arrival.wait()

    lax.fori_loop(0, sizes.rows, step, 0)

    def close(row, carry):
        departure(row).wait()
        return carry

    lax.fori_loop(0, sizes.rows, close, 0)


def feature_gradient(sizes, band, taps, after):
    shape = (sizes.channels, sizes.rows, sizes.frames, sizes.cols)
    return pl.pallas_call(
        functools.partial(feature_kernel, sizes),
        in_specs=[HBM, HBM, VMEM],
        out_specs=HBM,
        out_shape=pltpu.HBM(shape, BF16),
        scratch_shapes=[
            pltpu.VMEM((sizes.rows, sizes.channels, sizes.frames, sizes.cols), BF16),
            pltpu.VMEM(band.shape, BF16),
            pltpu.VMEM(taps.shape, BF16),
            pltpu.SemaphoreType.DMA((sizes.rows,)),
            pltpu.SemaphoreType.DMA((2,)),
        ],
        compiler_params=pltpu.CompilerParams(vmem_limit_bytes=32 * MIB),
        cost_estimate=pl.CostEstimate(
            flops=2 * sizes.rows * sizes.window * sizes.depth * sizes.cols,
            bytes_accessed=2 * math.prod(shape),
            transcendentals=0,
        ),
        name="feature_grad",
    )(band, taps, after)


def scatter(values, axis):
    return lax.all_to_all(values, axis, split_axis=0, concat_axis=0, tiled=True)


def exchange(values, axis, relative):
    return lax.ppermute(values, axis, [(i, i ^ relative) for i in range(lax.axis_size(axis))])


def small_call(kernel, inputs, specs, outputs, name):
    return pl.pallas_call(
        kernel,
        in_specs=specs,
        out_specs=jax.tree.map(lambda _: VMEM, outputs),
        out_shape=outputs,
        compiler_params=pltpu.CompilerParams(vmem_limit_bytes=8 * MIB),
        name=name,
    )(*inputs)


def sum_of(refs):
    total = refs[0][...].astype(F32)
    for ref in refs[1:]:
        total = total + ref[...].astype(F32)
    return total


def add_pair_kernel(fc_rows, copies, me_ref, keep_ref, got_ref, *outs):
    chips = keep_ref.shape[0]
    for chip in range(chips):
        total = keep_ref[chip, :fc_rows].astype(F32) + got_ref[chip, :fc_rows].astype(F32)
        outs[chip][...] = total.astype(BF16)
    rows = (keep_ref.shape[1] - fc_rows) // copies
    for relative, out_ref in enumerate(outs[chips:]):
        at = pl.ds(pl.multiple_of(fc_rows + (me_ref[0] ^ relative) * rows, 16), rows)
        for chip in range(chips):
            total = keep_ref[chip, at, :].astype(F32) + got_ref[chip, at, :].astype(F32)
            out_ref[chip] = total.astype(BF16)


def add_pair(me, fc_rows, copies, keep, got):
    chips, rows, width = keep.shape
    fc = (jax.ShapeDtypeStruct((fc_rows, width), BF16),) * chips
    att = (jax.ShapeDtypeStruct((chips, (rows - fc_rows) // copies, width), BF16),) * copies
    outs = small_call(
        functools.partial(add_pair_kernel, fc_rows, copies),
        (me, keep, got),
        [SMEM, VMEM, VMEM],
        fc + att,
        "add_pair",
    )
    return outs[:chips], outs[chips:]


def add_cut_kernel(chips, copies, me_ref, *refs):
    fc, att = refs[:chips], refs[chips : chips + copies]
    outs = refs[chips + copies :]
    rows = outs[0].shape[0]
    for relative, out_ref in enumerate(outs[:copies]):
        at = pl.ds(pl.multiple_of((me_ref[0] ^ relative) * rows, 16), rows)
        out_ref[...] = sum_of([ref.at[at, :] for ref in fc]).astype(BF16)
    for chip, out_ref in enumerate(outs[copies:]):
        out_ref[...] = sum_of([ref.at[chip] for ref in att]).astype(BF16)


def add_cut(me, fc, att):
    chips, copies = len(fc), len(att)
    rows, width = fc[0].shape
    outs = (jax.ShapeDtypeStruct((rows // copies, width), BF16),) * copies
    outs += (jax.ShapeDtypeStruct(att[0].shape[1:], BF16),) * chips
    outs = small_call(
        functools.partial(add_cut_kernel, chips, copies),
        (me,) + tuple(fc) + tuple(att),
        [SMEM] + [VMEM] * (chips + copies),
        outs,
        "add_cut",
    )
    return outs[:copies], outs[copies:]


def join_kernel(copies, conv_ref, *refs):
    fc, att, out_ref = refs[:copies], refs[copies:-1], refs[-1]
    at = fc[0].shape[0]
    out_ref[:at, :] = sum_of(fc).astype(BF16)
    out_ref[at : at + att[0].shape[0], :] = sum_of(att).astype(BF16)
    at += att[0].shape[0]
    conv = sum_of([conv_ref.at[place] for place in range(conv_ref.shape[0])])
    strips = out_ref.shape[1] // conv.shape[1]
    tall = conv.shape[0] // strips
    conv = [conv[strip * tall : (strip + 1) * tall] for strip in range(strips)]
    out_ref[at:, :] = jnp.concatenate(conv, axis=1).astype(BF16)


def join(fc, att, conv_all):
    width = fc[0].shape[1]
    rows = fc[0].shape[0] + att[0].shape[0] + conv_all.shape[1] * conv_all.shape[2] // width
    return small_call(
        functools.partial(join_kernel, len(fc)),
        (conv_all,) + tuple(fc) + tuple(att),
        [VMEM] * (1 + len(fc) + len(att)),
        jax.ShapeDtypeStruct((rows, width), BF16),
        "join",
    )


def finish_kernel(copies, lanes, me_ref, *refs):
    pieces = refs[:copies]
    qkv_ref, proj_ref, fc1_ref, fc2_ref, conv_ref, fc, att = refs[copies:]
    width = proj_ref.shape[1]
    fc_rows, att_rows = fc.shape[0] // copies, att.shape[0] // copies
    total = None
    for relative, piece in enumerate(pieces):
        place = me_ref[0] ^ relative
        at = pl.ds(pl.multiple_of(place * fc_rows, 16), fc_rows)
        fc[at, :] = piece[:fc_rows, :].astype(F32)
        at = pl.ds(pl.multiple_of(place * att_rows, 16), att_rows)
        att[at, :] = piece[fc_rows : fc_rows + att_rows, :].astype(F32)
        conv = piece[fc_rows + att_rows :, :].astype(F32)
        total = conv if total is None else total + conv
    share = proj_ref.shape[0]
    at = 0
    for part in range(0, fc1_ref.shape[1], width):
        fc1_ref[:, part : part + width] = fc[at : at + share, :]
        at += share
    fc2_ref[...] = fc[at : at + fc2_ref.shape[0], :]
    at = 0
    for part in range(0, qkv_ref.shape[1], width):
        qkv_ref[:, part : part + width] = att[at : at + share, :]
        at += share
    proj_ref[...] = att[at : at + share, :]
    total = jnp.concatenate(
        [total[:, strip : strip + lanes] for strip in range(0, width, lanes)], axis=0
    )
    time_taps, row_taps, col_taps, colours, channels = conv_ref.shape
    for a in range(time_taps):
        for b in range(row_taps):
            for e in range(col_taps):
                at = ((a * row_taps + b) * col_taps + e) * colours
                conv_ref[a, b, e] = total[at : at + colours, :channels]


def finish(me, pieces, fc_rows, att_rows, lanes, shapes):
    copies, width = len(pieces), pieces[0].shape[1]
    return pl.pallas_call(
        functools.partial(finish_kernel, copies, lanes),
        in_specs=[SMEM] + [VMEM] * copies,
        out_specs=(VMEM,) * 5,
        out_shape=tuple(jax.ShapeDtypeStruct(shape, F32) for shape in shapes),
        scratch_shapes=[
            pltpu.VMEM((copies * fc_rows, width), F32),
            pltpu.VMEM((copies * att_rows, width), F32),
        ],
        compiler_params=pltpu.CompilerParams(vmem_limit_bytes=12 * MIB),
        name="finish",
    )(me, *pieces)


def shards(
    features,
    conv_weight,
    out_grad,
    pos_embed,
    patch_weight,
    norm1,
    qkv_weight,
    proj_weight,
    norm2,
    fc1_weight,
    fc2_weight,
):
    space = lax.axis_size("space")
    copies = lax.axis_size("dp")
    sizes = Sizes(features, space)
    width = pos_embed.shape[1]
    hidden_width = fc1_weight.shape[1]
    me = lax.axis_index("space").astype(jnp.int32).reshape(1)
    me_dp = lax.axis_index("dp").astype(jnp.int32).reshape(1)
    x = in_hbm(features[0].transpose(0, 2, 1, 3))
    wire, taps = conv_forward(sizes, conv_weight.reshape(-1, COLOURS, sizes.channels), x)
    wire = scatter(wire, "space")
    patch, band = prepare(sizes, taps, patch_weight)
    patch = in_hbm(patch)
    pos, qkv, proj, fc1, fc2, cotangent = (
        in_hbm(array)
        for array in (pos_embed, qkv_weight, proj_weight, fc1_weight, fc2_weight, out_grad[0])
    )
    params = (pos, patch, norm1, qkv, proj, norm2, fc1, fc2)
    block_out, wire_grad, keep, send, fc_rows = transformer(
        sizes, copies, me, wire, cotangent, params
    )

    wire_grad = scatter(wire_grad, "space")
    conv_part, tap_rows = conv_weight_grad(sizes, wire_grad, x)

    conv_all = scatter(
        jnp.broadcast_to(conv_part.astype(BF16)[None], (space,) + conv_part.shape), "space"
    )

    fc, att = add_pair(me_dp, fc_rows, copies, keep, exchange(send, "space", 1))
    fc = [fc[0]] + [exchange(fc[r], "space", 2 * r) for r in range(1, len(fc))]
    att = [att[0]] + [exchange(att[r], "dp", r) for r in range(1, copies)]
    fc, att = add_cut(me_dp, fc, att)
    fc_piece, att_piece = fc[0].shape[0], att[0].shape[0]
    fc = [fc[0]] + [exchange(fc[r], "dp", r) for r in range(1, copies)]
    att = [att[0]] + [exchange(att[r], "space", 2 * r) for r in range(1, len(att))]
    piece = join(fc, att, conv_all)
    pieces = [piece] + [exchange(piece, "dp", r) for r in range(1, copies)]
    feature_grad = feature_gradient(sizes, in_hbm(band), in_hbm(tap_rows), piece)
    share = width // space
    shapes = (
        (share, 3 * width),
        (share, width),
        (share, hidden_width),
        (hidden_width // space, width),
        conv_weight.shape,
    )
    qkv_grad, proj_grad, fc1_grad, fc2_grad, conv_grad = finish(
        me_dp, pieces, fc_piece, att_piece, conv_part.shape[1], shapes
    )

    return (
        block_out[None],
        feature_grad.transpose(0, 2, 1, 3)[None],
        conv_grad,
        qkv_grad,
        proj_grad,
        fc1_grad,
        fc2_grad,
    )


def solution(mesh):
    placed = (
        P("dp", None, None, "space", None),
        P(),
        P("dp", "space", None, None),
        P(),
        P(),
        P(),
        P(),
        P(),
        P(),
        P(),
        P(),
    )
    return jax.shard_map(
        shards,
        mesh=mesh,
        in_specs=placed,
        out_specs=(
            P("dp", "space", None, None),
            P("dp", None, None, "space", None),
            P(),
            P("space", None),
            P("space", None),
            P("space", None),
            P("space", None),
        ),
        check_vma=False,
    )
```

```python
import functools
import math

import jax
import jax.numpy as jnp
from jax import lax
from jax.experimental import pallas as pl
from jax.experimental.pallas import tpu as pltpu
from jax.sharding import PartitionSpec as P

HEADS = 6
PATCH = 14
COLOURS = 3
TAPS = 3
F32 = jnp.float32
BF16 = jnp.bfloat16
MIB = 1 << 20
VMEM = pl.BlockSpec(memory_space=pltpu.VMEM)
SMEM = pl.BlockSpec(memory_space=pltpu.SMEM)
HBM = pl.BlockSpec(memory_space=pltpu.HBM)


def in_hbm(array):
    return pltpu.with_memory_space_constraint(array, pltpu.HBM)


def dot(a, b):
    return jnp.dot(a, b, preferred_element_type=F32)


def dot_nt(a, b):
    return lax.dot_general(a, b, (((1,), (1,)), ((), ())), preferred_element_type=F32)


def dot_tn(a, b):
    return lax.dot_general(a, b, (((0,), (0,)), ((), ())), preferred_element_type=F32)


def split(index, size):
    if size & (size - 1) == 0:
        shift = size.bit_length() - 1
        return index >> shift, index & (size - 1)
    high = jnp.floor((index.astype(F32) + 0.5) * (1.0 / size)).astype(jnp.int32)
    return high, index - high * size


def rows_of(count):
    return lax.broadcasted_iota(jnp.int32, (count, 1), 0)


def cols_of(count):
    return lax.broadcasted_iota(jnp.int32, (1, count), 1)


def match(left, right):
    return jnp.where(left == right, 1.0, 0.0).astype(BF16)


def round_up(value, unit):
    return -(-value // unit) * unit


class Sizes:
    def __init__(self, features, space):
        self.space = space
        self.channels, self.frames, self.rows, self.cols = features.shape[1:]
        self.per_dev = self.frames // space
        self.ext = self.rows + 2
        self.height = self.rows * space
        self.patch_rows = self.height // PATCH
        self.patch_cols = self.cols // PATCH
        self.tokens = self.patch_rows * self.patch_cols
        self.block = round_up(self.ext * COLOURS * self.per_dev, 8)
        self.q_used = COLOURS * PATCH
        self.q_pad = round_up(self.q_used, 64)
        self.plane = COLOURS * self.frames
        self.group = TAPS * self.plane
        self.window = TAPS * self.group
        self.depth = self.channels * self.frames


def wire_keys(sizes, index):
    peer, rest = split(index, sizes.block)
    plane, frame = split(rest, sizes.per_dev)
    ext, colour = split(plane, COLOURS)
    key = (frame * COLOURS + colour) * 4096 + peer * sizes.rows + ext
    return jnp.where(plane < sizes.ext * COLOURS, key, -2)


def patch_keys(sizes, index):
    lead, q = split(index, sizes.q_pad)
    frame, patch_row = split(lead, sizes.patch_rows)
    colour, row = split(q, PATCH)
    key = (frame * COLOURS + colour) * 4096 + patch_row * PATCH + row + 1
    return jnp.where(q < sizes.q_used, key, -1)


def tile_keys(sizes, index):
    return index


def tile_wire_keys(sizes, index):
    peer, rest = split(index, sizes.block)
    plane, frame = split(rest, sizes.per_dev)
    key = plane * sizes.frames + peer * sizes.per_dev + frame
    return jnp.where(plane < sizes.ext * COLOURS, key, -2)


def flipped(tap):
    row, _ = split(tap, TAPS * COLOURS)
    return tap + (TAPS - 1 - 2 * row) * (TAPS * COLOURS)


def column_order(sizes):
    inner, patch = split(rows_of(sizes.cols), sizes.patch_cols)
    return match(patch * PATCH + inner, cols_of(sizes.cols))


def conv_forward_kernel(
    sizes, weight_ref, x_hbm, out_ref, weight_out_ref, x_ref, band_ref, acc_ref, plane_ref, rows_ref, sems
):
    taps = TAPS * TAPS * COLOURS

    def arrival(row):
        return pltpu.make_async_copy(x_hbm.at[:, row], x_ref.at[row], sems.at[row])

    for row in range(sizes.rows):
        arrival(row).start()

    channel, frame_in = split(cols_of(sizes.depth), sizes.frames)
    spread = match(rows_of(sizes.channels), channel)
    for at in range(weight_ref.shape[0]):
        rows_ref[at * COLOURS : (at + 1) * COLOURS, :] = weight_ref[at].astype(F32)
    weight_out_ref[...] = rows_ref[...].astype(BF16)
    wide = dot(weight_out_ref[...], spread)
    lag = frame_in - rows_of(sizes.frames) + 2
    here = [lag == a for a in range(TAPS)]
    for tap in range(taps):
        row, rest = divmod(tap, TAPS * COLOURS)
        real = (TAPS - 1 - row) * TAPS * COLOURS + rest
        block = jnp.zeros((sizes.frames, sizes.depth), F32)
        for a in range(TAPS):
            at = a * taps + real
            block = jnp.where(here[a], wide[at : at + 1, :], block)
        band_ref[tap * sizes.frames : (tap + 1) * sizes.frames, :] = block.astype(BF16)
    acc_ref[...] = jnp.zeros(acc_ref.shape, F32)

    def step(row, carry):
        arrival(row).wait()
        x = x_ref[row].reshape(sizes.depth, sizes.cols)
        at = pl.ds(pl.multiple_of(row * sizes.group, 16), sizes.window)
        acc_ref[at, :] += dot(band_ref[...], x)
        return carry

    lax.fori_loop(0, sizes.rows, step, 0)

    zero = jnp.zeros((sizes.plane, 1), F32)
    for ext in range(sizes.ext):
        at = ext * sizes.group
        first = acc_ref[at : at + sizes.plane, :]
        second = acc_ref[at + sizes.plane : at + 2 * sizes.plane, :]
        third = acc_ref[at + 2 * sizes.plane : at + 3 * sizes.plane, :]
        first = jnp.concatenate([zero, first[:, : sizes.cols - 1]], axis=1)
        third = jnp.concatenate([third[:, 1:], zero], axis=1)
        plane_ref[ext * sizes.plane : (ext + 1) * sizes.plane, :] = (
            first + second + third
        ).astype(BF16)
    wire = tile_wire_keys(sizes, rows_of(sizes.space * sizes.block))
    order = match(wire, cols_of(sizes.ext * sizes.plane))
    moved = dot(order, plane_ref[...]).astype(BF16)
    out_ref[...] = moved


def conv_forward(sizes, weight, x):
    return pl.pallas_call(
        functools.partial(conv_forward_kernel, sizes),
        in_specs=[VMEM, HBM],
        out_specs=(VMEM, VMEM),
        out_shape=(
            jax.ShapeDtypeStruct((sizes.space * sizes.block, sizes.cols), BF16),
            jax.ShapeDtypeStruct((weight.shape[0] * weight.shape[1], sizes.channels), BF16),
        ),
        scratch_shapes=[
            pltpu.VMEM((sizes.rows, sizes.channels, sizes.frames, sizes.cols), BF16),
            pltpu.VMEM((sizes.window, sizes.depth), BF16),
            pltpu.VMEM((sizes.ext * sizes.group, sizes.cols), F32),
            pltpu.VMEM((sizes.ext * sizes.plane, sizes.cols), BF16),
            pltpu.VMEM((weight.shape[0] * weight.shape[1], sizes.channels), F32),
            pltpu.SemaphoreType.DMA((sizes.rows,)),
        ],
        compiler_params=pltpu.CompilerParams(vmem_limit_bytes=32 * MIB),
        cost_estimate=pl.CostEstimate(
            flops=2 * sizes.rows * sizes.window * sizes.depth * sizes.cols,
            bytes_accessed=2 * x.size,
            transcendentals=0,
        ),
        name="conv_forward",
    )(weight, x)


def prepare_kernel(sizes, weight_ref, patch_ref, patch_out_ref, band_ref):
    step = pl.program_id(0)
    taps = TAPS * TAPS * COLOURS

    @pl.when(step == 0)
    def _():
        inner, q = split(rows_of(PATCH * sizes.q_pad), sizes.q_pad)
        source = jnp.where(q < sizes.q_used, q * PATCH + inner, -1)
        order = match(source, cols_of(patch_ref.shape[0]))
        patch_out_ref[...] = dot(order, patch_ref[...]).astype(BF16)

    chunk = band_ref.shape[0]
    tap, frame_in = split(cols_of(sizes.window), sizes.frames)
    pick = match(rows_of(taps), flipped(tap))
    channel, frame_out = split(rows_of(chunk) + step * chunk, sizes.frames)
    spread = match(channel, cols_of(sizes.channels))
    lag = frame_out - frame_in + 2
    total = None
    for a in range(TAPS):
        weight = weight_ref[a * taps : (a + 1) * taps, :]
        wide = dot(spread, dot_tn(weight, pick).astype(BF16))
        wide = jnp.where(lag == a, wide, 0.0)
        total = wide if total is None else total + wide
    band_ref[...] = total.astype(BF16)


def prepare(sizes, weight, patch_weight):
    width = patch_weight.shape[1]
    steps = 4
    patch_shape = (PATCH * sizes.q_pad, width)
    return pl.pallas_call(
        functools.partial(prepare_kernel, sizes),
        grid=(steps,),
        in_specs=[
            pl.BlockSpec(weight.shape, lambda i: (0, 0)),
            pl.BlockSpec(patch_weight.shape, lambda i: (0, 0)),
        ],
        out_specs=(
            pl.BlockSpec(patch_shape, lambda i: (0, 0)),
            pl.BlockSpec((sizes.depth // steps, sizes.window), lambda i: (i, 0)),
        ),
        out_shape=(
            pltpu.HBM(patch_shape, BF16),
            pltpu.HBM((sizes.depth, sizes.window), BF16),
        ),
        compiler_params=pltpu.CompilerParams(vmem_limit_bytes=24 * MIB),
        cost_estimate=pl.CostEstimate(
            flops=4 * 10**9, bytes_accessed=4 * MIB, transcendentals=0
        ),
        name="prepare",
    )(weight, patch_weight)


def normalise(values):
    average = jnp.mean(values, axis=-1, keepdims=True)
    centered = values - average
    variance = jnp.mean(centered * centered, axis=-1, keepdims=True)
    scale = lax.rsqrt(variance + 1e-06)
    return centered * scale, scale


def normalise_back(grad, unit, scale):
    mean_grad = jnp.mean(grad, axis=-1, keepdims=True)
    mean_both = jnp.mean(grad * unit, axis=-1, keepdims=True)
    return scale * (grad - mean_grad - unit * mean_both)


def fetch(pairs, sems):
    copies = [pltpu.make_async_copy(src, dst, sems.at[i]) for i, (src, dst) in enumerate(pairs)]
    for copy in copies:
        copy.start()
    return copies


def first_kernel(
    sizes,
    wire_ref,
    norm1_ref,
    norm2_ref,
    patch_hbm,
    pos_hbm,
    cotangent_hbm,
    qkv_hbm,
    proj_hbm,
    fc1_hbm,
    fc2_hbm,
    out_ref,
    normed_ref,
    packed_ref,
    probs_ref,
    probs_b_ref,
    attended_ref,
    unit_ref,
    scale_ref,
    grad_ref,
    normed2_ref,
    hidden_ref,
    grad_before_ref,
    patch_ref,
    qkv_ref,
    proj_ref,
    pixels_ref,
    patches_ref,
    pos_ref,
    cotangent_ref,
    fc1_ref,
    fc2_ref,
    sems,
):
    pairs = (
        (patch_hbm, patch_ref),
        (pos_hbm, pos_ref),
        (qkv_hbm, qkv_ref),
        (proj_hbm, proj_ref),
        (fc1_hbm, fc1_ref),
        (cotangent_hbm, cotangent_ref),
        (fc2_hbm, fc2_ref),
    )
    arrivals = fetch(pairs, sems)
    tokens, width = pos_ref.shape
    frames = sizes.per_dev
    count = frames * tokens
    hidden_width = fc1_ref.shape[1]
    head = width // HEADS
    wire_rows = sizes.space * sizes.block
    leads = frames * sizes.patch_rows
    q_pad = sizes.q_pad
    pc = sizes.patch_cols

    order = match(patch_keys(sizes, rows_of(leads * q_pad)), wire_keys(sizes, cols_of(wire_rows)))
    pixels_ref[...] = dot(order, wire_ref[...]).astype(BF16)
    columns = column_order(sizes)
    for lead in range(leads):
        turned = dot_nt(columns, pixels_ref[lead * q_pad : (lead + 1) * q_pad, :])
        for inner in range(PATCH):
            patches_ref[lead * pc : (lead + 1) * pc, inner * q_pad : (inner + 1) * q_pad] = turned[
                inner * pc : (inner + 1) * pc, :
            ].astype(BF16)

    for arrival in arrivals[:2]:
        arrival.wait()
    pos = pos_ref[...].astype(F32)
    embedded = dot(patches_ref[...], patch_ref[...])
    embedded = embedded + (pos if frames == 1 else jnp.concatenate([pos] * frames, axis=0))
    unit1, scale1 = normalise(embedded)
    unit_ref[...] = unit1
    scale_ref[...] = scale1
    normed = (unit1 * norm1_ref[...]).astype(BF16)
    normed_ref[...] = normed
    arrivals[2].wait()
    packed_ref[...] = dot(normed, qkv_ref[...]).astype(BF16)

    lanes = min(128, width)
    per_group = lanes // head
    lane_head, _ = split(cols_of(lanes), head)
    inv = 1.0 / float(head) ** 0.5
    masks = [jnp.where(lane_head == sub, 1.0, 0.0).astype(BF16) for sub in range(per_group)]
    places = [
        (frame, group, slice(frame * tokens, (frame + 1) * tokens))
        for frame in range(frames)
        for group in range(width // lanes)
    ]
    for frame, group, at in places:
        queries = packed_ref[at, group * lanes : (group + 1) * lanes]
        keys_in = packed_ref[at, width + group * lanes : width + (group + 1) * lanes]
        for sub in range(per_group):
            probs_ref[frame * HEADS + group * per_group + sub] = dot_nt(
                queries * masks[sub], keys_in
            )
    scores = probs_ref[...] * inv
    scores = jnp.exp(scores - jnp.max(scores, axis=-1, keepdims=True))
    probs = scores * (1.0 / jnp.sum(scores, axis=-1, keepdims=True))
    probs_ref[...] = probs
    probs_b_ref[...] = probs.astype(BF16)
    for frame, group, at in places:
        values_in = packed_ref[at, 2 * width + group * lanes : 2 * width + (group + 1) * lanes]
        joined = None
        for sub in range(per_group):
            value = dot(probs_b_ref[frame * HEADS + group * per_group + sub], values_in)
            joined = value if joined is None else jnp.where(lane_head == sub, value, joined)
        attended_ref[at, group * lanes : (group + 1) * lanes] = joined.astype(BF16)

    for arrival in arrivals[3:]:
        arrival.wait()
    residual = embedded + dot(attended_ref[...], proj_ref[...])
    unit2, scale2 = normalise(residual)
    gain2 = norm2_ref[...]
    normed2 = (unit2 * gain2).astype(BF16)
    normed2_ref[...] = normed2
    cotangent = cotangent_ref[...].reshape(count, width)

    chunk = width
    result = residual
    grad_normed2 = None
    for part in range(hidden_width // chunk):
        cut = slice(part * chunk, (part + 1) * chunk)
        before = dot(normed2, fc1_ref[:, cut])
        cdf = 0.5 + 0.5 * lax.erf(before * math.sqrt(0.5))
        hidden = (before * cdf).astype(BF16)
        result = result + dot(hidden, fc2_ref[cut, :])
        slope = cdf + before * (jnp.exp(-0.5 * before * before) * (1.0 / math.sqrt(2.0 * math.pi)))
        grad_hidden = dot_nt(cotangent, fc2_ref[cut, :]).astype(BF16)
        grad_before = (grad_hidden.astype(F32) * slope).astype(BF16)
        hidden_ref[:, cut] = hidden
        grad_before_ref[:, cut] = grad_before
        piece = dot_nt(grad_before, fc1_ref[:, cut])
        grad_normed2 = piece if grad_normed2 is None else grad_normed2 + piece
    out_ref[...] = result.astype(BF16).reshape(frames, tokens, width)

    grad_normed2 = grad_normed2.astype(BF16).astype(F32) * gain2
    grad_ref[...] = cotangent.astype(F32) + normalise_back(grad_normed2, unit2, scale2)


def second_kernel(
    sizes,
    packed_ref,
    probs_ref,
    probs_b_ref,
    grad_ref,
    unit_ref,
    scale_ref,
    norm1_ref,
    patch_ref,
    qkv_ref,
    proj_ref,
    wire_hbm,
    grad_packed_ref,
    grad_att_ref,
    scores_ref,
    scores_b_ref,
    pixels_ref,
    patches_ref,
    wire_out_ref,
    wire_sems,
):
    count, width = grad_ref.shape
    frames = sizes.per_dev
    tokens = count // frames
    head = width // HEADS
    wire_rows = sizes.space * sizes.block
    leads = frames * sizes.patch_rows
    q_pad = sizes.q_pad
    pc = sizes.patch_cols
    lanes = min(128, width)
    per_group = lanes // head
    lane_head, _ = split(cols_of(lanes), head)
    inv = 1.0 / float(head) ** 0.5

    grad_residual = grad_ref[...]
    grad_att_ref[...] = dot_nt(grad_residual.astype(BF16), proj_ref[...]).astype(BF16)
    masks = [jnp.where(lane_head == sub, 1.0, 0.0).astype(BF16) for sub in range(per_group)]
    places = [
        (frame, group, slice(frame * tokens, (frame + 1) * tokens))
        for frame in range(frames)
        for group in range(width // lanes)
    ]
    for frame, group, at in places:
        grad_att = grad_att_ref[at, group * lanes : (group + 1) * lanes]
        values_in = packed_ref[at, 2 * width + group * lanes : 2 * width + (group + 1) * lanes]
        for sub in range(per_group):
            scores_ref[frame * HEADS + group * per_group + sub] = dot_nt(
                grad_att * masks[sub], values_in
            )
    grad_probs = scores_ref[...].astype(BF16).astype(F32)
    weighted = grad_probs * probs_ref[...]
    inner = jnp.sum(weighted, axis=-1, keepdims=True)
    scores_b_ref[...] = ((weighted - probs_ref[...] * inner) * inv).astype(BF16)
    for frame, group, at in places:
        cut = slice(group * lanes, (group + 1) * lanes)
        cut_k = slice(width + group * lanes, width + (group + 1) * lanes)
        cut_v = slice(2 * width + group * lanes, 2 * width + (group + 1) * lanes)
        queries = packed_ref[at, cut]
        keys_in = packed_ref[at, cut_k]
        grad_att = grad_att_ref[at, cut]
        grad_q = grad_k = grad_v = None
        for sub in range(per_group):
            place = frame * HEADS + group * per_group + sub
            grad_scores = scores_b_ref[place]
            one_q = dot(grad_scores, keys_in)
            one_k = dot_tn(grad_scores, queries * masks[sub])
            one_v = dot_tn(probs_b_ref[place], grad_att * masks[sub])
            grad_q = one_q if grad_q is None else jnp.where(lane_head == sub, one_q, grad_q)
            grad_k = one_k if grad_k is None else grad_k + one_k
            grad_v = one_v if grad_v is None else grad_v + one_v
        grad_packed_ref[at, cut] = grad_q.astype(BF16)
        grad_packed_ref[at, cut_k] = grad_k.astype(BF16)
        grad_packed_ref[at, cut_v] = grad_v.astype(BF16)

    grad_normed = dot_nt(grad_packed_ref[...], qkv_ref[...]).astype(BF16).astype(F32) * norm1_ref[...]
    back = normalise_back(grad_normed, unit_ref[...], scale_ref[...])
    grad_embedded = (grad_residual + back).astype(BF16)
    patches_ref[...] = dot_nt(grad_embedded, patch_ref[...]).astype(BF16)
    columns = column_order(sizes)
    for lead in range(leads):
        turned = jnp.concatenate(
            [
                patches_ref[lead * pc : (lead + 1) * pc, inner * q_pad : (inner + 1) * q_pad]
                for inner in range(PATCH)
            ],
            axis=0,
        )
        pixels_ref[lead * q_pad : (lead + 1) * q_pad, :] = dot_tn(turned, columns).astype(BF16)
    order = match(wire_keys(sizes, rows_of(wire_rows)), patch_keys(sizes, cols_of(leads * q_pad)))
    parts = wire_sems.shape[0]
    tall = wire_rows // parts
    leaving = []
    for part in range(parts):
        at = slice(part * tall, (part + 1) * tall)
        wire_out_ref[at, :] = dot(order[at], pixels_ref[...]).astype(BF16)
        leaving.append(
            pltpu.make_async_copy(wire_out_ref.at[at, :], wire_hbm.at[at, :], wire_sems.at[part])
        )
        leaving[-1].start()
    for copy in leaving:
        copy.wait()


def third_kernel(
    space,
    fc_rows,
    me_ref,
    normed_ref,
    grad_packed_ref,
    attended_ref,
    grad_ref,
    normed2_ref,
    grad_before_ref,
    hidden_ref,
    cotangent_ref,
    keep_ref,
    send_ref,
    qkv_grad_ref,
    proj_grad_ref,
    fc1_grad_ref,
    fc2_grad_ref,
):
    count, width = grad_ref.shape
    hidden_width = hidden_ref.shape[1]
    qkv_grad_ref[...] = dot_tn(normed_ref[...], grad_packed_ref[...])
    proj_grad_ref[...] = dot_tn(attended_ref[...], grad_ref[...].astype(BF16))
    fc1_grad_ref[...] = dot_tn(normed2_ref[...], grad_before_ref[...])
    fc2_grad_ref[...] = dot_tn(hidden_ref[...], cotangent_ref[...].reshape(count, width))
    share = width // space
    fc = [(fc1_grad_ref, share, c) for c in range(0, hidden_width, width)]
    fc.append((fc2_grad_ref, hidden_width // space, 0))
    att = [(qkv_grad_ref, share, c) for c in range(0, 3 * width, width)]
    att.append((proj_grad_ref, share, 0))
    for chip in range(space // 2):
        for other, target in ((0, keep_ref), (1, send_ref)):
            peer = me_ref[0] ^ (2 * chip + other)
            blocks = []
            for pieces, held in ((fc, fc_rows), (att, keep_ref.shape[1] - fc_rows)):
                blocks += [
                    ref[pl.ds(pl.multiple_of(peer * rows, 8), rows), column : column + width]
                    for ref, rows, column in pieces
                ]
                spare = held - sum(rows for _, rows, _ in pieces)
                if spare:
                    blocks.append(jnp.zeros((spare, width), F32))
            target[chip] = jnp.concatenate(blocks, axis=0).astype(BF16)


def transformer(sizes, copies, me, wire, cotangent, params):
    pos, patch, norm1, qkv, proj, norm2, fc1, fc2 = params
    tokens, width = pos.shape
    hidden_width = fc1.shape[1]
    count = sizes.per_dev * tokens
    pixel_shape = (sizes.per_dev * sizes.patch_rows * sizes.q_pad, sizes.cols)
    patches_shape = (count, PATCH * sizes.q_pad)
    norm1, norm2 = norm1[None], norm2[None]

    tall = jax.ShapeDtypeStruct((count, width), BF16)
    wide = jax.ShapeDtypeStruct((count, hidden_width), BF16)
    (
        block_out,
        normed,
        packed,
        probs,
        probs_b,
        attended,
        unit,
        scale,
        grad,
        normed2,
        hidden,
        grad_before,
        patch,
        qkv,
        proj,
    ) = pl.pallas_call(
        functools.partial(first_kernel, sizes),
        in_specs=[VMEM] * 3 + [HBM] * 7,
        out_specs=(VMEM,) * 15,
        out_shape=(
            jax.ShapeDtypeStruct(cotangent.shape, BF16),
            tall,
            jax.ShapeDtypeStruct((count, 3 * width), BF16),
            jax.ShapeDtypeStruct((sizes.per_dev * HEADS, tokens, tokens), F32),
            jax.ShapeDtypeStruct((sizes.per_dev * HEADS, tokens, tokens), BF16),
            tall,
            jax.ShapeDtypeStruct((count, width), F32),
            jax.ShapeDtypeStruct((count, 1), F32),
            jax.ShapeDtypeStruct((count, width), F32),
            tall,
            wide,
            wide,
            jax.ShapeDtypeStruct(patch.shape, BF16),
            jax.ShapeDtypeStruct(qkv.shape, BF16),
            jax.ShapeDtypeStruct(proj.shape, BF16),
        ),
        scratch_shapes=[
            pltpu.VMEM(pixel_shape, BF16),
            pltpu.VMEM(patches_shape, BF16),
        ]
        + [pltpu.VMEM(array.shape, BF16) for array in (pos, cotangent, fc1, fc2)]
        + [pltpu.SemaphoreType.DMA((7,))],
        compiler_params=pltpu.CompilerParams(vmem_limit_bytes=24 * MIB),
        cost_estimate=pl.CostEstimate(
            flops=4 * count * (patch.size + qkv.size + proj.size + fc1.size + fc2.size),
            bytes_accessed=12 * MIB,
            transcendentals=2 * count * hidden_width,
        ),
        name="block_forward",
    )(wire, norm1, norm2, patch, pos, cotangent, qkv, proj, fc1, fc2)

    wire_grad, grad_packed = pl.pallas_call(
        functools.partial(second_kernel, sizes),
        in_specs=[VMEM] * 10,
        out_specs=(HBM, VMEM),
        out_shape=(
            pltpu.HBM(wire.shape, BF16),
            jax.ShapeDtypeStruct((count, 3 * width), BF16),
        ),
        scratch_shapes=[
            pltpu.VMEM((count, width), BF16),
            pltpu.VMEM(probs.shape, F32),
            pltpu.VMEM(probs.shape, BF16),
            pltpu.VMEM(pixel_shape, BF16),
            pltpu.VMEM(patches_shape, BF16),
            pltpu.VMEM(wire.shape, BF16),
            pltpu.SemaphoreType.DMA((4,)),
        ],
        compiler_params=pltpu.CompilerParams(vmem_limit_bytes=20 * MIB),
        cost_estimate=pl.CostEstimate(
            flops=4 * count * (patch.size + qkv.size + proj.size),
            bytes_accessed=6 * MIB,
            transcendentals=0,
        ),
        name="block_backward",
    )(packed, probs, probs_b, grad, unit, scale, norm1, patch, qkv, proj)

    total = qkv.size + proj.size + fc1.size + fc2.size
    fc_rows = round_up((fc1.size + fc2.size) // (width * sizes.space), 16 * copies)
    att_rows = round_up((qkv.size + proj.size) // (width * sizes.space), 16 * copies)
    shares = jax.ShapeDtypeStruct((sizes.space // 2, fc_rows + att_rows, width), BF16)
    keep, send = pl.pallas_call(
        functools.partial(third_kernel, sizes.space, fc_rows),
        in_specs=[SMEM] + [VMEM] * 8,
        out_specs=(VMEM, VMEM),
        out_shape=(shares, shares),
        scratch_shapes=[pltpu.VMEM(array.shape, F32) for array in (qkv, proj, fc1, fc2)],
        compiler_params=pltpu.CompilerParams(vmem_limit_bytes=24 * MIB),
        cost_estimate=pl.CostEstimate(
            flops=2 * count * total, bytes_accessed=8 * MIB, transcendentals=0
        ),
        name="weight_grads",
    )(me, normed, grad_packed, attended, grad, normed2, grad_before, hidden, cotangent)
    return block_out, wire_grad, keep, send, fc_rows


def conv_weight_kernel(
    sizes, wire_ref, x_hbm, out_ref, taps_hbm, x_ref, taps_ref, cross_ref, diag_ref, sems, sem
):
    wire_rows = sizes.space * sizes.block
    taps = TAPS * TAPS * COLOURS

    def arrival(row):
        return pltpu.make_async_copy(x_hbm.at[:, row], x_ref.at[row], sems.at[row])

    for row in range(sizes.rows):
        arrival(row).start()

    order = match(rows_of(sizes.ext * sizes.plane), tile_wire_keys(sizes, cols_of(wire_rows)))
    tile = dot(order, wire_ref[...]).astype(BF16)
    for tap in range(TAPS):
        if tap == 1:
            moved = tile
        else:
            shift = match(rows_of(sizes.cols), cols_of(sizes.cols) + (1 - tap))
            moved = dot(tile, shift).astype(BF16)
        for ext in range(sizes.ext):
            at = ext * sizes.group + tap * sizes.plane
            taps_ref[at : at + sizes.plane, :] = moved[ext * sizes.plane : (ext + 1) * sizes.plane]

    departure = pltpu.make_async_copy(taps_ref, taps_hbm, sem)
    departure.start()
    cross_ref[...] = jnp.zeros(cross_ref.shape, F32)

    def step(row, carry):
        arrival(row).wait()
        x = x_ref[row].reshape(sizes.depth, sizes.cols)
        window = taps_ref[pl.ds(pl.multiple_of(row * sizes.group, 16), sizes.window), :]
        cross_ref[...] += dot_nt(window, x)
        return carry

    lax.fori_loop(0, sizes.rows, step, 0)

    diag_ref[...] = jnp.zeros(diag_ref.shape, F32)
    channel, frame_in = split(cols_of(sizes.depth), sizes.frames)
    lag = frame_in - rows_of(sizes.frames) + 2
    for tap in range(taps):
        cross = cross_ref[tap * sizes.frames : (tap + 1) * sizes.frames, :]
        row, rest = divmod(tap, TAPS * COLOURS)
        real = (TAPS - 1 - row) * TAPS * COLOURS + rest
        for a in range(TAPS):
            at = a * taps + real
            diag_ref[at : at + 1, :] = jnp.sum(
                jnp.where(lag == a, cross, 0.0), axis=0, keepdims=True
            )
    spread = match(rows_of(out_ref.shape[1]), channel)
    left = diag_ref[...]
    total = jnp.zeros(out_ref.shape, F32)
    for _ in range(3):
        part = left.astype(BF16)
        left = left - part.astype(F32)
        total = total + dot_nt(part, spread)
    out_ref[...] = total
    departure.wait()


def conv_weight_grad(sizes, wire, x):
    taps = TAPS * TAPS * TAPS * COLOURS
    taps_pad = round_up(taps, 16)
    lanes = round_up(sizes.channels, 128)
    return pl.pallas_call(
        functools.partial(conv_weight_kernel, sizes),
        in_specs=[VMEM, HBM],
        out_specs=(VMEM, HBM),
        out_shape=(
            jax.ShapeDtypeStruct((taps_pad, lanes), F32),
            pltpu.HBM((sizes.ext * sizes.group, sizes.cols), BF16),
        ),
        scratch_shapes=[
            pltpu.VMEM((sizes.rows, sizes.channels, sizes.frames, sizes.cols), BF16),
            pltpu.VMEM((sizes.ext * sizes.group, sizes.cols), BF16),
            pltpu.VMEM((sizes.window, sizes.depth), F32),
            pltpu.VMEM((taps_pad, sizes.depth), F32),
            pltpu.SemaphoreType.DMA((sizes.rows,)),
            pltpu.SemaphoreType.DMA(()),
        ],
        compiler_params=pltpu.CompilerParams(vmem_limit_bytes=32 * MIB),
        cost_estimate=pl.CostEstimate(
            flops=2 * sizes.rows * sizes.window * sizes.depth * sizes.cols,
            bytes_accessed=2 * x.size,
            transcendentals=0,
        ),
        name="conv_weight_grad",
    )(wire, x)


def feature_kernel(
    sizes, band_hbm, taps_hbm, _, out_hbm, held_ref, band_ref, taps_ref, sems, fetch_sems
):
    arrivals = fetch(((band_hbm, band_ref), (taps_hbm, taps_ref)), fetch_sems)

    def departure(row):
        return pltpu.make_async_copy(held_ref.at[row], out_hbm.at[:, row], sems.at[row])

    def step(row, carry):
        window = taps_ref[pl.ds(pl.multiple_of(row * sizes.group, 16), sizes.window), :]
        held_ref[row] = dot(band_ref[...], window).astype(BF16).reshape(held_ref.shape[1:])
        departure(row).start()
        return carry

    for arrival in arrivals:
        arrival.wait()

    lax.fori_loop(0, sizes.rows, step, 0)

    def close(row, carry):
        departure(row).wait()
        return carry

    lax.fori_loop(0, sizes.rows, close, 0)


def feature_gradient(sizes, band, taps, after):
    shape = (sizes.channels, sizes.rows, sizes.frames, sizes.cols)
    return pl.pallas_call(
        functools.partial(feature_kernel, sizes),
        in_specs=[HBM, HBM, VMEM],
        out_specs=HBM,
        out_shape=pltpu.HBM(shape, BF16),
        scratch_shapes=[
            pltpu.VMEM((sizes.rows, sizes.channels, sizes.frames, sizes.cols), BF16),
            pltpu.VMEM(band.shape, BF16),
            pltpu.VMEM(taps.shape, BF16),
            pltpu.SemaphoreType.DMA((sizes.rows,)),
            pltpu.SemaphoreType.DMA((2,)),
        ],
        compiler_params=pltpu.CompilerParams(vmem_limit_bytes=32 * MIB),
        cost_estimate=pl.CostEstimate(
            flops=2 * sizes.rows * sizes.window * sizes.depth * sizes.cols,
            bytes_accessed=2 * math.prod(shape),
            transcendentals=0,
        ),
        name="feature_grad",
    )(band, taps, after)


def scatter(values, axis):
    return lax.all_to_all(values, axis, split_axis=0, concat_axis=0, tiled=True)


def exchange(values, axis, relative):
    return lax.ppermute(values, axis, [(i, i ^ relative) for i in range(lax.axis_size(axis))])


def small_call(kernel, inputs, specs, outputs, name):
    return pl.pallas_call(
        kernel,
        in_specs=specs,
        out_specs=jax.tree.map(lambda _: VMEM, outputs),
        out_shape=outputs,
        compiler_params=pltpu.CompilerParams(vmem_limit_bytes=8 * MIB),
        name=name,
    )(*inputs)


def sum_of(refs):
    total = refs[0][...].astype(F32)
    for ref in refs[1:]:
        total = total + ref[...].astype(F32)
    return total


def add_pair_kernel(fc_rows, copies, me_ref, keep_ref, got_ref, *outs):
    chips = keep_ref.shape[0]
    own_ref = outs[0]
    for chip in range(chips):
        total = keep_ref[chip, :fc_rows].astype(F32) + got_ref[chip, :fc_rows].astype(F32)
        if chip:
            outs[chip][...] = total.astype(BF16)
        else:
            own_ref[:fc_rows, :] = total.astype(BF16)
    rows = (keep_ref.shape[1] - fc_rows) // copies
    for relative in range(copies):
        at = pl.ds(pl.multiple_of(fc_rows + (me_ref[0] ^ relative) * rows, 16), rows)
        for chip in range(chips):
            total = keep_ref[chip, at, :].astype(F32) + got_ref[chip, at, :].astype(F32)
            if relative:
                outs[chips - 1 + relative][chip] = total.astype(BF16)
            else:
                low = fc_rows + chip * rows
                own_ref[low : low + rows, :] = total.astype(BF16)


def add_pair(me, fc_rows, copies, keep, got):
    chips, rows, width = keep.shape
    piece = (rows - fc_rows) // copies
    fc = (jax.ShapeDtypeStruct((fc_rows + chips * piece, width), BF16),)
    fc += (jax.ShapeDtypeStruct((fc_rows, width), BF16),) * (chips - 1)
    att = (jax.ShapeDtypeStruct((chips, piece, width), BF16),) * (copies - 1)
    outs = small_call(
        functools.partial(add_pair_kernel, fc_rows, copies),
        (me, keep, got),
        [SMEM, VMEM, VMEM],
        fc + att,
        "add_pair",
    )
    return outs[0], outs[1:chips], outs[chips:]


def add_cut_kernel(chips, copies, me_ref, own_ref, *refs):
    fc, att = refs[: chips - 1], refs[chips - 1 : chips + copies - 2]
    outs = refs[chips + copies - 2 :]
    rows, piece = outs[0].shape[0], outs[-1].shape[0]
    for relative, out_ref in enumerate(outs[:copies]):
        at = pl.ds(pl.multiple_of((me_ref[0] ^ relative) * rows, 16), rows)
        out_ref[...] = sum_of([ref.at[at, :] for ref in (own_ref,) + tuple(fc)]).astype(BF16)
    for chip, out_ref in enumerate(outs[copies:]):
        low = copies * rows + chip * piece
        terms = [own_ref.at[low : low + piece, :]] + [ref.at[chip] for ref in att]
        out_ref[...] = sum_of(terms).astype(BF16)


def add_cut(me, own, fc, att):
    chips, copies = len(fc) + 1, len(att) + 1
    rows, width = fc[0].shape
    outs = (jax.ShapeDtypeStruct((rows // copies, width), BF16),) * copies
    outs += (jax.ShapeDtypeStruct(att[0].shape[1:], BF16),) * chips
    outs = small_call(
        functools.partial(add_cut_kernel, chips, copies),
        (me, own) + tuple(fc) + tuple(att),
        [SMEM] + [VMEM] * (chips + copies - 1),
        outs,
        "add_cut",
    )
    return outs[:copies], outs[copies:]


def join_kernel(copies, conv_ref, *refs):
    fc, att, out_ref = refs[:copies], refs[copies:-1], refs[-1]
    at = fc[0].shape[0]
    out_ref[:at, :] = sum_of(fc).astype(BF16)
    out_ref[at : at + att[0].shape[0], :] = sum_of(att).astype(BF16)
    at += att[0].shape[0]
    conv = sum_of([conv_ref.at[place] for place in range(conv_ref.shape[0])])
    strips = out_ref.shape[1] // conv.shape[1]
    tall = conv.shape[0] // strips
    conv = [conv[strip * tall : (strip + 1) * tall] for strip in range(strips)]
    out_ref[at:, :] = jnp.concatenate(conv, axis=1).astype(BF16)


def join(fc, att, conv_all):
    width = fc[0].shape[1]
    rows = fc[0].shape[0] + att[0].shape[0] + conv_all.shape[1] * conv_all.shape[2] // width
    return small_call(
        functools.partial(join_kernel, len(fc)),
        (conv_all,) + tuple(fc) + tuple(att),
        [VMEM] * (1 + len(fc) + len(att)),
        jax.ShapeDtypeStruct((rows, width), BF16),
        "join",
    )


def finish_kernel(copies, lanes, me_ref, *refs):
    pieces = refs[:copies]
    qkv_ref, proj_ref, fc1_ref, fc2_ref, conv_ref, fc, att = refs[copies:]
    width = proj_ref.shape[1]
    fc_rows, att_rows = fc.shape[0] // copies, att.shape[0] // copies
    total = None
    for relative, piece in enumerate(pieces):
        place = me_ref[0] ^ relative
        at = pl.ds(pl.multiple_of(place * fc_rows, 16), fc_rows)
        fc[at, :] = piece[:fc_rows, :].astype(F32)
        at = pl.ds(pl.multiple_of(place * att_rows, 16), att_rows)
        att[at, :] = piece[fc_rows : fc_rows + att_rows, :].astype(F32)
        conv = piece[fc_rows + att_rows :, :].astype(F32)
        total = conv if total is None else total + conv
    share = proj_ref.shape[0]
    at = 0
    for part in range(0, fc1_ref.shape[1], width):
        fc1_ref[:, part : part + width] = fc[at : at + share, :]
        at += share
    fc2_ref[...] = fc[at : at + fc2_ref.shape[0], :]
    at = 0
    for part in range(0, qkv_ref.shape[1], width):
        qkv_ref[:, part : part + width] = att[at : at + share, :]
        at += share
    proj_ref[...] = att[at : at + share, :]
    total = jnp.concatenate(
        [total[:, strip : strip + lanes] for strip in range(0, width, lanes)], axis=0
    )
    time_taps, row_taps, col_taps, colours, channels = conv_ref.shape
    for a in range(time_taps):
        for b in range(row_taps):
            for e in range(col_taps):
                at = ((a * row_taps + b) * col_taps + e) * colours
                conv_ref[a, b, e] = total[at : at + colours, :channels]


def finish(me, pieces, fc_rows, att_rows, lanes, shapes):
    copies, width = len(pieces), pieces[0].shape[1]
    return pl.pallas_call(
        functools.partial(finish_kernel, copies, lanes),
        in_specs=[SMEM] + [VMEM] * copies,
        out_specs=(VMEM,) * 5,
        out_shape=tuple(jax.ShapeDtypeStruct(shape, F32) for shape in shapes),
        scratch_shapes=[
            pltpu.VMEM((copies * fc_rows, width), F32),
            pltpu.VMEM((copies * att_rows, width), F32),
        ],
        compiler_params=pltpu.CompilerParams(vmem_limit_bytes=12 * MIB),
        name="finish",
    )(me, *pieces)


def shards(
    features,
    conv_weight,
    out_grad,
    pos_embed,
    patch_weight,
    norm1,
    qkv_weight,
    proj_weight,
    norm2,
    fc1_weight,
    fc2_weight,
):
    space = lax.axis_size("space")
    copies = lax.axis_size("dp")
    sizes = Sizes(features, space)
    width = pos_embed.shape[1]
    hidden_width = fc1_weight.shape[1]
    me = lax.axis_index("space").astype(jnp.int32).reshape(1)
    me_dp = lax.axis_index("dp").astype(jnp.int32).reshape(1)
    x = in_hbm(features[0].transpose(0, 2, 1, 3))
    wire, taps = conv_forward(sizes, conv_weight.reshape(-1, COLOURS, sizes.channels), x)
    wire = scatter(wire, "space")
    patch, band = prepare(sizes, taps, patch_weight)
    patch = in_hbm(patch)
    pos, qkv, proj, fc1, fc2, cotangent = (
        in_hbm(array)
        for array in (pos_embed, qkv_weight, proj_weight, fc1_weight, fc2_weight, out_grad[0])
    )
    params = (pos, patch, norm1, qkv, proj, norm2, fc1, fc2)
    block_out, wire_grad, keep, send, fc_rows = transformer(
        sizes, copies, me, wire, cotangent, params
    )

    wire_grad = scatter(wire_grad, "space")
    conv_part, tap_rows = conv_weight_grad(sizes, wire_grad, x)

    conv_all = scatter(
        jnp.broadcast_to(conv_part.astype(BF16)[None], (space,) + conv_part.shape), "space"
    )

    own, fc, att = add_pair(me_dp, fc_rows, copies, keep, exchange(send, "space", 1))
    fc = [exchange(part, "space", 2 * r) for r, part in enumerate(fc, 1)]
    att = [exchange(part, "dp", r) for r, part in enumerate(att, 1)]
    fc, att = add_cut(me_dp, own, fc, att)
    fc_piece, att_piece = fc[0].shape[0], att[0].shape[0]
    fc = [fc[0]] + [exchange(fc[r], "dp", r) for r in range(1, copies)]
    att = [att[0]] + [exchange(att[r], "space", 2 * r) for r in range(1, len(att))]
    piece = join(fc, att, conv_all)
    pieces = [piece] + [exchange(piece, "dp", r) for r in range(1, copies)]
    feature_grad = feature_gradient(sizes, in_hbm(band), in_hbm(tap_rows), piece)
    share = width // space
    shapes = (
        (share, 3 * width),
        (share, width),
        (share, hidden_width),
        (hidden_width // space, width),
        conv_weight.shape,
    )
    qkv_grad, proj_grad, fc1_grad, fc2_grad, conv_grad = finish(
        me_dp, pieces, fc_piece, att_piece, conv_part.shape[1], shapes
    )

    return (
        block_out[None],
        feature_grad.transpose(0, 2, 1, 3)[None],
        conv_grad,
        qkv_grad,
        proj_grad,
        fc1_grad,
        fc2_grad,
    )


def solution(mesh):
    placed = (
        P("dp", None, None, "space", None),
        P(),
        P("dp", "space", None, None),
        P(),
        P(),
        P(),
        P(),
        P(),
        P(),
        P(),
        P(),
    )
    return jax.shard_map(
        shards,
        mesh=mesh,
        in_specs=placed,
        out_specs=(
            P("dp", "space", None, None),
            P("dp", None, None, "space", None),
            P(),
            P("space", None),
            P("space", None),
            P("space", None),
            P("space", None),
        ),
        check_vma=False,
    )
```
